32 devices in a mesh: gx: 4 (over y, x), gy: 8 (over z, core).
Axes of the slice: x: 2, y: 2, z: 4, core: 2. Of those that a mesh axis runs over, the one named last changes fastest.
Arguments:
- velocity_u: float32 [16, 64, 1024], P(None, 'gx', 'gy'), may hold values from -4 to 4
- velocity_v: float32 [16, 64, 1024], P(None, 'gx', 'gy'), may hold values from -4 to 4
- buoyancy: float32 [16, 64, 1024], P(None, 'gx', 'gy'), may hold values from -5 to 5
- surface: float32 [64, 1024], P('gx', 'gy'), may hold values from -0.5 to 0.5
- transport_u: float32 [64, 1024], P('gx', 'gy'), may hold values from -2 to 2
- transport_v: float32 [64, 1024], P('gx', 'gy'), may hold values from -2 to 2
- ocean: int32 [64, 1024], P('gx', 'gy'), may hold values 0 or 1
- layers: int32 [64, 1024], P('gx', 'gy'), may hold values from 4 to 16
Outputs:
- new_u: float32 [16, 64, 1024], P(None, 'gx', 'gy')
- new_v: float32 [16, 64, 1024], P(None, 'gx', 'gy')
- new_buoyancy: float32 [16, 64, 1024], P(None, 'gx', 'gy')
- new_surface: float32 [64, 1024], P('gx', 'gy')
- new_transport_u: float32 [64, 1024], P('gx', 'gy')
- new_transport_v: float32 [64, 1024], P('gx', 'gy')
The draws below stay inside these ranges and needn't reach their ends.
All inputs are finite; a program needn't handle non-finite values. No bound on the sum of `ocean` on one device may be relied on, other than what follows from the above.
Results may differ from the reference program's by a relative error of at most 0.0001.
Values sent between devices are 32-bit elements; how exact they have to be, the bound alone decides.
A program may use at most 64 MiB of HBM per device.

```python
import jax
import jax.numpy as jnp

LEVELS = 16
SUB = 8
STEPS = 2
NX = 64
NY = 1024


def plant(result, key, least, high):
    shape = result.shape
    index_at = [jax.random.randint(jax.random.fold_in(key, axis), (), 0, shape[axis]) for axis in range(len(shape))]
    result = result.at[tuple(index_at)].set(least)
    longest = shape.index(max(shape))
    index_at[longest] = (index_at[longest] + 1) % shape[longest]
    return result.at[tuple(index_at)].set(high)


def steps_of(stream_key, shape, split, least, largest):
    level, own = 1.0, jax.random.fold_in(stream_key, 6)
    for axis_at, parts in split:
        draws = jnp.exp(jax.random.uniform(jax.random.fold_in(own, axis_at), (parts,), jnp.float32, least / len(split), largest / len(split)))
        level = level * jnp.repeat(draws, shape[axis_at] // parts).reshape([-1 if axis == axis_at else 1 for axis in range(len(shape))])
    return level


def centred(own_key, shape, spread, reach, cuts=(), dtype=jnp.bfloat16):
    values = spread * jax.random.normal(own_key, shape, jnp.float32)
    if cuts:
        values = values * steps_of(own_key, shape, cuts, -0.22, 0.18)
    return jnp.clip(values, -reach, reach).astype(dtype)


def setup_inputs(seed: int = 0) -> dict:
    arg_keys = jax.random.split(jax.random.key(seed), 9)
    velocity_u = centred(arg_keys[0], (LEVELS, NX, NY), 0.5, 4.0, ((1, 4), (2, 8)), jnp.float32)
    velocity_v = centred(arg_keys[1], (LEVELS, NX, NY), 0.5, 4.0, ((1, 4), (2, 8)), jnp.float32)
    buoyancy = centred(arg_keys[2], (LEVELS, NX, NY), 1.0, 5.0, ((1, 4), (2, 8)), jnp.float32)
    surface = centred(arg_keys[3], (NX, NY), 0.1, 0.5, ((0, 4), (1, 8)), jnp.float32)
    transport_u = centred(arg_keys[4], (NX, NY), 0.3, 2.0, ((0, 4), (1, 8)), jnp.float32)
    transport_v = centred(arg_keys[5], (NX, NY), 0.3, 2.0, ((0, 4), (1, 8)), jnp.float32)
    ocean = plant((jax.random.randint(arg_keys[6], (NX, NY), 0, 8) < 7).astype(jnp.int32), jax.random.fold_in(arg_keys[6], 1), 0, 1)
    layers = plant(jax.random.randint(arg_keys[7], (NX, NY), LEVELS // 4, LEVELS + 1), jax.random.fold_in(arg_keys[7], 1), LEVELS // 4, LEVELS).astype(jnp.int32)
    return dict(velocity_u=velocity_u, velocity_v=velocity_v, buoyancy=buoyancy, surface=surface, transport_u=transport_u, transport_v=transport_v, ocean=ocean, layers=layers)


PRESSURE_COEF = 0.5
CORIOLIS = 0.1
VISCOSITY = 0.02
TIME_STEP = 0.2
DIVERGENCE_COEF = 0.25
GRAVITY_COEF = 0.25
DRAG_KEEP = 0.98
SURFACE_CORIOLIS = 0.05


def trim_rim(field, width):
    return field[..., width:field.shape[-2] - width, width:field.shape[-1] - width]


def diff_x(field):
    return (field[..., 2:, 1:-1] - field[..., :-2, 1:-1]) * 0.5


def diff_y(field):
    return (field[..., 1:-1, 2:] - field[..., 1:-1, :-2]) * 0.5


def laplace(field):
    return (field[..., 2:, 1:-1] + field[..., :-2, 1:-1] + field[..., 1:-1, 2:]
            + field[..., 1:-1, :-2] - 4.0 * field[..., 1:-1, 1:-1])


def pad_rim(field, width):
    spec = [(0, 0)] * (field.ndim - 2) + [(width, width), (width, width)]
    return jnp.pad(field, spec)


def advance(near_state, biharm, active):
    levels = near_state.shape[1]
    vel_u = trim_rim(near_state[0], 1)
    vel_v = trim_rim(near_state[1], 1)
    buoy_near = near_state[2]
    pressure = jnp.cumsum(buoy_near, axis=0) / levels
    tend_u = -PRESSURE_COEF * diff_x(pressure) + CORIOLIS * vel_v - VISCOSITY * biharm[0]
    tend_v = -PRESSURE_COEF * diff_y(pressure) - CORIOLIS * vel_u - VISCOSITY * biharm[1]
    tend_b = -(vel_u * diff_x(buoy_near) + vel_v * diff_y(buoy_near)) - VISCOSITY * biharm[2]
    star_u = active * (vel_u + TIME_STEP * tend_u)
    star_v = active * (vel_v + TIME_STEP * tend_v)
    new_buoy = active * (trim_rim(buoy_near, 1) + TIME_STEP * tend_b)
    force_u = jnp.sum(active * tend_u, axis=0) / levels
    force_v = jnp.sum(active * tend_v, axis=0) / levels
    return star_u, star_v, new_buoy, force_u, force_v


def surface_step(sea_level, flow_u, flow_v, force_u, force_v, wet_mask, column_depth):
    eta_mid = trim_rim(wet_mask, 1) * (trim_rim(sea_level, 1)
                                       - DIVERGENCE_COEF * (diff_x(flow_u) + diff_y(flow_v)))
    wet_inner = trim_rim(wet_mask, 2)
    total_depth = trim_rim(column_depth, 2) + trim_rim(eta_mid, 1)
    old_u = trim_rim(flow_u, 2)
    old_v = trim_rim(flow_v, 2)
    next_u = wet_inner * (DRAG_KEEP * old_u + TIME_STEP * trim_rim(force_u, 2)
                          - GRAVITY_COEF * total_depth * diff_x(eta_mid) + SURFACE_CORIOLIS * old_v)
    next_v = wet_inner * (DRAG_KEEP * old_v + TIME_STEP * trim_rim(force_v, 2)
                          - GRAVITY_COEF * total_depth * diff_y(eta_mid) - SURFACE_CORIOLIS * old_u)
    return (trim_rim(eta_mid, 1), next_u, next_v, trim_rim(force_u, 2), trim_rim(force_v, 2),
            wet_inner, trim_rim(column_depth, 2))


def couple_columns(star_u, star_v, total_u, total_v, active, layer_count, column_depth, substeps):
    column_u = jnp.sum(star_u, axis=0) / layer_count
    column_v = jnp.sum(star_v, axis=0) / layer_count
    new_u = active * (star_u - column_u + (total_u / substeps) / column_depth)
    new_v = active * (star_v - column_v + (total_v / substeps) / column_depth)
    return new_u, new_v


def reference(velocity_u, velocity_v, buoyancy, surface, transport_u, transport_v, ocean, layers):
    levels = velocity_u.shape[0]
    wet_mask = ocean.astype(jnp.float32)
    active = wet_mask[None] * (jnp.arange(levels)[:, None, None] < layers[None]).astype(jnp.float32)
    layer_count = layers.astype(jnp.float32)
    column_depth = layer_count / levels
    stacked = jnp.stack([velocity_u, velocity_v, buoyancy])
    sea_level, flow_u, flow_v = surface, transport_u, transport_v
    for step_index in range(STEPS):
        near_state = pad_rim(stacked, 1)
        lap_masked = active * laplace(near_state)
        biharm = laplace(pad_rim(lap_masked, 1))
        star_u, star_v, new_buoy, force_u, force_v = advance(near_state, biharm, active)
        total_u = jnp.zeros(surface.shape, jnp.float32)
        total_v = jnp.zeros(surface.shape, jnp.float32)
        for sub_index in range(SUB):
            pieces = surface_step(*[pad_rim(item, 2) for item in
                                    (sea_level, flow_u, flow_v, force_u, force_v, wet_mask, column_depth)])
            sea_level, flow_u, flow_v = pieces[0], pieces[1], pieces[2]
            total_u = total_u + flow_u
            total_v = total_v + flow_v
        new_u, new_v = couple_columns(star_u, star_v, total_u, total_v, active, layer_count,
                                      column_depth, SUB)
        stacked = jnp.stack([new_u, new_v, new_buoy])
    return (stacked[0], stacked[1], stacked[2], sea_level, flow_u, flow_v)
```

```python
import jax
import jax.numpy as jnp
from jax import lax
from jax.experimental import pallas as pl
from jax.experimental.pallas import tpu as pltpu
from jax.sharding import PartitionSpec as P

SUB = 8
STEPS = 2
LANES = 128
ROWS = 16
LEVELS = 16
FIELDS = 3
STACK = FIELDS * LEVELS
MESH = pl.DeviceIdType.MESH
F32 = jnp.float32

DIRS = [(-1, 0), (1, 0), (0, -1), (0, 1), (-1, -1), (-1, 1), (1, -1), (1, 1)]
SIDES = [(-1, -1), (0, -1), (1, -1), (-1, 1), (0, 1), (1, 1)]
MOVING = 2 * LEVELS
CODE_ROW = 2 * STACK
RIM = CODE_ROW + 8
HALF = LANES // 2


RIMS, FORCE, PLANE, EARLY = 0, 1, 2, 3


def turn(x, shift, axis):
    return pltpu.roll(x, shift % x.shape[axis] if isinstance(shift, int) else shift, axis)


def fold(cells):
    low = lax.broadcasted_iota(jnp.int32, (8, LANES), 1) < HALF
    return jnp.where(low, cells[0:8], turn(cells[8:16], HALF, 1))


def unfold(cells):
    return jnp.concatenate([cells, turn(cells, HALF, 1)], axis=0)


def pack_flat(arrays):
    lane = lax.broadcasted_iota(jnp.int32, (ROWS, LANES), 1)
    to_left = to_right = jnp.zeros((ROWS, LANES), F32)
    for a, cells in enumerate(arrays):
        to_right = jnp.where((lane >> 4) == a, turn(cells, 16 * a + 16, 1), to_right)
        to_left = jnp.where((lane >> 4) == a, turn(cells, 16 * a, 1), to_left)
    return fold(to_left), fold(to_right)


def wide(own, up, down, sides, a):
    lane = lax.broadcasted_iota(jnp.int32, (ROWS, LANES), 1)
    blocks = []
    for r in range(3):
        from_left, from_right = unfold(sides[r]), unfold(sides[r + 3])
        left, right = turn(from_left, 112 - 16 * a, 1), turn(from_right, -16 * a, 1)
        blocks.append(jnp.where(lane < 16, right, jnp.where(lane >= 112, left, 0.0)))
    main = jnp.concatenate([up, own, down], axis=0)
    return jnp.concatenate([main, jnp.concatenate(blocks, axis=0)], axis=1)


def barotropic(state, push_u, push_v, code_wide):
    wet = (code_wide > 0.0).astype(F32)
    depth = code_wide / LEVELS
    zero = jnp.zeros((ROWS, LANES), F32)

    def substep(_, carry):
        eta, tu, tv, sum_u, sum_v = carry
        div = (turn(tu, -1, 0) - turn(tu, 1, 0)) + (turn(tv, -1, 1) - turn(tv, 1, 1))
        eta = wet * (eta - 0.125 * div)
        thick = 0.125 * (depth + eta)
        new_u = wet * (
            0.98 * tu + push_u - thick * (turn(eta, -1, 0) - turn(eta, 1, 0)) + 0.05 * tv
        )
        new_v = wet * (
            0.98 * tv + push_v - thick * (turn(eta, -1, 1) - turn(eta, 1, 1)) - 0.05 * tu
        )
        sum_u = sum_u + new_u[ROWS : 2 * ROWS, 0:LANES]
        sum_v = sum_v + new_v[ROWS : 2 * ROWS, 0:LANES]
        return eta, new_u, new_v, sum_u, sum_v

    eta, tu, tv, sum_u, sum_v = lax.fori_loop(
        0, SUB, substep, state + (zero, zero), unroll=True
    )
    own = tuple(c[ROWS : 2 * ROWS, 0:LANES] for c in (eta, tu, tv))
    return own, sum_u, sum_v


def store_kernel(*refs):
    count = (len(refs) - 1) // 2
    sem = refs[-1]
    copies = [
        pltpu.make_async_copy(src, dst, sem.at[i])
        for i, (src, dst) in enumerate(zip(refs[:count], refs[count:-1]))
    ]
    for copy in copies:
        copy.start()
    for copy in copies:
        copy.wait()


def kernel(
    vel_u, vel_v, buoy, surface, trans_u, trans_v, ocean, layers,
    out_u, out_v, out_b, out_eta, out_tu, out_tv,
    star_u, star_v,
    fx, lp, dyb, near_ext, code_ext, in_3d, in_2d, in_int,
    x_send, y_send, x_recv, y_recv, gx_send, gy_send, gx_recv, gy_recv,
    fx_send, fy_send, fx_recv, fy_recv, in_sem, send_sem, recv_sem,
):
    loads = []
    for a, ref in enumerate((vel_u, vel_v, buoy)):
        loads.append(pltpu.make_async_copy(ref, in_3d.at[a], in_sem.at[a]))
    for a, ref in enumerate((surface, trans_u, trans_v)):
        loads.append(pltpu.make_async_copy(ref, in_2d.at[a], in_sem.at[3 + a]))
    for a, ref in enumerate((ocean, layers)):
        loads.append(pltpu.make_async_copy(ref, in_int.at[a], in_sem.at[6 + a]))
    for load in loads:
        load.start()
    gx, gy = lax.axis_index("gx"), lax.axis_index("gy")
    nx, ny = lax.axis_size("gx"), lax.axis_size("gy")

    def exists(d):
        ok = jnp.bool_(True)
        if d[0] == -1:
            ok = jnp.logical_and(ok, gx > 0)
        if d[0] == 1:
            ok = jnp.logical_and(ok, gx < nx - 1)
        if d[1] == -1:
            ok = jnp.logical_and(ok, gy > 0)
        if d[1] == 1:
            ok = jnp.logical_and(ok, gy < ny - 1)
        return ok

    here = {d: exists(d) for d in DIRS}
    barrier = pltpu.get_barrier_semaphore()
    total_near = jnp.int32(0)
    for d in DIRS:
        total_near = total_near + here[d].astype(jnp.int32)

        @pl.when(here[d])
        def _(d=d):
            pl.semaphore_signal(barrier, inc=1, device_id=(gx + d[0], gy + d[1]), device_id_type=MESH)

    for d in DIRS:
        @pl.when(jnp.logical_not(here[d]))
        def _(d=d):
            for p in range(STEPS):
                if d[1] == 0:
                    s = 0 if d[0] < 0 else 1
                    x_recv[p, s] = jnp.zeros(x_recv.shape[2:], F32)
                    gx_recv[p, s] = jnp.zeros(gx_recv.shape[2:], F32)
                    fx_recv[p, s] = jnp.zeros(fx_recv.shape[2:], F32)
                else:
                    s = SIDES.index(d)
                    y_recv[p, s] = jnp.zeros(y_recv.shape[2:], F32)
                    gy_recv[p, s] = jnp.zeros(gy_recv.shape[2:], F32)
                    fy_recv[p, s] = jnp.zeros(fy_recv.shape[2:], F32)

    def copies(phase, step):
        result = []
        for i, d in enumerate(DIRS):
            back = (-d[0], -d[1])
            if d[1] == 0:
                src_at, dst_at = (0 if d[0] < 0 else 1), (0 if back[0] < 0 else 1)
                if phase == FORCE:
                    src, dst = fx_send.at[step], fx_recv.at[step, dst_at]
                elif phase == PLANE:
                    rows = pl.ds(0, (4 if step == 0 else 3) * ROWS)
                    src, dst = gx_send.at[step, rows], gx_recv.at[step, dst_at, rows]
                else:
                    if step == 0:
                        rows = pl.ds(0, RIM)
                    elif phase == EARLY:
                        rows = pl.ds(2 * MOVING, 2 * LEVELS)
                    else:
                        rows = pl.ds(0, 2 * MOVING)
                    src, dst = x_send.at[step, src_at, rows], x_recv.at[step, dst_at, rows]
            else:
                src_at, dst_at = (0 if d[1] < 0 else 1), SIDES.index(back)
                if phase == FORCE:
                    src, dst = fy_send.at[step, src_at], fy_recv.at[step, dst_at]
                elif phase == PLANE:
                    src, dst = gy_send.at[step, src_at], gy_recv.at[step, dst_at]
                elif phase == EARLY:
                    continue
                else:
                    src, dst = y_send.at[step, src_at], y_recv.at[step, dst_at]
                    if d[0] != 0:
                        rows = pl.ds(0, 8) if d[0] < 0 else pl.ds(8, 8)
                        src, dst = src.at[rows], dst.at[rows]
            at = phase * STEPS + step
            copy = pltpu.make_async_remote_copy(
                src_ref=src, dst_ref=dst,
                send_sem=send_sem.at[at, i], recv_sem=recv_sem.at[at, DIRS.index(back)],
                device_id=(gx + d[0], gy + d[1]), device_id_type=MESH,
            )
            result.append((d, copy))
        return result

    def start(phase, step):
        for d, copy in copies(phase, step):
            @pl.when(here[d])
            def _(copy=copy):
                copy.start()

    def arrive(phase, step):
        by_dir = dict(copies(phase, step))
        for d in by_dir:
            @pl.when(here[d])
            def _(d=d):
                by_dir[(-d[0], -d[1])].wait_recv()

    def sent(phase, step):
        for d, copy in copies(phase, step):
            @pl.when(here[d])
            def _(copy=copy):
                copy.wait_send()

    lane = lax.broadcasted_iota(jnp.int32, (ROWS, LANES), 1)
    pair = lane >> 1
    odd = (lane & 1) == 1
    zero = jnp.zeros((ROWS, LANES), F32)

    def put(step, j, near_at, far_at, cells, strips):
        x_send[step, 0, pl.ds(near_at, 1)] = cells[0:1]
        x_send[step, 0, pl.ds(far_at, 1)] = cells[1:2]
        x_send[step, 1, pl.ds(near_at, 1)] = cells[ROWS - 1 : ROWS]
        x_send[step, 1, pl.ds(far_at, 1)] = cells[ROWS - 2 : ROWS - 1]
        to_left, to_right = strips
        rolled = turn(cells, 2 * j + 2, 1)
        to_right = jnp.where(pair == j, rolled, to_right)
        to_left = jnp.where(pair == j + 1, rolled, to_left)
        return to_left, to_right

    def put_v(step, j, cells, strips):
        fx[j, pl.ds(2, ROWS)] = cells
        return put(step, j, j, MOVING + j, cells, strips)

    def put_b(step, k, cells, strips):
        j = MOVING + k
        return put(step, j, 2 * MOVING + k, 2 * MOVING + LEVELS + k, cells, strips)

    def send_state(step, strips, flats):
        y_send[step, 0] = strips[0]
        y_send[step, 1] = strips[1]
        start(RIMS, step)
        flat_left, flat_right = pack_flat(flats)
        gy_send[step, 0] = flat_left
        gy_send[step, 1] = flat_right
        for a, cells in enumerate(flats):
            gx_send[step, ROWS * a : ROWS * (a + 1)] = cells
        start(PLANE, step)

    loads[6].wait()
    loads[7].wait()
    lay = in_int[1].astype(F32)
    code = jnp.where(in_int[0] > 0, lay, 0.0)
    strips = put(0, STACK, CODE_ROW, CODE_ROW + 1, code, (zero, zero))
    for a in range(FIELDS):
        loads[a].wait()

        def pack(k, strips, a=a):
            cells = in_3d[a, k]
            if a < 2:
                return put_v(0, a * LEVELS + k, cells, strips)
            fx[MOVING + k, pl.ds(2, ROWS)] = cells
            return put_b(0, k, cells, strips)

        strips = lax.fori_loop(0, LEVELS, pack, strips, unroll=True)
    for a in range(3):
        loads[3 + a].wait()
    pl.semaphore_wait(barrier, total_near)
    sea, flow_u, flow_v = in_2d[0], in_2d[1], in_2d[2]
    send_state(0, strips, (sea, flow_u, flow_v, code))

    lane18 = lax.broadcasted_iota(jnp.int32, (ROWS + 2, LANES), 1)
    for step in range(STEPS):
        arrive(RIMS, step)
        if step:
            arrive(EARLY, step)
        from_left, from_right = y_recv[step, 1], y_recv[step, 4]
        near = jnp.where(odd, from_left, turn(from_right, -2, 1))
        far = jnp.where(odd, turn(from_left, 1, 1), turn(from_right, -3, 1))
        inner = turn(jnp.where(odd, strips[1], strips[0]), -1, 1)
        near_ext[pl.ds(1, ROWS)] = near
        odd8 = odd[0:8]
        top = jnp.where(odd8, y_recv[step, 0, 8:16], turn(y_recv[step, 3, 8:16], -2, 1))
        low = jnp.where(odd8, y_recv[step, 2, 0:8], turn(y_recv[step, 5, 0:8], -2, 1))
        near_ext[pl.ds(0, 1)] = top[7:8]
        near_ext[pl.ds(ROWS + 1, 1)] = low[0:1]

        if step == 0:
            code_ext[pl.ds(0, 1)] = x_recv[0, 0, pl.ds(CODE_ROW, 1)]
            code_ext[pl.ds(1, ROWS)] = code
            code_ext[pl.ds(ROWS + 1, 1)] = x_recv[0, 1, pl.ds(CODE_ROW, 1)]
            at = 2 * STACK
            code_near = jnp.where(
                odd,
                jnp.broadcast_to(near[:, at + 1 : at + 2], (ROWS, LANES)),
                jnp.broadcast_to(near[:, at : at + 1], (ROWS, LANES)),
            )
            act_near = ((pair & (LEVELS - 1)).astype(F32) < code_near).astype(F32)
            code18 = code_ext[pl.ds(0, ROWS + 2)]
        lap_near = act_near * (
            far + inner + near_ext[pl.ds(0, ROWS)] + near_ext[pl.ds(2, ROWS)] - 4.0 * near
        )
        near18 = near_ext[pl.ds(0, ROWS + 2)]

        def biharm(j, near_at, far_at, act18):
            fx[j, pl.ds(0, 1)] = x_recv[step, 0, pl.ds(far_at, 1)]
            fx[j, pl.ds(1, 1)] = x_recv[step, 0, pl.ds(near_at, 1)]
            fx[j, pl.ds(ROWS + 2, 1)] = x_recv[step, 1, pl.ds(near_at, 1)]
            fx[j, pl.ds(ROWS + 3, 1)] = x_recv[step, 1, pl.ds(far_at, 1)]
            mid = fx[j, pl.ds(1, ROWS + 2)]
            edge = turn(near18, 127 - 2 * j, 1)
            ahead = jnp.where(lane18 == LANES - 1, edge, turn(mid, -1, 1))
            behind = jnp.where(lane18 == 0, edge, turn(mid, 1, 1))
            lap = act18 * (
                fx[j, pl.ds(0, ROWS + 2)] + fx[j, pl.ds(2, ROWS + 2)] + ahead + behind - 4.0 * mid
            )
            lp[j, pl.ds(0, ROWS + 2)] = lap
            mid = lp[j, pl.ds(1, ROWS)]
            edge = turn(lap_near, 127 - 2 * j, 1)
            ahead = jnp.where(lane == LANES - 1, edge, turn(mid, -1, 1))
            behind = jnp.where(lane == 0, edge, turn(mid, 1, 1))
            return lp[j, pl.ds(0, ROWS)] + lp[j, pl.ds(2, ROWS)] + ahead + behind - 4.0 * mid

        def buoyancy(k, carry):
            level_at = lax.convert_element_type(k, F32)
            act18 = (level_at < code18).astype(F32)
            act = (level_at < code).astype(F32)
            at = 2 * LEVELS + k
            bih_b = biharm(at, 2 * MOVING + k, 2 * MOVING + LEVELS + k, act18)
            u, v = fx[k, pl.ds(2, ROWS)], fx[LEVELS + k, pl.ds(2, ROWS)]
            b = fx[at, pl.ds(2, ROWS)]
            b_x = fx[at, pl.ds(3, ROWS)] - fx[at, pl.ds(1, ROWS)]
            tend_b = -0.5 * (u * b_x + v * dyb[k, pl.ds(0, ROWS)]) - 0.02 * bih_b
            new_b = act * (b + 0.2 * tend_b)
            if step == STEPS - 1:
                out_b[k] = new_b
            else:
                fx[at, pl.ds(2, ROWS)] = new_b
            return carry

        def level(k, carry):
            press_x, press_y, force_u, force_v, col_u, col_v = carry
            level_at = lax.convert_element_type(k, F32)
            act18 = (level_at < code18).astype(F32)
            act = (level_at < code).astype(F32)
            bih_u = biharm(k, k, MOVING + k, act18)
            bih_v = biharm(LEVELS + k, LEVELS + k, MOVING + LEVELS + k, act18)
            u, v = fx[k, pl.ds(2, ROWS)], fx[LEVELS + k, pl.ds(2, ROWS)]
            at = 2 * LEVELS + k
            fx[at, pl.ds(1, 1)] = x_recv[step, 0, pl.ds(2 * MOVING + k, 1)]
            fx[at, pl.ds(ROWS + 2, 1)] = x_recv[step, 1, pl.ds(2 * MOVING + k, 1)]
            b = fx[at, pl.ds(2, ROWS)]
            edge = turn(near, 127 - 2 * at, 1)
            b_x = fx[at, pl.ds(3, ROWS)] - fx[at, pl.ds(1, ROWS)]
            b_y = jnp.where(lane == LANES - 1, edge, turn(b, -1, 1)) - jnp.where(
                lane == 0, edge, turn(b, 1, 1)
            )
            dyb[k, pl.ds(0, ROWS)] = b_y
            press_x, press_y = press_x + b_x, press_y + b_y
            tend_u = (-0.25 / LEVELS) * press_x + 0.1 * v - 0.02 * bih_u
            tend_v = (-0.25 / LEVELS) * press_y - 0.1 * u - 0.02 * bih_v
            su = act * (u + 0.2 * tend_u)
            sv = act * (v + 0.2 * tend_v)
            star_u[k] = su
            star_v[k] = sv
            return (
                press_x, press_y, force_u + act * tend_u, force_v + act * tend_v,
                col_u + su, col_v + sv,
            )

        _, _, force_u, force_v, col_u, col_v = lax.fori_loop(
            0, LEVELS, level, (zero,) * 6, unroll=True
        )
        force_u, force_v = force_u / LEVELS, force_v / LEVELS
        fx_send[step, 0:ROWS] = force_u
        fx_send[step, ROWS : 2 * ROWS] = force_v
        flat_left, flat_right = pack_flat((force_u, force_v))
        fy_send[step, 0] = flat_left
        fy_send[step, 1] = flat_right
        start(FORCE, step)
        lax.fori_loop(0, LEVELS, buoyancy, 0, unroll=True)
        if step < STEPS - 1:
            def pack_b(k, strips):
                return put_b(step + 1, k, fx[MOVING + k, pl.ds(2, ROWS)], strips)

            strips = lax.fori_loop(0, LEVELS, pack_b, (zero, zero), unroll=True)
            start(EARLY, step + 1)
        arrive(PLANE, step)
        sides = [gy_recv[step, r] for r in range(6)]

        def plane(own, a):
            rows = slice(ROWS * a, ROWS * (a + 1))
            return wide(own, gx_recv[step, 0, rows], gx_recv[step, 1, rows], sides, a)

        if step == 0:
            code_wide = plane(code, 3)
        state = (plane(sea, 0), plane(flow_u, 1), plane(flow_v, 2))
        arrive(FORCE, step)
        sides_f = [fy_recv[step, r] for r in range(6)]
        push_u, push_v = (
            0.2 * wide(
                own, fx_recv[step, 0, ROWS * a : ROWS * (a + 1)],
                fx_recv[step, 1, ROWS * a : ROWS * (a + 1)], sides_f, a,
            )
            for a, own in enumerate((force_u, force_v))
        )
        (sea, flow_u, flow_v), sum_u, sum_v = barotropic(state, push_u, push_v, code_wide)
        scale = LEVELS / SUB
        shift_u = (scale * sum_u - col_u) / lay
        shift_v = (scale * sum_v - col_v) / lay
        if step < STEPS - 1:
            def couple(k, strips):
                act = (lax.convert_element_type(k, F32) < code).astype(F32)
                strips = put_v(step + 1, k, act * (star_u[k] + shift_u), strips)
                return put_v(step + 1, LEVELS + k, act * (star_v[k] + shift_v), strips)

            strips = lax.fori_loop(0, LEVELS, couple, strips, unroll=True)
            send_state(step + 1, strips, (sea, flow_u, flow_v))
        else:
            def finish(k, carry):
                act = lax.convert_element_type(k, F32) < code
                out_u[k] = jnp.where(act, star_u[k] + shift_u, 0.0)
                out_v[k] = jnp.where(act, star_v[k] + shift_v, 0.0)
                return carry

            lax.fori_loop(0, LEVELS, finish, 0, unroll=True)
            out_eta[...] = sea
            out_tu[...] = flow_u
            out_tv[...] = flow_v

    for step in range(STEPS):
        for phase in (RIMS, FORCE, PLANE, EARLY):
            if phase != EARLY or step:
                sent(phase, step)


def per_device(velocity_u, velocity_v, buoyancy, surface, transport_u, transport_v, ocean, layers):
    cube = jax.ShapeDtypeStruct(velocity_u.shape, F32)
    flat = jax.ShapeDtypeStruct(surface.shape, F32)
    hbm = pl.BlockSpec(memory_space=pltpu.HBM)
    vmem = pl.BlockSpec(memory_space=pltpu.VMEM)
    outs = (cube, cube, cube, flat, flat, flat)
    args = [
        pltpu.with_memory_space_constraint(x, pltpu.HBM)
        for x in (velocity_u, velocity_v, buoyancy, surface, transport_u, transport_v, ocean, layers)
    ]
    ext = 24
    block = (LEVELS, ROWS, LANES)
    middle = pl.pallas_call(
        kernel,
        out_shape=outs,
        in_specs=[hbm] * 8,
        out_specs=(vmem,) * 6,
        scratch_shapes=[
            pltpu.VMEM(block, F32),
            pltpu.VMEM(block, F32),
            pltpu.VMEM((STACK, ext, LANES), F32),
            pltpu.VMEM((STACK, ext, LANES), F32),
            pltpu.VMEM((LEVELS, ext, LANES), F32),
            pltpu.VMEM((ext, LANES), F32),
            pltpu.VMEM((ext, LANES), F32),
            pltpu.VMEM((FIELDS,) + block, F32),
            pltpu.VMEM((3, ROWS, LANES), F32),
            pltpu.VMEM((2, ROWS, LANES), jnp.int32),
            pltpu.VMEM((STEPS, 2, RIM, LANES), F32),
            pltpu.VMEM((STEPS, 2, ROWS, LANES), F32),
            pltpu.VMEM((STEPS, 2, RIM, LANES), F32),
            pltpu.VMEM((STEPS, 6, ROWS, LANES), F32),
            pltpu.VMEM((STEPS, 4 * ROWS, LANES), F32),
            pltpu.VMEM((STEPS, 2, 8, LANES), F32),
            pltpu.VMEM((STEPS, 2, 4 * ROWS, LANES), F32),
            pltpu.VMEM((STEPS, 6, 8, LANES), F32),
            pltpu.VMEM((STEPS, 2 * ROWS, LANES), F32),
            pltpu.VMEM((STEPS, 2, 8, LANES), F32),
            pltpu.VMEM((STEPS, 2, 2 * ROWS, LANES), F32),
            pltpu.VMEM((STEPS, 6, 8, LANES), F32),
            pltpu.SemaphoreType.DMA((8,)),
            pltpu.SemaphoreType.DMA((4 * STEPS, 8)),
            pltpu.SemaphoreType.DMA((4 * STEPS, 8)),
        ],
        compiler_params=pltpu.CompilerParams(
            collective_id=0, has_side_effects=True, vmem_limit_bytes=16 * 2**20
        ),
    )(*args)
    return tuple(
        pl.pallas_call(
            store_kernel,
            out_shape=outs,
            in_specs=[vmem] * 6,
            out_specs=(hbm,) * 6,
            scratch_shapes=[pltpu.SemaphoreType.DMA((6,))],
            compiler_params=pltpu.CompilerParams(vmem_limit_bytes=16 * 2**20),
        )(*middle)
    )


def solution(mesh):
    cube, flat = P(None, "gx", "gy"), P("gx", "gy")
    return jax.shard_map(
        per_device,
        mesh=mesh,
        in_specs=(cube, cube, cube, flat, flat, flat, flat, flat),
        out_specs=(cube, cube, cube, flat, flat, flat),
        check_vma=False,
    )
```

```python
import jax
import jax.numpy as jnp
from jax import lax
from jax.experimental import pallas as pl
from jax.experimental.pallas import tpu as pltpu
from jax.sharding import PartitionSpec as P

SUB = 8
STEPS = 2
LANES = 128
ROWS = 16
LEVELS = 16
FIELDS = 3
STACK = FIELDS * LEVELS
MESH = pl.DeviceIdType.MESH
F32 = jnp.float32
BF16 = jnp.bfloat16

DIRS = [(-1, 0), (1, 0), (0, -1), (0, 1), (-1, -1), (-1, 1), (1, -1), (1, 1)]
SIDES = [(-1, -1), (0, -1), (1, -1), (-1, 1), (0, 1), (1, 1)]
MOVING = 2 * LEVELS
CODE_ROW = 2 * STACK
RIM = CODE_ROW + 8
HALF = LANES // 2


RIMS, FORCE, PLANE, EARLY = 0, 1, 2, 3
EXT = 32
OWN = 8


def turn(x, shift, axis):
    return pltpu.roll(x, shift % x.shape[axis] if isinstance(shift, int) else shift, axis)


def fold(cells):
    low = lax.broadcasted_iota(jnp.int32, (8, LANES), 1) < HALF
    return jnp.where(low, cells[0:8], turn(cells[8:16], HALF, 1))


def unfold(cells):
    return jnp.concatenate([cells, turn(cells, HALF, 1)], axis=0)


def split(x):
    high = x.astype(BF16)
    return high, (x - high.astype(F32)).astype(BF16)


def pick(mask, x):
    return tuple(jnp.where(mask, part.astype(F32), 0.0).astype(BF16) for part in split(x))


def lane_weights():
    src = lax.broadcasted_iota(jnp.int32, (LANES, LANES), 0)
    dst = lax.broadcasted_iota(jnp.int32, (LANES, LANES), 1)
    ahead, behind = (src == dst + 1).astype(F32), (src == dst - 1).astype(F32)
    odd = (src & 1) == 1
    first = jnp.logical_and(odd, dst == 0).astype(F32)
    last = jnp.logical_and(jnp.logical_not(odd), dst == LANES - 1).astype(F32)
    return [
        [(ahead + behind).astype(BF16), (ahead - behind).astype(BF16)],
        [(last + first).astype(BF16), (last - first).astype(BF16)],
    ]


def pack_flat(arrays):
    lane = lax.broadcasted_iota(jnp.int32, (ROWS, LANES), 1)
    to_left = to_right = jnp.zeros((ROWS, LANES), F32)
    for a, cells in enumerate(arrays):
        to_right = jnp.where((lane >> 4) == a, turn(cells, 16 * a + 16, 1), to_right)
        to_left = jnp.where((lane >> 4) == a, turn(cells, 16 * a, 1), to_left)
    return fold(to_left), fold(to_right)


def wide(own, up, down, sides, a):
    lane = lax.broadcasted_iota(jnp.int32, (ROWS, LANES), 1)
    blocks = []
    for r in range(3):
        from_left, from_right = unfold(sides[r]), unfold(sides[r + 3])
        left, right = turn(from_left, 112 - 16 * a, 1), turn(from_right, -16 * a, 1)
        blocks.append(jnp.where(lane < 16, right, jnp.where(lane >= 112, left, 0.0)))
    main = jnp.concatenate([up, own, down], axis=0)
    return jnp.concatenate([main, jnp.concatenate(blocks, axis=0)], axis=1)


def barotropic(state, push_u, push_v, code_wide):
    wet = (code_wide > 0.0).astype(F32)
    depth = code_wide / LEVELS
    zero = jnp.zeros((ROWS, LANES), F32)

    def substep(_, carry):
        eta, tu, tv, sum_u, sum_v = carry
        div = (turn(tu, -1, 0) - turn(tu, 1, 0)) + (turn(tv, -1, 1) - turn(tv, 1, 1))
        eta = wet * (eta - 0.125 * div)
        thick = 0.125 * (depth + eta)
        new_u = wet * (
            0.98 * tu + push_u - thick * (turn(eta, -1, 0) - turn(eta, 1, 0)) + 0.05 * tv
        )
        new_v = wet * (
            0.98 * tv + push_v - thick * (turn(eta, -1, 1) - turn(eta, 1, 1)) - 0.05 * tu
        )
        sum_u = sum_u + new_u[ROWS : 2 * ROWS, 0:LANES]
        sum_v = sum_v + new_v[ROWS : 2 * ROWS, 0:LANES]
        return eta, new_u, new_v, sum_u, sum_v

    eta, tu, tv, sum_u, sum_v = lax.fori_loop(
        0, SUB, substep, state + (zero, zero), unroll=True
    )
    own = tuple(c[ROWS : 2 * ROWS, 0:LANES] for c in (eta, tu, tv))
    return own, sum_u, sum_v


def store_kernel(*refs):
    count = (len(refs) - 1) // 2
    sem = refs[-1]
    copies = [
        pltpu.make_async_copy(src, dst, sem.at[i])
        for i, (src, dst) in enumerate(zip(refs[:count], refs[count:-1]))
    ]
    for copy in copies:
        copy.start()
    for copy in copies:
        copy.wait()


def kernel(
    vel_u, vel_v, buoy, surface, trans_u, trans_v, ocean, layers,
    out_u, out_v, out_b, out_eta, out_tu, out_tv,
    star_u, star_v,
    fx, lp, near_ext, code_ext, in_3d, in_2d, in_int,
    lane_w, mom_in, buoy_in, mom_out, buoy_out,
    x_send, y_send, x_recv, y_recv, gx_send, gy_send, gx_recv, gy_recv,
    fx_send, fy_send, fx_recv, fy_recv, in_sem, send_sem, recv_sem,
):
    loads = []
    for a, ref in enumerate((vel_u, vel_v, buoy)):
        loads.append(pltpu.make_async_copy(ref, in_3d.at[a], in_sem.at[a]))
    for a, ref in enumerate((surface, trans_u, trans_v)):
        loads.append(pltpu.make_async_copy(ref, in_2d.at[a], in_sem.at[3 + a]))
    for a, ref in enumerate((ocean, layers)):
        loads.append(pltpu.make_async_copy(ref, in_int.at[a], in_sem.at[6 + a]))
    for load in loads:
        load.start()
    gx, gy = lax.axis_index("gx"), lax.axis_index("gy")
    nx, ny = lax.axis_size("gx"), lax.axis_size("gy")

    def exists(d):
        ok = jnp.bool_(True)
        if d[0] == -1:
            ok = jnp.logical_and(ok, gx > 0)
        if d[0] == 1:
            ok = jnp.logical_and(ok, gx < nx - 1)
        if d[1] == -1:
            ok = jnp.logical_and(ok, gy > 0)
        if d[1] == 1:
            ok = jnp.logical_and(ok, gy < ny - 1)
        return ok

    here = {d: exists(d) for d in DIRS}
    barrier = pltpu.get_barrier_semaphore()
    total_near = jnp.int32(0)
    for d in DIRS:
        total_near = total_near + here[d].astype(jnp.int32)

        @pl.when(here[d])
        def _(d=d):
            pl.semaphore_signal(barrier, inc=1, device_id=(gx + d[0], gy + d[1]), device_id_type=MESH)

    for d in DIRS:
        @pl.when(jnp.logical_not(here[d]))
        def _(d=d):
            for p in range(STEPS):
                if d[1] == 0:
                    s = 0 if d[0] < 0 else 1
                    x_recv[p, s] = jnp.zeros(x_recv.shape[2:], F32)
                    gx_recv[p, s] = jnp.zeros(gx_recv.shape[2:], F32)
                    fx_recv[p, s] = jnp.zeros(fx_recv.shape[2:], F32)
                else:
                    s = SIDES.index(d)
                    y_recv[p, s] = jnp.zeros(y_recv.shape[2:], F32)
                    gy_recv[p, s] = jnp.zeros(gy_recv.shape[2:], F32)
                    fy_recv[p, s] = jnp.zeros(fy_recv.shape[2:], F32)

    def copies(phase, step):
        result = []
        for i, d in enumerate(DIRS):
            back = (-d[0], -d[1])
            if d[1] == 0:
                src_at, dst_at = (0 if d[0] < 0 else 1), (0 if back[0] < 0 else 1)
                if phase == FORCE:
                    src, dst = fx_send.at[step], fx_recv.at[step, dst_at]
                elif phase == PLANE:
                    rows = pl.ds(0, (4 if step == 0 else 3) * ROWS)
                    src, dst = gx_send.at[step, rows], gx_recv.at[step, dst_at, rows]
                else:
                    if step == 0:
                        rows = pl.ds(0, RIM)
                    elif phase == EARLY:
                        rows = pl.ds(2 * MOVING, 2 * LEVELS)
                    else:
                        rows = pl.ds(0, 2 * MOVING)
                    src, dst = x_send.at[step, src_at, rows], x_recv.at[step, dst_at, rows]
            else:
                src_at, dst_at = (0 if d[1] < 0 else 1), SIDES.index(back)
                if phase == FORCE:
                    src, dst = fy_send.at[step, src_at], fy_recv.at[step, dst_at]
                elif phase == PLANE:
                    src, dst = gy_send.at[step, src_at], gy_recv.at[step, dst_at]
                elif phase == EARLY:
                    continue
                else:
                    src, dst = y_send.at[step, src_at], y_recv.at[step, dst_at]
                    if d[0] != 0:
                        rows = pl.ds(0, 8) if d[0] < 0 else pl.ds(8, 8)
                        src, dst = src.at[rows], dst.at[rows]
            at = phase * STEPS + step
            copy = pltpu.make_async_remote_copy(
                src_ref=src, dst_ref=dst,
                send_sem=send_sem.at[at, i], recv_sem=recv_sem.at[at, DIRS.index(back)],
                device_id=(gx + d[0], gy + d[1]), device_id_type=MESH,
            )
            result.append((d, copy))
        return result

    def start(phase, step):
        for d, copy in copies(phase, step):
            @pl.when(here[d])
            def _(copy=copy):
                copy.start()

    def arrive(phase, step):
        by_dir = dict(copies(phase, step))
        for d in by_dir:
            @pl.when(here[d])
            def _(d=d):
                by_dir[(-d[0], -d[1])].wait_recv()

    def sent(phase, step):
        for d, copy in copies(phase, step):
            @pl.when(here[d])
            def _(copy=copy):
                copy.wait_send()

    lane = lax.broadcasted_iota(jnp.int32, (ROWS, LANES), 1)
    pair = lane >> 1
    odd = (lane & 1) == 1
    zero = jnp.zeros((ROWS, LANES), F32)

    def put(step, j, near_at, far_at, cells, strips):
        x_send[step, 0, pl.ds(near_at, 1)] = cells[0:1]
        x_send[step, 0, pl.ds(far_at, 1)] = cells[1:2]
        x_send[step, 1, pl.ds(near_at, 1)] = cells[ROWS - 1 : ROWS]
        x_send[step, 1, pl.ds(far_at, 1)] = cells[ROWS - 2 : ROWS - 1]
        to_left, to_right = strips
        rolled = turn(cells, 2 * j + 2, 1)
        to_right = jnp.where(pair == j, rolled, to_right)
        to_left = jnp.where(pair == j + 1, rolled, to_left)
        return to_left, to_right

    def put_v(step, j, cells, strips):
        fx[pl.ds(EXT * j + OWN, ROWS)] = cells
        return put(step, j, j, MOVING + j, cells, strips)

    def put_b(step, k, cells, strips):
        j = MOVING + k
        return put(step, j, 2 * MOVING + k, 2 * MOVING + LEVELS + k, cells, strips)

    def send_state(step, strips, flats):
        y_send[step, 0] = strips[0]
        y_send[step, 1] = strips[1]
        start(RIMS, step)
        flat_left, flat_right = pack_flat(flats)
        gy_send[step, 0] = flat_left
        gy_send[step, 1] = flat_right
        for a, cells in enumerate(flats):
            gx_send[step, ROWS * a : ROWS * (a + 1)] = cells
        start(PLANE, step)

    for r, blocks in enumerate(lane_weights()):
        for c, block in enumerate(blocks):
            for at in (2 * r, 2 * r + 1):
                lane_w[LANES * at : LANES * (at + 1), LANES * c : LANES * (c + 1)] = block
    loads[6].wait()
    loads[7].wait()
    lay = in_int[1].astype(F32)
    code = jnp.where(in_int[0] > 0, lay, 0.0)
    strips = put(0, STACK, CODE_ROW, CODE_ROW + 1, code, (zero, zero))
    for a in range(FIELDS):
        loads[a].wait()

        def pack(k, strips, a=a):
            cells = in_3d[a, k]
            if a < 2:
                return put_v(0, a * LEVELS + k, cells, strips)
            fx[pl.ds(EXT * (MOVING + k) + OWN, ROWS)] = cells
            return put_b(0, k, cells, strips)

        strips = lax.fori_loop(0, LEVELS, pack, strips, unroll=True)
    for a in range(3):
        loads[3 + a].wait()
    pl.semaphore_wait(barrier, total_near)
    sea, flow_u, flow_v = in_2d[0], in_2d[1], in_2d[2]
    send_state(0, strips, (sea, flow_u, flow_v, code))

    for step in range(STEPS):
        arrive(RIMS, step)
        if step:
            arrive(EARLY, step)
        from_left, from_right = y_recv[step, 1], y_recv[step, 4]
        near = jnp.where(odd, from_left, turn(from_right, -2, 1))
        far = jnp.where(odd, turn(from_left, 1, 1), turn(from_right, -3, 1))
        inner = turn(jnp.where(odd, strips[1], strips[0]), -1, 1)
        near_ext[pl.ds(1, ROWS)] = near
        odd8 = odd[0:8]
        top = jnp.where(odd8, y_recv[step, 0, 8:16], turn(y_recv[step, 3, 8:16], -2, 1))
        low = jnp.where(odd8, y_recv[step, 2, 0:8], turn(y_recv[step, 5, 0:8], -2, 1))
        near_ext[pl.ds(0, 1)] = top[7:8]
        near_ext[pl.ds(ROWS + 1, 1)] = low[0:1]

        if step == 0:
            code_ext[pl.ds(0, 1)] = x_recv[0, 0, pl.ds(CODE_ROW, 1)]
            code_ext[pl.ds(ROWS + 1, 1)] = x_recv[0, 1, pl.ds(CODE_ROW, 1)]
            at = 2 * STACK
            code_near = jnp.where(
                odd,
                jnp.broadcast_to(near[:, at + 1 : at + 2], (ROWS, LANES)),
                jnp.broadcast_to(near[:, at : at + 1], (ROWS, LANES)),
            )
            act_near = ((pair & (LEVELS - 1)).astype(F32) < code_near).astype(F32)
        lap_near = act_near * (
            far + inner + near_ext[pl.ds(0, ROWS)] + near_ext[pl.ds(2, ROWS)] - 4.0 * near
        )

        def put_parts(ref, at, rows, parts, col):
            for c, part in enumerate(parts):
                ref[pl.ds(at, rows), LANES * (col + c) : LANES * (col + c + 1)] = part

        def stage(ref, first, count, source, edge):
            def one(i, carry):
                at = pl.multiple_of(ROWS * i, ROWS)
                cells = source[pl.ds(EXT * (first + i) + OWN, ROWS)]
                put_parts(ref, at, ROWS, split(cells), 0)
                put_parts(ref, at, ROWS, pick(pair == first + i, edge), 2)
                return carry

            lax.fori_loop(0, count, one, 0, unroll=True)

        def rim_rows(ref, first, count, near_at):
            row = lax.broadcasted_iota(jnp.int32, (count, LANES), 0)
            group = lax.broadcasted_iota(jnp.int32, (count, LANES), 1) >> 1
            for side in range(2):
                cells = x_recv[step, side, pl.ds(near_at, count)]
                at = ROWS * count + count * side
                corner = jnp.broadcast_to(
                    near_ext[pl.ds((ROWS + 1) * side, 1)], (count, LANES)
                )
                put_parts(ref, at, count, split(cells), 0)
                put_parts(ref, at, count, pick(group == first + row, corner), 2)
                fx[pl.ds(EXT * first + (OWN - 1, OWN + ROWS)[side], count, stride=EXT)] = cells

        def rim_laps(ref, first, count, near_at, far_at):
            level_of = lax.broadcasted_iota(jnp.int32, (count, LANES), 0) & (LEVELS - 1)
            for side in range(2):
                cells = x_recv[step, side, pl.ds(near_at, count)]
                beside = x_recv[step, side, pl.ds(far_at, count)] + x_send[
                    step, side, pl.ds(near_at, count)
                ]
                lanes_sum = ref[pl.ds(ROWS * count + count * side, count), 0:LANES]
                code_row = code_ext[pl.ds((ROWS + 1) * side, 1)]
                lap = jnp.where(
                    level_of.astype(F32) < code_row, beside + lanes_sum - 4.0 * cells, 0.0
                )
                lp[pl.ds(EXT * first + (OWN - 1, OWN + ROWS)[side], count, stride=EXT)] = lap

        def laplace(j, source, lanes_sum):
            at = EXT * j + OWN
            return (
                source[pl.ds(at - 1, ROWS)] + source[pl.ds(at + 1, ROWS)]
                + lanes_sum - 4.0 * source[pl.ds(at, ROWS)]
            )

        def own_laps(ref, first, count):
            def one(i, carry):
                level_at = lax.convert_element_type(i & (LEVELS - 1), F32)
                lanes_sum = ref[pl.ds(pl.multiple_of(ROWS * i, ROWS), ROWS), 0:LANES]
                lap = laplace(first + i, fx, lanes_sum)
                lp[pl.ds(EXT * (first + i) + OWN, ROWS)] = jnp.where(level_at < code, lap, 0.0)
                return carry

            lax.fori_loop(0, count, one, 0, unroll=True)

        def apply(source, rows, width):
            return jnp.dot(
                source[0:rows], lane_w[:, 0:width], preferred_element_type=F32
            )

        rows_uv, rows_b = MOVING * ROWS, LEVELS * ROWS
        rim_rows(buoy_in, MOVING, LEVELS, 2 * MOVING)
        stage(buoy_in, MOVING, LEVELS, fx, near)
        buoy_out[...] = apply(buoy_in, rows_b + 2 * LEVELS, 2 * LANES)
        rim_rows(mom_in, 0, MOVING, 0)
        stage(mom_in, 0, MOVING, fx, near)
        mom_out[...] = apply(mom_in, rows_uv + 2 * MOVING, LANES)
        rim_laps(mom_out, 0, MOVING, 0, MOVING)
        own_laps(mom_out, 0, MOVING)
        stage(mom_in, 0, MOVING, lp, lap_near)
        mom_out[0:rows_uv] = apply(mom_in, rows_uv, LANES)

        def buoyancy(k, carry):
            act = lax.convert_element_type(k, F32) < code
            at = EXT * (MOVING + k) + OWN
            rows = pl.ds(pl.multiple_of(ROWS * k, ROWS), ROWS)
            bih_b = laplace(MOVING + k, lp, buoy_out[rows, 0:LANES])
            u, v = fx[pl.ds(EXT * k + OWN, ROWS)], fx[pl.ds(EXT * (LEVELS + k) + OWN, ROWS)]
            b = fx[pl.ds(at, ROWS)]
            b_x = fx[pl.ds(at + 1, ROWS)] - fx[pl.ds(at - 1, ROWS)]
            b_y = buoy_out[rows, LANES : 2 * LANES]
            tend_b = -0.5 * (u * b_x + v * b_y) - 0.02 * bih_b
            new_b = jnp.where(act, b + 0.2 * tend_b, 0.0)
            if step == STEPS - 1:
                out_b[k] = new_b
            else:
                in_3d[2, k] = new_b
            return carry

        def level(k, carry):
            press_x, press_y, force_u, force_v, col_u, col_v = carry
            act = (lax.convert_element_type(k, F32) < code).astype(F32)
            rows = pl.ds(pl.multiple_of(ROWS * k, ROWS), ROWS)
            rows_v = pl.ds(pl.multiple_of(ROWS * (LEVELS + k), ROWS), ROWS)
            bih_u = laplace(k, lp, mom_out[rows])
            bih_v = laplace(LEVELS + k, lp, mom_out[rows_v])
            u, v = fx[pl.ds(EXT * k + OWN, ROWS)], fx[pl.ds(EXT * (LEVELS + k) + OWN, ROWS)]
            at = EXT * (MOVING + k) + OWN
            press_x = press_x + (fx[pl.ds(at + 1, ROWS)] - fx[pl.ds(at - 1, ROWS)])
            press_y = press_y + buoy_out[rows, LANES : 2 * LANES]
            tend_u = (-0.25 / LEVELS) * press_x + 0.1 * v - 0.02 * bih_u
            tend_v = (-0.25 / LEVELS) * press_y - 0.1 * u - 0.02 * bih_v
            su = act * (u + 0.2 * tend_u)
            sv = act * (v + 0.2 * tend_v)
            star_u[k] = su
            star_v[k] = sv
            return (
                press_x, press_y, force_u + act * tend_u, force_v + act * tend_v,
                col_u + su, col_v + sv,
            )

        _, _, force_u, force_v, col_u, col_v = lax.fori_loop(
            0, LEVELS, level, (zero,) * 6, unroll=True
        )
        force_u, force_v = force_u / LEVELS, force_v / LEVELS
        fx_send[step, 0:ROWS] = force_u
        fx_send[step, ROWS : 2 * ROWS] = force_v
        flat_left, flat_right = pack_flat((force_u, force_v))
        fy_send[step, 0] = flat_left
        fy_send[step, 1] = flat_right
        start(FORCE, step)
        rim_laps(buoy_out, MOVING, LEVELS, 2 * MOVING, 2 * MOVING + LEVELS)
        own_laps(buoy_out, MOVING, LEVELS)
        stage(buoy_in, MOVING, LEVELS, lp, lap_near)
        buoy_out[0:rows_b, 0:LANES] = apply(buoy_in, rows_b, LANES)
        lax.fori_loop(0, LEVELS, buoyancy, 0, unroll=True)
        if step < STEPS - 1:
            def pack_b(k, strips):
                cells = in_3d[2, k]
                fx[pl.ds(EXT * (MOVING + k) + OWN, ROWS)] = cells
                return put_b(step + 1, k, cells, strips)

            strips = lax.fori_loop(0, LEVELS, pack_b, (zero, zero), unroll=True)
            start(EARLY, step + 1)
        arrive(PLANE, step)
        sides = [gy_recv[step, r] for r in range(6)]

        def plane(own, a):
            rows = slice(ROWS * a, ROWS * (a + 1))
            return wide(own, gx_recv[step, 0, rows], gx_recv[step, 1, rows], sides, a)

        if step == 0:
            code_wide = plane(code, 3)
        state = (plane(sea, 0), plane(flow_u, 1), plane(flow_v, 2))
        arrive(FORCE, step)
        sides_f = [fy_recv[step, r] for r in range(6)]
        push_u, push_v = (
            0.2 * wide(
                own, fx_recv[step, 0, ROWS * a : ROWS * (a + 1)],
                fx_recv[step, 1, ROWS * a : ROWS * (a + 1)], sides_f, a,
            )
            for a, own in enumerate((force_u, force_v))
        )
        (sea, flow_u, flow_v), sum_u, sum_v = barotropic(state, push_u, push_v, code_wide)
        scale = LEVELS / SUB
        shift_u = (scale * sum_u - col_u) / lay
        shift_v = (scale * sum_v - col_v) / lay
        if step < STEPS - 1:
            def couple(k, strips):
                act = (lax.convert_element_type(k, F32) < code).astype(F32)
                strips = put_v(step + 1, k, act * (star_u[k] + shift_u), strips)
                return put_v(step + 1, LEVELS + k, act * (star_v[k] + shift_v), strips)

            strips = lax.fori_loop(0, LEVELS, couple, strips, unroll=True)
            send_state(step + 1, strips, (sea, flow_u, flow_v))
        else:
            def finish(k, carry):
                act = lax.convert_element_type(k, F32) < code
                out_u[k] = jnp.where(act, star_u[k] + shift_u, 0.0)
                out_v[k] = jnp.where(act, star_v[k] + shift_v, 0.0)
                return carry

            lax.fori_loop(0, LEVELS, finish, 0, unroll=True)
            out_eta[...] = sea
            out_tu[...] = flow_u
            out_tv[...] = flow_v

    for step in range(STEPS):
        for phase in (RIMS, FORCE, PLANE, EARLY):
            if phase != EARLY or step:
                sent(phase, step)


def per_device(velocity_u, velocity_v, buoyancy, surface, transport_u, transport_v, ocean, layers):
    cube = jax.ShapeDtypeStruct(velocity_u.shape, F32)
    flat = jax.ShapeDtypeStruct(surface.shape, F32)
    hbm = pl.BlockSpec(memory_space=pltpu.HBM)
    vmem = pl.BlockSpec(memory_space=pltpu.VMEM)
    outs = (cube, cube, cube, flat, flat, flat)
    args = [
        pltpu.with_memory_space_constraint(x, pltpu.HBM)
        for x in (velocity_u, velocity_v, buoyancy, surface, transport_u, transport_v, ocean, layers)
    ]
    ext = 24
    block = (LEVELS, ROWS, LANES)
    middle = pl.pallas_call(
        kernel,
        out_shape=outs,
        in_specs=[hbm] * 8,
        out_specs=(vmem,) * 6,
        scratch_shapes=[
            pltpu.VMEM(block, F32),
            pltpu.VMEM(block, F32),
            pltpu.VMEM((STACK * EXT, LANES), F32),
            pltpu.VMEM((STACK * EXT, LANES), F32),
            pltpu.VMEM((ext, LANES), F32),
            pltpu.VMEM((ext, LANES), F32),
            pltpu.VMEM((FIELDS,) + block, F32),
            pltpu.VMEM((3, ROWS, LANES), F32),
            pltpu.VMEM((2, ROWS, LANES), jnp.int32),
            pltpu.VMEM((4 * LANES, 2 * LANES), BF16),
            pltpu.VMEM((MOVING * (ROWS + 2), 4 * LANES), BF16),
            pltpu.VMEM((LEVELS * (ROWS + 2), 4 * LANES), BF16),
            pltpu.VMEM((MOVING * (ROWS + 2), LANES), F32),
            pltpu.VMEM((LEVELS * (ROWS + 2), 2 * LANES), F32),
            pltpu.VMEM((STEPS, 2, RIM, LANES), F32),
            pltpu.VMEM((STEPS, 2, ROWS, LANES), F32),
            pltpu.VMEM((STEPS, 2, RIM, LANES), F32),
            pltpu.VMEM((STEPS, 6, ROWS, LANES), F32),
            pltpu.VMEM((STEPS, 4 * ROWS, LANES), F32),
            pltpu.VMEM((STEPS, 2, 8, LANES), F32),
            pltpu.VMEM((STEPS, 2, 4 * ROWS, LANES), F32),
            pltpu.VMEM((STEPS, 6, 8, LANES), F32),
            pltpu.VMEM((STEPS, 2 * ROWS, LANES), F32),
            pltpu.VMEM((STEPS, 2, 8, LANES), F32),
            pltpu.VMEM((STEPS, 2, 2 * ROWS, LANES), F32),
            pltpu.VMEM((STEPS, 6, 8, LANES), F32),
            pltpu.SemaphoreType.DMA((8,)),
            pltpu.SemaphoreType.DMA((4 * STEPS, 8)),
            pltpu.SemaphoreType.DMA((4 * STEPS, 8)),
        ],
        compiler_params=pltpu.CompilerParams(
            collective_id=0, has_side_effects=True, vmem_limit_bytes=16 * 2**20
        ),
    )(*args)
    return tuple(
        pl.pallas_call(
            store_kernel,
            out_shape=outs,
            in_specs=[vmem] * 6,
            out_specs=(hbm,) * 6,
            scratch_shapes=[pltpu.SemaphoreType.DMA((6,))],
            compiler_params=pltpu.CompilerParams(vmem_limit_bytes=16 * 2**20),
        )(*middle)
    )


def solution(mesh):
    cube, flat = P(None, "gx", "gy"), P("gx", "gy")
    return jax.shard_map(
        per_device,
        mesh=mesh,
        in_specs=(cube, cube, cube, flat, flat, flat, flat, flat),
        out_specs=(cube, cube, cube, flat, flat, flat),
        check_vma=False,
    )
```

```python
import jax
import jax.numpy as jnp
from jax import lax
from jax.experimental import pallas as pl
from jax.experimental.pallas import tpu as pltpu
from jax.sharding import PartitionSpec as P

SUB = 8
STEPS = 2
LANES = 128
ROWS = 16
LEVELS = 16
FIELDS = 3
STACK = FIELDS * LEVELS
MESH = pl.DeviceIdType.MESH
F32 = jnp.float32
BF16 = jnp.bfloat16

DIRS = [(-1, 0), (1, 0), (0, -1), (0, 1), (-1, -1), (-1, 1), (1, -1), (1, 1)]
SIDES = [(-1, -1), (0, -1), (1, -1), (-1, 1), (0, 1), (1, 1)]
MOVING = 2 * LEVELS
FLAT_ROW = 2 * MOVING
BUOY_NEAR = FLAT_ROW + 8
BUOY_FAR = BUOY_NEAR + LEVELS
RIM = BUOY_FAR + LEVELS
HALF = LANES // 2


RIMS, FORCE, PLANE, EARLY = 0, 1, 2, 3
EXT = 32
OWN = 8
SCALE = LEVELS / SUB


def turn(x, shift, axis):
    return pltpu.roll(x, shift % x.shape[axis] if isinstance(shift, int) else shift, axis)


def fold(cells):
    low = lax.broadcasted_iota(jnp.int32, (8, LANES), 1) < HALF
    return jnp.where(low, cells[0:8], turn(cells[8:16], HALF, 1))


def unfold(cells):
    return jnp.concatenate([cells, turn(cells, HALF, 1)], axis=0)


def split(x):
    high = x.astype(BF16)
    return high, (x - high.astype(F32)).astype(BF16)


def pick(mask, x):
    return tuple(jnp.where(mask, part.astype(F32), 0.0).astype(BF16) for part in split(x))


def lane_weights():
    src = lax.broadcasted_iota(jnp.int32, (LANES, LANES), 0)
    dst = lax.broadcasted_iota(jnp.int32, (LANES, LANES), 1)
    ahead, behind = (src == dst + 1).astype(F32), (src == dst - 1).astype(F32)
    odd = (src & 1) == 1
    first = jnp.logical_and(odd, dst == 0).astype(F32)
    last = jnp.logical_and(jnp.logical_not(odd), dst == LANES - 1).astype(F32)
    return [
        [(ahead + behind).astype(BF16), (ahead - behind).astype(BF16)],
        [(last + first).astype(BF16), (last - first).astype(BF16)],
    ]


def pack_flat(arrays):
    lane = lax.broadcasted_iota(jnp.int32, (ROWS, LANES), 1)
    to_left = to_right = jnp.zeros((ROWS, LANES), F32)
    for a, cells in enumerate(arrays):
        to_right = jnp.where((lane >> 4) == a, turn(cells, 16 * a + 16, 1), to_right)
        to_left = jnp.where((lane >> 4) == a, turn(cells, 16 * a, 1), to_left)
    return fold(to_left), fold(to_right)


def wide(own, up, down, sides, a):
    lane = lax.broadcasted_iota(jnp.int32, (ROWS, LANES), 1)
    blocks = []
    for r in range(3):
        from_left, from_right = unfold(sides[r]), unfold(sides[r + 3])
        left, right = turn(from_left, 112 - 16 * a, 1), turn(from_right, -16 * a, 1)
        blocks.append(jnp.where(lane < 16, right, jnp.where(lane >= 112, left, 0.0)))
    main = jnp.concatenate([up, own, down], axis=0)
    return jnp.concatenate([main, jnp.concatenate(blocks, axis=0)], axis=1)


def substep(eta, tu, tv, wet, depth, push=None):
    div = (turn(tu, -1, 0) - turn(tu, 1, 0)) + (turn(tv, -1, 1) - turn(tv, 1, 1))
    eta = wet * (eta - 0.125 * div)
    thick = 0.125 * (depth + eta)
    new_u = 0.98 * tu - thick * (turn(eta, -1, 0) - turn(eta, 1, 0)) + 0.05 * tv
    new_v = 0.98 * tv - thick * (turn(eta, -1, 1) - turn(eta, 1, 1)) - 0.05 * tu
    if push is not None:
        new_u, new_v = new_u + push[0], new_v + push[1]
    return eta, wet * new_u, wet * new_v


def barotropic(state, push, wet, depth):
    eta, tu, tv = state
    tu, tv = tu + wet * push[0], tv + wet * push[1]

    def one(_, carry):
        eta, tu, tv, sum_u, sum_v = carry
        eta, tu, tv = substep(eta, tu, tv, wet, depth, push)
        return eta, tu, tv, sum_u + tu, sum_v + tv

    return lax.fori_loop(0, SUB - 1, one, (eta, tu, tv, tu, tv), unroll=True)


def inside(cells):
    return cells[ROWS : 2 * ROWS, 0:LANES]


def lane_pair(odd, cells, even_at, odd_at):
    shape = odd.shape
    return jnp.where(
        odd,
        jnp.broadcast_to(cells[:, odd_at : odd_at + 1], shape),
        jnp.broadcast_to(cells[:, even_at : even_at + 1], shape),
    )


def store_kernel(*refs):
    count = (len(refs) - 1) // 2
    sem = refs[-1]
    copies = [
        pltpu.make_async_copy(src, dst, sem.at[i])
        for i, (src, dst) in enumerate(zip(refs[:count], refs[count:-1]))
    ]
    for copy in copies:
        copy.start()
    for copy in copies:
        copy.wait()


def kernel(
    vel_u, vel_v, buoy, surface, trans_u, trans_v, ocean, layers,
    out_u, out_v, out_b, out_eta, out_tu, out_tv,
    star_u, star_v,
    fx, lp, near_ext, ring_rows, rim_new, in_3d, in_2d, in_int,
    lane_w, mom_in, buoy_in, mom_out, buoy_out,
    x_send, y_send, x_recv, y_recv, gx_send, gy_send, gx_recv, gy_recv,
    fx_send, fy_send, fx_recv, fy_recv, in_sem, send_sem, recv_sem,
):
    loads = []
    for a, ref in enumerate((vel_u, vel_v, buoy)):
        loads.append(pltpu.make_async_copy(ref, in_3d.at[a], in_sem.at[a]))
    for a, ref in enumerate((surface, trans_u, trans_v)):
        loads.append(pltpu.make_async_copy(ref, in_2d.at[a], in_sem.at[3 + a]))
    for a, ref in enumerate((ocean, layers)):
        loads.append(pltpu.make_async_copy(ref, in_int.at[a], in_sem.at[6 + a]))
    for load in loads:
        load.start()
    gx, gy = lax.axis_index("gx"), lax.axis_index("gy")
    nx, ny = lax.axis_size("gx"), lax.axis_size("gy")

    def exists(d):
        ok = jnp.bool_(True)
        if d[0] == -1:
            ok = jnp.logical_and(ok, gx > 0)
        if d[0] == 1:
            ok = jnp.logical_and(ok, gx < nx - 1)
        if d[1] == -1:
            ok = jnp.logical_and(ok, gy > 0)
        if d[1] == 1:
            ok = jnp.logical_and(ok, gy < ny - 1)
        return ok

    here = {d: exists(d) for d in DIRS}
    barrier = pltpu.get_barrier_semaphore()
    total_near = jnp.int32(0)
    for d in DIRS:
        total_near = total_near + here[d].astype(jnp.int32)

        @pl.when(here[d])
        def _(d=d):
            pl.semaphore_signal(barrier, inc=1, device_id=(gx + d[0], gy + d[1]), device_id_type=MESH)

    for d in DIRS:
        @pl.when(jnp.logical_not(here[d]))
        def _(d=d):
            for p in range(STEPS):
                if d[1] == 0:
                    s = 0 if d[0] < 0 else 1
                    x_recv[p, s] = jnp.zeros(x_recv.shape[2:], F32)
                    gx_recv[p, s] = jnp.zeros(gx_recv.shape[2:], F32)
                    fx_recv[p, s] = jnp.zeros(fx_recv.shape[2:], F32)
                else:
                    s = SIDES.index(d)
                    y_recv[p, s] = jnp.zeros(y_recv.shape[2:], F32)
                    gy_recv[p, s] = jnp.zeros(gy_recv.shape[2:], F32)
                    fy_recv[p, s] = jnp.zeros(fy_recv.shape[2:], F32)

    def copies(phase, step):
        result = []
        for i, d in enumerate(DIRS):
            back = (-d[0], -d[1])
            if d[1] == 0:
                src_at, dst_at = (0 if d[0] < 0 else 1), (0 if back[0] < 0 else 1)
                if phase == FORCE:
                    src, dst = fx_send.at[step], fx_recv.at[step, dst_at]
                elif phase == PLANE:
                    rows = pl.ds(0, (4 if step == 0 else 3) * ROWS)
                    src, dst = gx_send.at[step, rows], gx_recv.at[step, dst_at, rows]
                else:
                    if step == 0:
                        rows = pl.ds(0, RIM)
                    elif phase == EARLY:
                        rows = pl.ds(BUOY_NEAR, 2 * LEVELS)
                    else:
                        rows = pl.ds(0, BUOY_NEAR)
                    src, dst = x_send.at[step, src_at, rows], x_recv.at[step, dst_at, rows]
            else:
                src_at, dst_at = (0 if d[1] < 0 else 1), SIDES.index(back)
                if phase == FORCE:
                    src, dst = fy_send.at[step, src_at], fy_recv.at[step, dst_at]
                elif phase == PLANE:
                    src, dst = gy_send.at[step, src_at], gy_recv.at[step, dst_at]
                elif step and phase == RIMS:
                    continue
                else:
                    src, dst = y_send.at[step, src_at], y_recv.at[step, dst_at]
                    if d[0] != 0:
                        rows = pl.ds(0, 8) if d[0] < 0 else pl.ds(8, 8)
                        src, dst = src.at[rows], dst.at[rows]
            at = phase * STEPS + step
            copy = pltpu.make_async_remote_copy(
                src_ref=src, dst_ref=dst,
                send_sem=send_sem.at[at, i], recv_sem=recv_sem.at[at, DIRS.index(back)],
                device_id=(gx + d[0], gy + d[1]), device_id_type=MESH,
            )
            result.append((d, copy))
        return result

    def start(phase, step):
        for d, copy in copies(phase, step):
            @pl.when(here[d])
            def _(copy=copy):
                copy.start()

    def arrive(phase, step):
        by_dir = dict(copies(phase, step))
        for d in by_dir:
            @pl.when(here[d])
            def _(d=d):
                by_dir[(-d[0], -d[1])].wait_recv()

    def sent(phase, step):
        for d, copy in copies(phase, step):
            @pl.when(here[d])
            def _(copy=copy):
                copy.wait_send()

    lane = lax.broadcasted_iota(jnp.int32, (ROWS, LANES), 1)
    pair = lane >> 1
    odd = (lane & 1) == 1
    zero = jnp.zeros((ROWS, LANES), F32)

    def put(step, j, near_at, far_at, cells, strips):
        x_send[step, 0, pl.ds(near_at, 1)] = cells[0:1]
        x_send[step, 0, pl.ds(far_at, 1)] = cells[1:2]
        x_send[step, 1, pl.ds(near_at, 1)] = cells[ROWS - 1 : ROWS]
        x_send[step, 1, pl.ds(far_at, 1)] = cells[ROWS - 2 : ROWS - 1]
        to_left, to_right = strips
        rolled = turn(cells, 2 * j + 2, 1)
        to_right = jnp.where(pair == j, rolled, to_right)
        to_left = jnp.where(pair == j + 1, rolled, to_left)
        return to_left, to_right

    def put_v(step, j, cells, strips):
        return put(step, j, j, MOVING + j, cells, strips)

    def put_b(step, k, cells, strips):
        j = MOVING + k
        return put(step, j, BUOY_NEAR + k, BUOY_FAR + k, cells, strips)

    def put_flat(step, a, cells, strips):
        return put(step, STACK + a, FLAT_ROW + 2 * a, FLAT_ROW + 2 * a + 1, cells, strips)

    def send_plane(step, flats):
        flat_left, flat_right = pack_flat(flats)
        gy_send[step, 0] = flat_left
        gy_send[step, 1] = flat_right
        for a, cells in enumerate(flats):
            gx_send[step, ROWS * a : ROWS * (a + 1)] = cells
        start(PLANE, step)

    ring_rows[...] = jnp.zeros(ring_rows.shape, F32)
    for r, blocks in enumerate(lane_weights()):
        for c, block in enumerate(blocks):
            for at in (2 * r, 2 * r + 1):
                lane_w[LANES * at : LANES * (at + 1), LANES * c : LANES * (c + 1)] = block
    loads[6].wait()
    loads[7].wait()
    lay = in_int[1].astype(F32)
    code = jnp.where(in_int[0] > 0, lay, 0.0)
    strips = put_flat(0, 0, code, (zero, zero))
    for a in range(FIELDS):
        loads[a].wait()

        def pack(k, strips, a=a):
            cells = in_3d[a, k]
            fx[pl.ds(EXT * (a * LEVELS + k) + OWN, ROWS)] = cells
            if a < 2:
                return put_v(0, a * LEVELS + k, cells, strips)
            return put_b(0, k, cells, strips)

        strips = lax.fori_loop(0, LEVELS, pack, strips, unroll=True)
    flats = [code]
    for a in range(3):
        loads[3 + a].wait()
        flats.append(in_2d[a])
        strips = put_flat(0, 1 + a, in_2d[a], strips)
    y_send[0, 0] = strips[0]
    y_send[0, 1] = strips[1]
    pl.semaphore_wait(barrier, total_near)
    start(RIMS, 0)

    around = (ROWS + 8, LANES)
    lane24 = lax.broadcasted_iota(jnp.int32, around, 1)
    odd24 = (lane24 & 1) == 1
    level24 = ((lane24 >> 1) & (LEVELS - 1)).astype(F32)
    level_pair = level24[0:ROWS]
    moving24 = lane24 < 2 * MOVING
    is_u24 = lane24 < 2 * LEVELS
    upper = lax.broadcasted_iota(jnp.int32, (8, LANES), 0) < 4

    def cyclic(own, below, above):
        return jnp.concatenate([own, jnp.where(upper, below, above)], axis=0)

    def beside_columns(left24, right24, j):
        return jnp.where(
            lane24 < HALF, turn(right24, -2 * j - 2, 1), turn(left24, 126 - 2 * j, 1)
        )

    def side24(cells):
        tile = cells[:, LANES : 2 * LANES]
        return cyclic(tile[ROWS : 2 * ROWS], tile[2 * ROWS : 2 * ROWS + 8], tile[8:ROWS])

    for step in range(STEPS):
        if step == 0:
            arrive(RIMS, step)
        else:
            arrive(RIMS, step)
            arrive(EARLY, step)
        left24 = cyclic(y_recv[step, 1], y_recv[step, 2, 0:8], y_recv[step, 0, 8:16])
        right24 = cyclic(y_recv[step, 4], y_recv[step, 5, 0:8], y_recv[step, 3, 8:16])
        near24 = jnp.where(odd24, left24, turn(right24, -2, 1))
        far = jnp.where(odd, turn(left24[0:ROWS], 1, 1), turn(right24[0:ROWS], -3, 1))
        inner = turn(jnp.where(odd, strips[1], strips[0]), -1, 1)

        if step == 0:
            code_near = lane_pair(odd24, near24, 2 * STACK, 2 * STACK + 1)
            code_far = lane_pair(odd, far, 2 * STACK, 2 * STACK + 1)
            code_inner = lane_pair(odd, code, LANES - 1, 0)
            act_near = level24 < code_near
        else:
            shift_side = [
                (SCALE * side24(total) - beside_columns(left24, right24, STACK + 1 + a))
                / jnp.maximum(code_side, 1.0)
                for a, total in enumerate((sum_u, sum_v))
            ]

            def couple_pairs(cells, near_code, rows, levels, even_at, odd_at, sources):
                parity = odd24[0:rows]
                shift = jnp.where(
                    is_u24[0:rows],
                    lane_pair(parity, sources[0][0:rows], even_at, odd_at),
                    lane_pair(parity, sources[1][0:rows], even_at, odd_at),
                )
                moved = jnp.where(levels < near_code, cells + shift, 0.0)
                return jnp.where(moving24[0:rows], moved, cells)

            near24 = couple_pairs(
                near24, code_near, ROWS + 8, level24, 0, LANES - 1, shift_side
            )
            far = couple_pairs(far, code_far, ROWS, level_pair, 1, LANES - 2, shift_side)
            inner = couple_pairs(
                inner, code_inner, ROWS, level_pair, LANES - 1, 0, (shift_u, shift_v)
            )
            level16 = lax.broadcasted_iota(jnp.int32, (LEVELS, LANES), 0).astype(F32)
            for side in range(2):
                for away in range(2):
                    at = (ROWS - 1 - away, 2 * ROWS + away)[side]
                    code_row = x_recv[0, side, pl.ds(FLAT_ROW + away, 1)]
                    for a, total in enumerate((sum_u, sum_v)):
                        column = x_recv[1, side, pl.ds(FLAT_ROW + 2 * (1 + a) + away, 1)]
                        shift = (
                            SCALE * total[at : at + 1, 0:LANES] - column
                        ) / jnp.maximum(code_row, 1.0)
                        rows = pl.ds(MOVING * away + LEVELS * a, LEVELS)
                        rim_new[side, rows] = jnp.where(
                            level16 < code_row, x_recv[1, side, rows] + shift, 0.0
                        )

        near_ext[...] = near24
        near = near24[0:ROWS]
        lap_near = jnp.where(
            act_near,
            turn(near24, 1, 0) + turn(near24, -1, 0) - 4.0 * near24,
            0.0,
        )[0:ROWS] + jnp.where(act_near[0:ROWS], far + inner, 0.0)

        def rim_cells(side, first, count, at):
            if first == 0 and step:
                return rim_new[side, pl.ds(at, count)]
            return x_recv[step, side, pl.ds(at, count)]

        def put_parts(ref, at, rows, parts, col):
            for c, part in enumerate(parts):
                ref[pl.ds(at, rows), LANES * (col + c) : LANES * (col + c + 1)] = part

        def stage(ref, first, count, source, edge):
            def one(i, carry):
                at = pl.multiple_of(ROWS * i, ROWS)
                cells = source[pl.ds(EXT * (first + i) + OWN, ROWS)]
                put_parts(ref, at, ROWS, split(cells), 0)
                put_parts(ref, at, ROWS, pick(pair == first + i, edge), 2)
                return carry

            lax.fori_loop(0, count, one, 0, unroll=True)

        def rim_rows(ref, first, count, near_at):
            row = lax.broadcasted_iota(jnp.int32, (count, LANES), 0)
            group = lax.broadcasted_iota(jnp.int32, (count, LANES), 1) >> 1
            for side in range(2):
                cells = rim_cells(side, first, count, near_at)
                at = ROWS * count + count * side
                corner = jnp.broadcast_to(
                    near_ext[pl.ds((ROWS + 7, ROWS)[side], 1)], (count, LANES)
                )
                put_parts(ref, at, count, split(cells), 0)
                put_parts(ref, at, count, pick(group == first + row, corner), 2)
                fx[pl.ds(EXT * first + (OWN - 1, OWN + ROWS)[side], count, stride=EXT)] = cells

        def rim_laps(ref, first, count, near_at, far_at):
            level_of = lax.broadcasted_iota(jnp.int32, (count, LANES), 0) & (LEVELS - 1)
            for side in range(2):
                cells = rim_cells(side, first, count, near_at)
                edge = EXT * first + (OWN, OWN + ROWS - 1)[side]
                beside = rim_cells(side, first, count, far_at) + fx[
                    pl.ds(edge, count, stride=EXT)
                ]
                lanes_sum = ref[pl.ds(ROWS * count + count * side, count), 0:LANES]
                code_row = x_recv[0, side, pl.ds(FLAT_ROW, 1)]
                lap = jnp.where(
                    level_of.astype(F32) < code_row, beside + lanes_sum - 4.0 * cells, 0.0
                )
                lp[pl.ds(EXT * first + (OWN - 1, OWN + ROWS)[side], count, stride=EXT)] = lap

        def laplace(j, source, lanes_sum):
            at = EXT * j + OWN
            return (
                source[pl.ds(at - 1, ROWS)] + source[pl.ds(at + 1, ROWS)]
                + lanes_sum - 4.0 * source[pl.ds(at, ROWS)]
            )

        def own_laps(ref, first, count):
            def one(i, carry):
                level_at = lax.convert_element_type(i & (LEVELS - 1), F32)
                lanes_sum = ref[pl.ds(pl.multiple_of(ROWS * i, ROWS), ROWS), 0:LANES]
                lap = laplace(first + i, fx, lanes_sum)
                lp[pl.ds(EXT * (first + i) + OWN, ROWS)] = jnp.where(level_at < code, lap, 0.0)
                return carry

            lax.fori_loop(0, count, one, 0, unroll=True)

        def apply(source, rows, width):
            return jnp.dot(
                source[0:rows], lane_w[:, 0:width], preferred_element_type=F32
            )

        rows_uv, rows_b = MOVING * ROWS, LEVELS * ROWS
        rim_rows(buoy_in, MOVING, LEVELS, BUOY_NEAR)
        stage(buoy_in, MOVING, LEVELS, fx, near)
        buoy_out[...] = apply(buoy_in, rows_b + 2 * LEVELS, 2 * LANES)
        if step == 0:
            grids = []
            for a, own in enumerate(flats):
                near_at, far_at = FLAT_ROW + 2 * a, FLAT_ROW + 2 * a + 1
                ring_rows[a, 0:1] = x_recv[0, 1, pl.ds(near_at, 1)]
                ring_rows[a, 1:2] = x_recv[0, 1, pl.ds(far_at, 1)]
                ring_rows[a, 6:7] = x_recv[0, 0, pl.ds(far_at, 1)]
                ring_rows[a, 7:8] = x_recv[0, 0, pl.ds(near_at, 1)]
                main = jnp.concatenate([own, ring_rows[a]], axis=0)
                grids.append(jnp.concatenate(
                    [main, beside_columns(left24, right24, STACK + a)], axis=1
                ))
            code_side = grids[0][:, LANES : 2 * LANES]
            ahead = substep(
                *grids[1:], (grids[0] > 0.0).astype(F32), grids[0] / LEVELS
            )
            flats = [cells[0:ROWS, 0:LANES] for cells in ahead]
            send_plane(step, flats + [code])
        else:
            flats = [inside(c) for c in substep(eta, flow_u, flow_v, wet, depth)]
            send_plane(step, flats)
        rim_rows(mom_in, 0, MOVING, 0)
        stage(mom_in, 0, MOVING, fx, near)
        mom_out[...] = apply(mom_in, rows_uv + 2 * MOVING, LANES)
        rim_laps(mom_out, 0, MOVING, 0, MOVING)
        own_laps(mom_out, 0, MOVING)
        stage(mom_in, 0, MOVING, lp, lap_near)
        mom_out[0:rows_uv] = apply(mom_in, rows_uv, LANES)

        def buoyancy(k, carry):
            act = lax.convert_element_type(k, F32) < code
            at = EXT * (MOVING + k) + OWN
            rows = pl.ds(pl.multiple_of(ROWS * k, ROWS), ROWS)
            bih_b = laplace(MOVING + k, lp, buoy_out[rows, 0:LANES])
            u, v = fx[pl.ds(EXT * k + OWN, ROWS)], fx[pl.ds(EXT * (LEVELS + k) + OWN, ROWS)]
            b = fx[pl.ds(at, ROWS)]
            b_x = fx[pl.ds(at + 1, ROWS)] - fx[pl.ds(at - 1, ROWS)]
            b_y = buoy_out[rows, LANES : 2 * LANES]
            tend_b = -0.5 * (u * b_x + v * b_y) - 0.02 * bih_b
            new_b = jnp.where(act, b + 0.2 * tend_b, 0.0)
            if step == STEPS - 1:
                out_b[k] = new_b
            else:
                in_3d[2, k] = new_b
            return carry

        def level(k, carry):
            press_x, press_y, force_u, force_v, col_u, col_v = carry
            act = (lax.convert_element_type(k, F32) < code).astype(F32)
            rows = pl.ds(pl.multiple_of(ROWS * k, ROWS), ROWS)
            rows_v = pl.ds(pl.multiple_of(ROWS * (LEVELS + k), ROWS), ROWS)
            bih_u = laplace(k, lp, mom_out[rows])
            bih_v = laplace(LEVELS + k, lp, mom_out[rows_v])
            u, v = fx[pl.ds(EXT * k + OWN, ROWS)], fx[pl.ds(EXT * (LEVELS + k) + OWN, ROWS)]
            at = EXT * (MOVING + k) + OWN
            press_x = press_x + (fx[pl.ds(at + 1, ROWS)] - fx[pl.ds(at - 1, ROWS)])
            press_y = press_y + buoy_out[rows, LANES : 2 * LANES]
            tend_u = (-0.25 / LEVELS) * press_x + 0.1 * v - 0.02 * bih_u
            tend_v = (-0.25 / LEVELS) * press_y - 0.1 * u - 0.02 * bih_v
            su = act * (u + 0.2 * tend_u)
            sv = act * (v + 0.2 * tend_v)
            star_u[k] = su
            star_v[k] = sv
            return (
                press_x, press_y, force_u + act * tend_u, force_v + act * tend_v,
                col_u + su, col_v + sv,
            )

        _, _, force_u, force_v, col_u, col_v = lax.fori_loop(
            0, LEVELS, level, (zero,) * 6, unroll=True
        )
        force_u, force_v = force_u / LEVELS, force_v / LEVELS
        fx_send[step, 0:ROWS] = force_u
        fx_send[step, ROWS : 2 * ROWS] = force_v
        flat_left, flat_right = pack_flat((force_u, force_v))
        fy_send[step, 0] = flat_left
        fy_send[step, 1] = flat_right
        start(FORCE, step)
        if step < STEPS - 1:
            def pack_star(k, strips):
                strips = put_v(step + 1, k, star_u[k], strips)
                return put_v(step + 1, LEVELS + k, star_v[k], strips)

            strips = lax.fori_loop(0, LEVELS, pack_star, (zero, zero), unroll=True)
            strips = put_flat(step + 1, 1, col_u, strips)
            strips = put_flat(step + 1, 2, col_v, strips)
            start(RIMS, step + 1)
        rim_laps(buoy_out, MOVING, LEVELS, BUOY_NEAR, BUOY_FAR)
        own_laps(buoy_out, MOVING, LEVELS)
        stage(buoy_in, MOVING, LEVELS, lp, lap_near)
        buoy_out[0:rows_b, 0:LANES] = apply(buoy_in, rows_b, LANES)
        lax.fori_loop(0, LEVELS, buoyancy, 0, unroll=True)
        if step < STEPS - 1:
            def pack_b(k, strips):
                cells = in_3d[2, k]
                fx[pl.ds(EXT * (MOVING + k) + OWN, ROWS)] = cells
                return put_b(step + 1, k, cells, strips)

            strips = lax.fori_loop(0, LEVELS, pack_b, strips, unroll=True)
            y_send[step + 1, 0] = strips[0]
            y_send[step + 1, 1] = strips[1]
            start(EARLY, step + 1)
        arrive(PLANE, step)
        sides = [gy_recv[step, r] for r in range(6)]

        def plane(own, a):
            rows = slice(ROWS * a, ROWS * (a + 1))
            return wide(own, gx_recv[step, 0, rows], gx_recv[step, 1, rows], sides, a)

        if step == 0:
            code_wide = plane(code, 3)
            wet, depth = (code_wide > 0.0).astype(F32), code_wide / LEVELS
        state = [plane(cells, a) for a, cells in enumerate(flats)]
        arrive(FORCE, step)
        sides_f = [fy_recv[step, r] for r in range(6)]
        push = [
            0.2 * wide(
                own, fx_recv[step, 0, ROWS * a : ROWS * (a + 1)],
                fx_recv[step, 1, ROWS * a : ROWS * (a + 1)], sides_f, a,
            )
            for a, own in enumerate((force_u, force_v))
        ]
        eta, flow_u, flow_v, sum_u, sum_v = barotropic(state, push, wet, depth)
        shift_u = (SCALE * inside(sum_u) - col_u) / lay
        shift_v = (SCALE * inside(sum_v) - col_v) / lay

        def couple(k, carry):
            act = lax.convert_element_type(k, F32) < code
            new_u = jnp.where(act, star_u[k] + shift_u, 0.0)
            new_v = jnp.where(act, star_v[k] + shift_v, 0.0)
            if step == STEPS - 1:
                out_u[k] = new_u
                out_v[k] = new_v
            else:
                fx[pl.ds(EXT * k + OWN, ROWS)] = new_u
                fx[pl.ds(EXT * (LEVELS + k) + OWN, ROWS)] = new_v
            return carry

        lax.fori_loop(0, LEVELS, couple, 0, unroll=True)

    out_eta[...] = inside(eta)
    out_tu[...] = inside(flow_u)
    out_tv[...] = inside(flow_v)
    for step in range(STEPS):
        for phase in (RIMS, FORCE, PLANE, EARLY):
            if phase != EARLY or step:
                sent(phase, step)


def per_device(velocity_u, velocity_v, buoyancy, surface, transport_u, transport_v, ocean, layers):
    cube = jax.ShapeDtypeStruct(velocity_u.shape, F32)
    flat = jax.ShapeDtypeStruct(surface.shape, F32)
    hbm = pl.BlockSpec(memory_space=pltpu.HBM)
    vmem = pl.BlockSpec(memory_space=pltpu.VMEM)
    outs = (cube, cube, cube, flat, flat, flat)
    args = [
        pltpu.with_memory_space_constraint(x, pltpu.HBM)
        for x in (velocity_u, velocity_v, buoyancy, surface, transport_u, transport_v, ocean, layers)
    ]
    block = (LEVELS, ROWS, LANES)
    middle = pl.pallas_call(
        kernel,
        out_shape=outs,
        in_specs=[hbm] * 8,
        out_specs=(vmem,) * 6,
        scratch_shapes=[
            pltpu.VMEM(block, F32),
            pltpu.VMEM(block, F32),
            pltpu.VMEM((STACK * EXT, LANES), F32),
            pltpu.VMEM((STACK * EXT, LANES), F32),
            pltpu.VMEM((ROWS + 8, LANES), F32),
            pltpu.VMEM((4, 8, LANES), F32),
            pltpu.VMEM((2, 2 * MOVING, LANES), F32),
            pltpu.VMEM((FIELDS,) + block, F32),
            pltpu.VMEM((3, ROWS, LANES), F32),
            pltpu.VMEM((2, ROWS, LANES), jnp.int32),
            pltpu.VMEM((4 * LANES, 2 * LANES), BF16),
            pltpu.VMEM((MOVING * (ROWS + 2), 4 * LANES), BF16),
            pltpu.VMEM((LEVELS * (ROWS + 2), 4 * LANES), BF16),
            pltpu.VMEM((MOVING * (ROWS + 2), LANES), F32),
            pltpu.VMEM((LEVELS * (ROWS + 2), 2 * LANES), F32),
            pltpu.VMEM((STEPS, 2, RIM, LANES), F32),
            pltpu.VMEM((STEPS, 2, ROWS, LANES), F32),
            pltpu.VMEM((STEPS, 2, RIM, LANES), F32),
            pltpu.VMEM((STEPS, 6, ROWS, LANES), F32),
            pltpu.VMEM((STEPS, 4 * ROWS, LANES), F32),
            pltpu.VMEM((STEPS, 2, 8, LANES), F32),
            pltpu.VMEM((STEPS, 2, 4 * ROWS, LANES), F32),
            pltpu.VMEM((STEPS, 6, 8, LANES), F32),
            pltpu.VMEM((STEPS, 2 * ROWS, LANES), F32),
            pltpu.VMEM((STEPS, 2, 8, LANES), F32),
            pltpu.VMEM((STEPS, 2, 2 * ROWS, LANES), F32),
            pltpu.VMEM((STEPS, 6, 8, LANES), F32),
            pltpu.SemaphoreType.DMA((8,)),
            pltpu.SemaphoreType.DMA((4 * STEPS, 8)),
            pltpu.SemaphoreType.DMA((4 * STEPS, 8)),
        ],
        compiler_params=pltpu.CompilerParams(
            collective_id=0, has_side_effects=True, vmem_limit_bytes=16 * 2**20
        ),
    )(*args)
    return tuple(
        pl.pallas_call(
            store_kernel,
            out_shape=outs,
            in_specs=[vmem] * 6,
            out_specs=(hbm,) * 6,
            scratch_shapes=[pltpu.SemaphoreType.DMA((6,))],
            compiler_params=pltpu.CompilerParams(vmem_limit_bytes=16 * 2**20),
        )(*middle)
    )


def solution(mesh):
    cube, flat = P(None, "gx", "gy"), P("gx", "gy")
    return jax.shard_map(
        per_device,
        mesh=mesh,
        in_specs=(cube, cube, cube, flat, flat, flat, flat, flat),
        out_specs=(cube, cube, cube, flat, flat, flat),
        check_vma=False,
    )
```

```python
import functools

import jax
import jax.numpy as jnp
from jax import lax
from jax.experimental import pallas as pl
from jax.experimental.pallas import tpu as pltpu
from jax.sharding import PartitionSpec as P

SUB = 8
STEPS = 2
LANES = 128
ROWS = 16
LEVELS = 16
FIELDS = 3
STACK = FIELDS * LEVELS
MESH = pl.DeviceIdType.MESH
F32 = jnp.float32
BF16 = jnp.bfloat16

DIRS = [(-1, 0), (1, 0), (0, -1), (0, 1), (-1, -1), (-1, 1), (1, -1), (1, 1)]
SIDES = [(-1, -1), (0, -1), (1, -1), (-1, 1), (0, 1), (1, 1)]
MOVING = 2 * LEVELS
FLAT_ROW = 2 * MOVING
BUOY_NEAR = FLAT_ROW + 8
BUOY_FAR = BUOY_NEAR + LEVELS
RIM = BUOY_FAR + LEVELS
HALF = LANES // 2


RIMS, FORCE, PLANE, EARLY = 0, 1, 2, 3
EXT = 32
OWN = 8
SCALE = LEVELS / SUB


def turn(x, shift, axis):
    return pltpu.roll(x, shift % x.shape[axis] if isinstance(shift, int) else shift, axis)


def fold(cells):
    low = lax.broadcasted_iota(jnp.int32, (8, LANES), 1) < HALF
    return jnp.where(low, cells[0:8], turn(cells[8:16], HALF, 1))


def unfold(cells):
    return jnp.concatenate([cells, turn(cells, HALF, 1)], axis=0)


def split(x):
    high = x.astype(BF16)
    return high, (x - high.astype(F32)).astype(BF16)


def pick(mask, x):
    return tuple(jnp.where(mask, part.astype(F32), 0.0).astype(BF16) for part in split(x))


def lane_weights():
    src = lax.broadcasted_iota(jnp.int32, (LANES, LANES), 0)
    dst = lax.broadcasted_iota(jnp.int32, (LANES, LANES), 1)
    ahead, behind = (src == dst + 1).astype(F32), (src == dst - 1).astype(F32)
    odd = (src & 1) == 1
    first = jnp.logical_and(odd, dst == 0).astype(F32)
    last = jnp.logical_and(jnp.logical_not(odd), dst == LANES - 1).astype(F32)
    return [
        [(ahead + behind).astype(BF16), (ahead - behind).astype(BF16)],
        [(last + first).astype(BF16), (last - first).astype(BF16)],
    ]


def pack_flat(arrays):
    lane = lax.broadcasted_iota(jnp.int32, (ROWS, LANES), 1)
    to_left = to_right = jnp.zeros((ROWS, LANES), F32)
    for a, cells in enumerate(arrays):
        to_right = jnp.where((lane >> 4) == a, turn(cells, 16 * a + 16, 1), to_right)
        to_left = jnp.where((lane >> 4) == a, turn(cells, 16 * a, 1), to_left)
    return fold(to_left), fold(to_right)


def wide(own, up, down, sides, a):
    lane = lax.broadcasted_iota(jnp.int32, (ROWS, LANES), 1)
    blocks = []
    for r in range(3):
        from_left, from_right = unfold(sides[r]), unfold(sides[r + 3])
        left, right = turn(from_left, 112 - 16 * a, 1), turn(from_right, -16 * a, 1)
        blocks.append(jnp.where(lane < 16, right, jnp.where(lane >= 112, left, 0.0)))
    main = jnp.concatenate([up, own, down], axis=0)
    return jnp.concatenate([main, jnp.concatenate(blocks, axis=0)], axis=1)


def substep(eta, tu, tv, wet, depth, push=None):
    div = (turn(tu, -1, 0) - turn(tu, 1, 0)) + (turn(tv, -1, 1) - turn(tv, 1, 1))
    eta = wet * (eta - 0.125 * div)
    thick = 0.125 * (depth + eta)
    new_u = 0.98 * tu - thick * (turn(eta, -1, 0) - turn(eta, 1, 0)) + 0.05 * tv
    new_v = 0.98 * tv - thick * (turn(eta, -1, 1) - turn(eta, 1, 1)) - 0.05 * tu
    if push is not None:
        new_u, new_v = new_u + push[0], new_v + push[1]
    return eta, wet * new_u, wet * new_v


def barotropic(state, push, wet, depth):
    eta, tu, tv = state
    tu, tv = tu + wet * push[0], tv + wet * push[1]

    def one(_, carry):
        eta, tu, tv, sum_u, sum_v = carry
        eta, tu, tv = substep(eta, tu, tv, wet, depth, push)
        return eta, tu, tv, sum_u + tu, sum_v + tv

    return lax.fori_loop(0, SUB - 1, one, (eta, tu, tv, tu, tv), unroll=True)


def inside(cells):
    return cells[ROWS : 2 * ROWS, 0:LANES]


def lane_pair(odd, cells, even_at, odd_at):
    shape = odd.shape
    return jnp.where(
        odd,
        jnp.broadcast_to(cells[:, odd_at : odd_at + 1], shape),
        jnp.broadcast_to(cells[:, even_at : even_at + 1], shape),
    )


def store_kernel(*refs):
    count = (len(refs) - 1) // 2
    sem = refs[-1]
    copies = [
        pltpu.make_async_copy(src, dst, sem.at[i])
        for i, (src, dst) in enumerate(zip(refs[:count], refs[count:-1]))
    ]
    for copy in copies:
        copy.start()
    for copy in copies:
        copy.wait()


def kernel(
    vel_u, vel_v, buoy, surface, trans_u, trans_v, ocean, layers,
    out_u, out_v, out_b, out_eta, out_tu, out_tv,
    star_u, star_v,
    fx, lp, near_ext, ring_rows, rim_new, in_3d, in_2d, in_int,
    lane_w, mom_in, buoy_in, mom_out, buoy_out,
    x_send, y_send, x_recv, y_recv, gx_send, gy_send, gx_recv, gy_recv,
    fx_send, fy_send, fx_recv, fy_recv, in_sem, send_sem, recv_sem,
):
    loads = []
    for a, ref in enumerate((vel_u, vel_v, buoy)):
        loads.append(pltpu.make_async_copy(ref, in_3d.at[a], in_sem.at[a]))
    for a, ref in enumerate((surface, trans_u, trans_v)):
        loads.append(pltpu.make_async_copy(ref, in_2d.at[a], in_sem.at[3 + a]))
    for a, ref in enumerate((ocean, layers)):
        loads.append(pltpu.make_async_copy(ref, in_int.at[a], in_sem.at[6 + a]))
    for load in loads:
        load.start()
    gx, gy = lax.axis_index("gx"), lax.axis_index("gy")
    nx, ny = lax.axis_size("gx"), lax.axis_size("gy")

    def exists(d):
        ok = jnp.bool_(True)
        if d[0] == -1:
            ok = jnp.logical_and(ok, gx > 0)
        if d[0] == 1:
            ok = jnp.logical_and(ok, gx < nx - 1)
        if d[1] == -1:
            ok = jnp.logical_and(ok, gy > 0)
        if d[1] == 1:
            ok = jnp.logical_and(ok, gy < ny - 1)
        return ok

    here = {d: exists(d) for d in DIRS}
    barrier = pltpu.get_barrier_semaphore()
    total_near = jnp.int32(0)
    for d in DIRS:
        total_near = total_near + here[d].astype(jnp.int32)

        @pl.when(here[d])
        def _(d=d):
            pl.semaphore_signal(barrier, inc=1, device_id=(gx + d[0], gy + d[1]), device_id_type=MESH)

    for d in DIRS:
        @pl.when(jnp.logical_not(here[d]))
        def _(d=d):
            for p in range(STEPS):
                if d[1] == 0:
                    s = 0 if d[0] < 0 else 1
                    x_recv[p, s] = jnp.zeros(x_recv.shape[2:], F32)
                    gx_recv[p, s] = jnp.zeros(gx_recv.shape[2:], F32)
                    fx_recv[p, s] = jnp.zeros(fx_recv.shape[2:], F32)
                else:
                    s = SIDES.index(d)
                    y_recv[p, s] = jnp.zeros(y_recv.shape[2:], F32)
                    gy_recv[p, s] = jnp.zeros(gy_recv.shape[2:], F32)
                    fy_recv[p, s] = jnp.zeros(fy_recv.shape[2:], F32)

    def copies(phase, step):
        result = []
        for i, d in enumerate(DIRS):
            back = (-d[0], -d[1])
            if d[1] == 0:
                src_at, dst_at = (0 if d[0] < 0 else 1), (0 if back[0] < 0 else 1)
                if phase == FORCE:
                    src, dst = fx_send.at[step], fx_recv.at[step, dst_at]
                elif phase == PLANE:
                    rows = pl.ds(0, (4 if step == 0 else 3) * ROWS)
                    src, dst = gx_send.at[step, rows], gx_recv.at[step, dst_at, rows]
                else:
                    if step == 0:
                        rows = pl.ds(0, RIM)
                    elif phase == EARLY:
                        rows = pl.ds(BUOY_NEAR, 2 * LEVELS)
                    else:
                        rows = pl.ds(0, BUOY_NEAR)
                    src, dst = x_send.at[step, src_at, rows], x_recv.at[step, dst_at, rows]
            else:
                src_at, dst_at = (0 if d[1] < 0 else 1), SIDES.index(back)
                if phase == FORCE:
                    src, dst = fy_send.at[step, src_at], fy_recv.at[step, dst_at]
                elif phase == PLANE:
                    src, dst = gy_send.at[step, src_at], gy_recv.at[step, dst_at]
                elif step and phase == RIMS:
                    continue
                else:
                    src, dst = y_send.at[step, src_at], y_recv.at[step, dst_at]
                    if d[0] != 0:
                        rows = pl.ds(0, 8) if d[0] < 0 else pl.ds(8, 8)
                        src, dst = src.at[rows], dst.at[rows]
            at = phase * STEPS + step
            copy = functools.partial(
                pltpu.make_async_remote_copy, src_ref=src, dst_ref=dst,
                send_sem=send_sem.at[at, i], recv_sem=recv_sem.at[at, DIRS.index(back)],
                device_id=(gx + d[0], gy + d[1]), device_id_type=MESH,
            )
            result.append((d, copy))
        return result

    odd_row = lax.rem(gx, 2) == 1

    def start_rows(phase, step, two_hops):
        pending = [(d, copy) for d, copy in copies(phase, step) if d[0]]
        pending.sort(key=lambda item: (item[0][1] == 0) != two_hops)
        for d, copy in pending:
            @pl.when(jnp.logical_and(here[d], odd_row == (two_hops == (d[0] > 0))))
            def _(copy=copy):
                copy().start()

    def start_far(phase, step):
        start_rows(phase, step, True)
        for d, copy in copies(phase, step):
            if d[0] == 0:
                @pl.when(here[d])
                def _(copy=copy):
                    copy().start()

    def start_near(phase, step):
        start_rows(phase, step, False)

    def start(phase, step):
        start_far(phase, step)
        start_near(phase, step)

    def arrive(phase, step):
        by_dir = dict(copies(phase, step))
        for d in by_dir:
            @pl.when(here[d])
            def _(d=d):
                by_dir[(-d[0], -d[1])]().wait_recv()

    def sent(phase, step):
        for d, copy in copies(phase, step):
            @pl.when(here[d])
            def _(copy=copy):
                copy().wait_send()

    lane = lax.broadcasted_iota(jnp.int32, (ROWS, LANES), 1)
    pair = lane >> 1
    odd = (lane & 1) == 1
    zero = jnp.zeros((ROWS, LANES), F32)

    def put(step, j, near_at, far_at, cells, strips):
        x_send[step, 0, pl.ds(near_at, 1)] = cells[0:1]
        x_send[step, 0, pl.ds(far_at, 1)] = cells[1:2]
        x_send[step, 1, pl.ds(near_at, 1)] = cells[ROWS - 1 : ROWS]
        x_send[step, 1, pl.ds(far_at, 1)] = cells[ROWS - 2 : ROWS - 1]
        to_left, to_right = strips
        rolled = turn(cells, 2 * j + 2, 1)
        to_right = jnp.where(pair == j, rolled, to_right)
        to_left = jnp.where(pair == j + 1, rolled, to_left)
        return to_left, to_right

    def put_v(step, j, cells, strips):
        return put(step, j, j, MOVING + j, cells, strips)

    def put_b(step, k, cells, strips):
        j = MOVING + k
        return put(step, j, BUOY_NEAR + k, BUOY_FAR + k, cells, strips)

    def put_flat(step, a, cells, strips):
        return put(step, STACK + a, FLAT_ROW + 2 * a, FLAT_ROW + 2 * a + 1, cells, strips)

    def send_plane(step, flats):
        flat_left, flat_right = pack_flat(flats)
        gy_send[step, 0] = flat_left
        gy_send[step, 1] = flat_right
        for a, cells in enumerate(flats):
            gx_send[step, ROWS * a : ROWS * (a + 1)] = cells
        start(PLANE, step)

    ring_rows[...] = jnp.zeros(ring_rows.shape, F32)
    for r, blocks in enumerate(lane_weights()):
        for c, block in enumerate(blocks):
            for at in (2 * r, 2 * r + 1):
                lane_w[LANES * at : LANES * (at + 1), LANES * c : LANES * (c + 1)] = block
    def put_parts(ref, at, rows, parts, col):
        for c, part in enumerate(parts):
            ref[pl.ds(at, rows), LANES * (col + c) : LANES * (col + c + 1)] = part

    def stage_own(ref, first, count, source):
        def one(i, carry):
            at = pl.multiple_of(ROWS * i, ROWS)
            put_parts(ref, at, ROWS, split(source[pl.ds(EXT * (first + i) + OWN, ROWS)]), 0)
            return carry

        lax.fori_loop(0, count, one, 0, unroll=True)

    def stage_edge(ref, first, count, edge):
        def one(i, carry):
            at = pl.multiple_of(ROWS * i, ROWS)
            put_parts(ref, at, ROWS, pick(pair == first + i, edge), 2)
            return carry

        lax.fori_loop(0, count, one, 0, unroll=True)

    loads[6].wait()
    loads[7].wait()
    lay = in_int[1].astype(F32)
    code = jnp.where(in_int[0] > 0, lay, 0.0)
    strips = put_flat(0, 0, code, (zero, zero))
    for a in range(FIELDS):
        loads[a].wait()

        def pack(k, strips, a=a):
            cells = in_3d[a, k]
            fx[pl.ds(EXT * (a * LEVELS + k) + OWN, ROWS)] = cells
            if a < 2:
                return put_v(0, a * LEVELS + k, cells, strips)
            return put_b(0, k, cells, strips)

        strips = lax.fori_loop(0, LEVELS, pack, strips, unroll=True)
    flats = [code]
    for a in range(3):
        loads[3 + a].wait()
        flats.append(in_2d[a])
        strips = put_flat(0, 1 + a, in_2d[a], strips)
    y_send[0, 0] = strips[0]
    y_send[0, 1] = strips[1]
    pl.semaphore_wait(barrier, total_near)
    start_far(RIMS, 0)
    stage_own(mom_in, 0, MOVING, fx)
    start_near(RIMS, 0)
    stage_own(buoy_in, MOVING, LEVELS, fx)

    around = (ROWS + 8, LANES)
    lane24 = lax.broadcasted_iota(jnp.int32, around, 1)
    odd24 = (lane24 & 1) == 1
    level24 = ((lane24 >> 1) & (LEVELS - 1)).astype(F32)
    level_pair = level24[0:ROWS]
    moving24 = lane24 < 2 * MOVING
    is_u24 = lane24 < 2 * LEVELS
    upper = lax.broadcasted_iota(jnp.int32, (8, LANES), 0) < 4

    def cyclic(own, below, above):
        return jnp.concatenate([own, jnp.where(upper, below, above)], axis=0)

    def beside_columns(left24, right24, j):
        return jnp.where(
            lane24 < HALF, turn(right24, -2 * j - 2, 1), turn(left24, 126 - 2 * j, 1)
        )

    def side24(cells):
        tile = cells[:, LANES : 2 * LANES]
        return cyclic(tile[ROWS : 2 * ROWS], tile[2 * ROWS : 2 * ROWS + 8], tile[8:ROWS])

    for step in range(STEPS):
        if step == 0:
            arrive(RIMS, step)
        else:
            arrive(RIMS, step)
            arrive(EARLY, step)
        left24 = cyclic(y_recv[step, 1], y_recv[step, 2, 0:8], y_recv[step, 0, 8:16])
        right24 = cyclic(y_recv[step, 4], y_recv[step, 5, 0:8], y_recv[step, 3, 8:16])
        near24 = jnp.where(odd24, left24, turn(right24, -2, 1))
        far = jnp.where(odd, turn(left24[0:ROWS], 1, 1), turn(right24[0:ROWS], -3, 1))
        inner = turn(jnp.where(odd, strips[1], strips[0]), -1, 1)

        if step == 0:
            code_near = lane_pair(odd24, near24, 2 * STACK, 2 * STACK + 1)
            code_far = lane_pair(odd, far, 2 * STACK, 2 * STACK + 1)
            code_inner = lane_pair(odd, code, LANES - 1, 0)
            act_near = level24 < code_near
        else:
            shift_side = [
                (SCALE * side24(total) - beside_columns(left24, right24, STACK + 1 + a))
                / jnp.maximum(code_side, 1.0)
                for a, total in enumerate((sum_u, sum_v))
            ]

            def couple_pairs(cells, near_code, rows, levels, even_at, odd_at, sources):
                parity = odd24[0:rows]
                shift = jnp.where(
                    is_u24[0:rows],
                    lane_pair(parity, sources[0][0:rows], even_at, odd_at),
                    lane_pair(parity, sources[1][0:rows], even_at, odd_at),
                )
                moved = jnp.where(levels < near_code, cells + shift, 0.0)
                return jnp.where(moving24[0:rows], moved, cells)

            near24 = couple_pairs(
                near24, code_near, ROWS + 8, level24, 0, LANES - 1, shift_side
            )
            far = couple_pairs(far, code_far, ROWS, level_pair, 1, LANES - 2, shift_side)
            inner = couple_pairs(
                inner, code_inner, ROWS, level_pair, LANES - 1, 0, (shift_u, shift_v)
            )
            level16 = lax.broadcasted_iota(jnp.int32, (LEVELS, LANES), 0).astype(F32)
            for side in range(2):
                for away in range(2):
                    at = (ROWS - 1 - away, 2 * ROWS + away)[side]
                    code_row = x_recv[0, side, pl.ds(FLAT_ROW + away, 1)]
                    for a, total in enumerate((sum_u, sum_v)):
                        column = x_recv[1, side, pl.ds(FLAT_ROW + 2 * (1 + a) + away, 1)]
                        shift = (
                            SCALE * total[at : at + 1, 0:LANES] - column
                        ) / jnp.maximum(code_row, 1.0)
                        rows = pl.ds(MOVING * away + LEVELS * a, LEVELS)
                        rim_new[side, rows] = jnp.where(
                            level16 < code_row, x_recv[1, side, rows] + shift, 0.0
                        )

        near_ext[...] = near24
        near = near24[0:ROWS]
        lap_near = jnp.where(
            act_near,
            turn(near24, 1, 0) + turn(near24, -1, 0) - 4.0 * near24,
            0.0,
        )[0:ROWS] + jnp.where(act_near[0:ROWS], far + inner, 0.0)

        def rim_cells(side, first, count, at):
            if first == 0 and step:
                return rim_new[side, pl.ds(at, count)]
            return x_recv[step, side, pl.ds(at, count)]

        def rim_rows(ref, first, count, near_at):
            row = lax.broadcasted_iota(jnp.int32, (count, LANES), 0)
            group = lax.broadcasted_iota(jnp.int32, (count, LANES), 1) >> 1
            for side in range(2):
                cells = rim_cells(side, first, count, near_at)
                at = ROWS * count + count * side
                corner = jnp.broadcast_to(
                    near_ext[pl.ds((ROWS + 7, ROWS)[side], 1)], (count, LANES)
                )
                put_parts(ref, at, count, split(cells), 0)
                put_parts(ref, at, count, pick(group == first + row, corner), 2)
                fx[pl.ds(EXT * first + (OWN - 1, OWN + ROWS)[side], count, stride=EXT)] = cells

        def rim_laps(ref, first, count, near_at, far_at):
            level_of = lax.broadcasted_iota(jnp.int32, (count, LANES), 0) & (LEVELS - 1)
            for side in range(2):
                cells = rim_cells(side, first, count, near_at)
                edge = EXT * first + (OWN, OWN + ROWS - 1)[side]
                beside = rim_cells(side, first, count, far_at) + fx[
                    pl.ds(edge, count, stride=EXT)
                ]
                lanes_sum = ref[pl.ds(ROWS * count + count * side, count), 0:LANES]
                code_row = x_recv[0, side, pl.ds(FLAT_ROW, 1)]
                lap = jnp.where(
                    level_of.astype(F32) < code_row, beside + lanes_sum - 4.0 * cells, 0.0
                )
                lp[pl.ds(EXT * first + (OWN - 1, OWN + ROWS)[side], count, stride=EXT)] = lap

        def laplace(j, source, lanes_sum):
            at = EXT * j + OWN
            return (
                source[pl.ds(at - 1, ROWS)] + source[pl.ds(at + 1, ROWS)]
                + lanes_sum - 4.0 * source[pl.ds(at, ROWS)]
            )

        def own_laps(ref, first, count):
            def one(i, carry):
                level_at = lax.convert_element_type(i & (LEVELS - 1), F32)
                lanes_sum = ref[pl.ds(pl.multiple_of(ROWS * i, ROWS), ROWS), 0:LANES]
                lap = laplace(first + i, fx, lanes_sum)
                lp[pl.ds(EXT * (first + i) + OWN, ROWS)] = jnp.where(level_at < code, lap, 0.0)
                return carry

            lax.fori_loop(0, count, one, 0, unroll=True)

        def apply(source, rows, width):
            return jnp.dot(
                source[0:rows], lane_w[:, 0:width], preferred_element_type=F32
            )

        rows_uv, rows_b = MOVING * ROWS, LEVELS * ROWS
        rim_rows(buoy_in, MOVING, LEVELS, BUOY_NEAR)
        stage_edge(buoy_in, MOVING, LEVELS, near)
        buoy_out[...] = apply(buoy_in, rows_b + 2 * LEVELS, 2 * LANES)
        if step == 0:
            grids = []
            for a, own in enumerate(flats):
                near_at, far_at = FLAT_ROW + 2 * a, FLAT_ROW + 2 * a + 1
                ring_rows[a, 0:1] = x_recv[0, 1, pl.ds(near_at, 1)]
                ring_rows[a, 1:2] = x_recv[0, 1, pl.ds(far_at, 1)]
                ring_rows[a, 6:7] = x_recv[0, 0, pl.ds(far_at, 1)]
                ring_rows[a, 7:8] = x_recv[0, 0, pl.ds(near_at, 1)]
                main = jnp.concatenate([own, ring_rows[a]], axis=0)
                grids.append(jnp.concatenate(
                    [main, beside_columns(left24, right24, STACK + a)], axis=1
                ))
            code_side = grids[0][:, LANES : 2 * LANES]
            ahead = substep(
                *grids[1:], (grids[0] > 0.0).astype(F32), grids[0] / LEVELS
            )
            flats = [cells[0:ROWS, 0:LANES] for cells in ahead]
            send_plane(step, flats + [code])
        else:
            flats = [inside(c) for c in substep(eta, flow_u, flow_v, wet, depth)]
            send_plane(step, flats)
        rim_rows(mom_in, 0, MOVING, 0)
        stage_edge(mom_in, 0, MOVING, near)
        mom_out[...] = apply(mom_in, rows_uv + 2 * MOVING, LANES)
        rim_laps(mom_out, 0, MOVING, 0, MOVING)
        own_laps(mom_out, 0, MOVING)
        stage_own(mom_in, 0, MOVING, lp)
        stage_edge(mom_in, 0, MOVING, lap_near)
        mom_out[0:rows_uv] = apply(mom_in, rows_uv, LANES)

        def buoyancy(k, carry):
            act = lax.convert_element_type(k, F32) < code
            at = EXT * (MOVING + k) + OWN
            rows = pl.ds(pl.multiple_of(ROWS * k, ROWS), ROWS)
            bih_b = laplace(MOVING + k, lp, buoy_out[rows, 0:LANES])
            u, v = fx[pl.ds(EXT * k + OWN, ROWS)], fx[pl.ds(EXT * (LEVELS + k) + OWN, ROWS)]
            b = fx[pl.ds(at, ROWS)]
            b_x = fx[pl.ds(at + 1, ROWS)] - fx[pl.ds(at - 1, ROWS)]
            b_y = buoy_out[rows, LANES : 2 * LANES]
            tend_b = -0.5 * (u * b_x + v * b_y) - 0.02 * bih_b
            new_b = jnp.where(act, b + 0.2 * tend_b, 0.0)
            if step == STEPS - 1:
                out_b[k] = new_b
            else:
                in_3d[2, k] = new_b
            return carry

        def level(k, carry):
            press_x, press_y, force_u, force_v, col_u, col_v = carry
            act = (lax.convert_element_type(k, F32) < code).astype(F32)
            rows = pl.ds(pl.multiple_of(ROWS * k, ROWS), ROWS)
            rows_v = pl.ds(pl.multiple_of(ROWS * (LEVELS + k), ROWS), ROWS)
            bih_u = laplace(k, lp, mom_out[rows])
            bih_v = laplace(LEVELS + k, lp, mom_out[rows_v])
            u, v = fx[pl.ds(EXT * k + OWN, ROWS)], fx[pl.ds(EXT * (LEVELS + k) + OWN, ROWS)]
            at = EXT * (MOVING + k) + OWN
            press_x = press_x + (fx[pl.ds(at + 1, ROWS)] - fx[pl.ds(at - 1, ROWS)])
            press_y = press_y + buoy_out[rows, LANES : 2 * LANES]
            tend_u = (-0.25 / LEVELS) * press_x + 0.1 * v - 0.02 * bih_u
            tend_v = (-0.25 / LEVELS) * press_y - 0.1 * u - 0.02 * bih_v
            su = act * (u + 0.2 * tend_u)
            sv = act * (v + 0.2 * tend_v)
            star_u[k] = su
            star_v[k] = sv
            return (
                press_x, press_y, force_u + act * tend_u, force_v + act * tend_v,
                col_u + su, col_v + sv,
            )

        _, _, force_u, force_v, col_u, col_v = lax.fori_loop(
            0, LEVELS, level, (zero,) * 6, unroll=True
        )
        force_u, force_v = force_u / LEVELS, force_v / LEVELS
        fx_send[step, 0:ROWS] = force_u
        fx_send[step, ROWS : 2 * ROWS] = force_v
        flat_left, flat_right = pack_flat((force_u, force_v))
        fy_send[step, 0] = flat_left
        fy_send[step, 1] = flat_right
        start(FORCE, step)
        if step < STEPS - 1:
            def pack_star(k, strips):
                strips = put_v(step + 1, k, star_u[k], strips)
                return put_v(step + 1, LEVELS + k, star_v[k], strips)

            strips = lax.fori_loop(0, LEVELS, pack_star, (zero, zero), unroll=True)
            strips = put_flat(step + 1, 1, col_u, strips)
            strips = put_flat(step + 1, 2, col_v, strips)
            start_far(RIMS, step + 1)
        rim_laps(buoy_out, MOVING, LEVELS, BUOY_NEAR, BUOY_FAR)
        own_laps(buoy_out, MOVING, LEVELS)
        stage_own(buoy_in, MOVING, LEVELS, lp)
        stage_edge(buoy_in, MOVING, LEVELS, lap_near)
        buoy_out[0:rows_b, 0:LANES] = apply(buoy_in, rows_b, LANES)
        lax.fori_loop(0, LEVELS, buoyancy, 0, unroll=True)
        if step < STEPS - 1:
            def pack_b(k, strips):
                cells = in_3d[2, k]
                fx[pl.ds(EXT * (MOVING + k) + OWN, ROWS)] = cells
                return put_b(step + 1, k, cells, strips)

            strips = lax.fori_loop(0, LEVELS, pack_b, strips, unroll=True)
            y_send[step + 1, 0] = strips[0]
            y_send[step + 1, 1] = strips[1]
            start_far(EARLY, step + 1)
            start_near(RIMS, step + 1)
            start_near(EARLY, step + 1)
            stage_own(buoy_in, MOVING, LEVELS, fx)
        arrive(PLANE, step)
        sides = [gy_recv[step, r] for r in range(6)]

        def plane(own, a):
            rows = slice(ROWS * a, ROWS * (a + 1))
            return wide(own, gx_recv[step, 0, rows], gx_recv[step, 1, rows], sides, a)

        if step == 0:
            code_wide = plane(code, 3)
            wet, depth = (code_wide > 0.0).astype(F32), code_wide / LEVELS
        state = [plane(cells, a) for a, cells in enumerate(flats)]
        arrive(FORCE, step)
        sides_f = [fy_recv[step, r] for r in range(6)]
        push = [
            0.2 * wide(
                own, fx_recv[step, 0, ROWS * a : ROWS * (a + 1)],
                fx_recv[step, 1, ROWS * a : ROWS * (a + 1)], sides_f, a,
            )
            for a, own in enumerate((force_u, force_v))
        ]
        eta, flow_u, flow_v, sum_u, sum_v = barotropic(state, push, wet, depth)
        shift_u = (SCALE * inside(sum_u) - col_u) / lay
        shift_v = (SCALE * inside(sum_v) - col_v) / lay

        def couple(k, carry):
            act = lax.convert_element_type(k, F32) < code
            new_u = jnp.where(act, star_u[k] + shift_u, 0.0)
            new_v = jnp.where(act, star_v[k] + shift_v, 0.0)
            if step == STEPS - 1:
                out_u[k] = new_u
                out_v[k] = new_v
            else:
                fx[pl.ds(EXT * k + OWN, ROWS)] = new_u
                fx[pl.ds(EXT * (LEVELS + k) + OWN, ROWS)] = new_v
            return carry

        lax.fori_loop(0, LEVELS, couple, 0, unroll=True)
        if step < STEPS - 1:
            stage_own(mom_in, 0, MOVING, fx)

    out_eta[...] = inside(eta)
    out_tu[...] = inside(flow_u)
    out_tv[...] = inside(flow_v)
    for step in range(STEPS):
        for phase in (RIMS, FORCE, PLANE, EARLY):
            if phase != EARLY or step:
                sent(phase, step)


def per_device(velocity_u, velocity_v, buoyancy, surface, transport_u, transport_v, ocean, layers):
    cube = jax.ShapeDtypeStruct(velocity_u.shape, F32)
    flat = jax.ShapeDtypeStruct(surface.shape, F32)
    hbm = pl.BlockSpec(memory_space=pltpu.HBM)
    vmem = pl.BlockSpec(memory_space=pltpu.VMEM)
    outs = (cube, cube, cube, flat, flat, flat)
    args = [
        pltpu.with_memory_space_constraint(x, pltpu.HBM)
        for x in (velocity_u, velocity_v, buoyancy, surface, transport_u, transport_v, ocean, layers)
    ]
    block = (LEVELS, ROWS, LANES)
    middle = pl.pallas_call(
        kernel,
        out_shape=outs,
        in_specs=[hbm] * 8,
        out_specs=(vmem,) * 6,
        scratch_shapes=[
            pltpu.VMEM(block, F32),
            pltpu.VMEM(block, F32),
            pltpu.VMEM((STACK * EXT, LANES), F32),
            pltpu.VMEM((STACK * EXT, LANES), F32),
            pltpu.VMEM((ROWS + 8, LANES), F32),
            pltpu.VMEM((4, 8, LANES), F32),
            pltpu.VMEM((2, 2 * MOVING, LANES), F32),
            pltpu.VMEM((FIELDS,) + block, F32),
            pltpu.VMEM((3, ROWS, LANES), F32),
            pltpu.VMEM((2, ROWS, LANES), jnp.int32),
            pltpu.VMEM((4 * LANES, 2 * LANES), BF16),
            pltpu.VMEM((MOVING * (ROWS + 2), 4 * LANES), BF16),
            pltpu.VMEM((LEVELS * (ROWS + 2), 4 * LANES), BF16),
            pltpu.VMEM((MOVING * (ROWS + 2), LANES), F32),
            pltpu.VMEM((LEVELS * (ROWS + 2), 2 * LANES), F32),
            pltpu.VMEM((STEPS, 2, RIM, LANES), F32),
            pltpu.VMEM((STEPS, 2, ROWS, LANES), F32),
            pltpu.VMEM((STEPS, 2, RIM, LANES), F32),
            pltpu.VMEM((STEPS, 6, ROWS, LANES), F32),
            pltpu.VMEM((STEPS, 4 * ROWS, LANES), F32),
            pltpu.VMEM((STEPS, 2, 8, LANES), F32),
            pltpu.VMEM((STEPS, 2, 4 * ROWS, LANES), F32),
            pltpu.VMEM((STEPS, 6, 8, LANES), F32),
            pltpu.VMEM((STEPS, 2 * ROWS, LANES), F32),
            pltpu.VMEM((STEPS, 2, 8, LANES), F32),
            pltpu.VMEM((STEPS, 2, 2 * ROWS, LANES), F32),
            pltpu.VMEM((STEPS, 6, 8, LANES), F32),
            pltpu.SemaphoreType.DMA((8,)),
            pltpu.SemaphoreType.DMA((4 * STEPS, 8)),
            pltpu.SemaphoreType.DMA((4 * STEPS, 8)),
        ],
        compiler_params=pltpu.CompilerParams(
            collective_id=0, has_side_effects=True, vmem_limit_bytes=16 * 2**20
        ),
    )(*args)
    return tuple(
        pl.pallas_call(
            store_kernel,
            out_shape=outs,
            in_specs=[vmem] * 6,
            out_specs=(hbm,) * 6,
            scratch_shapes=[pltpu.SemaphoreType.DMA((6,))],
            compiler_params=pltpu.CompilerParams(vmem_limit_bytes=16 * 2**20),
        )(*middle)
    )


def solution(mesh):
    cube, flat = P(None, "gx", "gy"), P("gx", "gy")
    return jax.shard_map(
        per_device,
        mesh=mesh,
        in_specs=(cube, cube, cube, flat, flat, flat, flat, flat),
        out_specs=(cube, cube, cube, flat, flat, flat),
        check_vma=False,
    )
```

```python
import functools

import jax
import jax.numpy as jnp
from jax import lax
from jax.experimental import pallas as pl
from jax.experimental.pallas import tpu as pltpu
from jax.sharding import PartitionSpec as P

SUB = 8
STEPS = 2
LANES = 128
ROWS = 16
LEVELS = 16
FIELDS = 3
STACK = FIELDS * LEVELS
MESH = pl.DeviceIdType.MESH
F32 = jnp.float32
BF16 = jnp.bfloat16

DIRS = [(-1, 0), (1, 0), (0, -1), (0, 1), (-1, -1), (-1, 1), (1, -1), (1, 1)]
SIDES = [(-1, -1), (0, -1), (1, -1), (-1, 1), (0, 1), (1, 1)]
MOVING = 2 * LEVELS
FLAT_ROW = 2 * MOVING
BUOY_NEAR = FLAT_ROW + 8
BUOY_FAR = BUOY_NEAR + LEVELS
CODE_PLANE = BUOY_FAR + LEVELS
RIM = CODE_PLANE + ROWS
HALF = LANES // 2


RIMS, FORCE, PLANE, EARLY = 0, 1, 2, 3
EXT = 32
OWN = 8
SCALE = LEVELS / SUB


def turn(x, shift, axis):
    return pltpu.roll(x, shift % x.shape[axis] if isinstance(shift, int) else shift, axis)


def fold(cells):
    low = lax.broadcasted_iota(jnp.int32, (8, LANES), 1) < HALF
    return jnp.where(low, cells[0:8], turn(cells[8:16], HALF, 1))


def unfold(cells):
    return jnp.concatenate([cells, turn(cells, HALF, 1)], axis=0)


def split(x):
    high = x.astype(BF16)
    return high, (x - high.astype(F32)).astype(BF16)


def pick(mask, x):
    return tuple(jnp.where(mask, part.astype(F32), 0.0).astype(BF16) for part in split(x))


def lane_weights():
    src = lax.broadcasted_iota(jnp.int32, (LANES, LANES), 0)
    dst = lax.broadcasted_iota(jnp.int32, (LANES, LANES), 1)
    ahead, behind = (src == dst + 1).astype(F32), (src == dst - 1).astype(F32)
    odd = (src & 1) == 1
    first = jnp.logical_and(odd, dst == 0).astype(F32)
    last = jnp.logical_and(jnp.logical_not(odd), dst == LANES - 1).astype(F32)
    return [
        [(ahead + behind).astype(BF16), (ahead - behind).astype(BF16)],
        [(last + first).astype(BF16), (last - first).astype(BF16)],
    ]


def pack_flat(arrays):
    lane = lax.broadcasted_iota(jnp.int32, (ROWS, LANES), 1)
    to_left = to_right = jnp.zeros((ROWS, LANES), F32)
    for a, cells in enumerate(arrays):
        to_right = jnp.where((lane >> 4) == a, turn(cells, 16 * a + 16, 1), to_right)
        to_left = jnp.where((lane >> 4) == a, turn(cells, 16 * a, 1), to_left)
    return fold(to_left), fold(to_right)


def wide(own, up, down, sides, a):
    lane = lax.broadcasted_iota(jnp.int32, (ROWS, LANES), 1)
    blocks = []
    for r in range(3):
        from_left, from_right = unfold(sides[r]), unfold(sides[r + 3])
        left, right = turn(from_left, 112 - 16 * a, 1), turn(from_right, -16 * a, 1)
        blocks.append(jnp.where(lane < 16, right, jnp.where(lane >= 112, left, 0.0)))
    main = jnp.concatenate([up, own, down], axis=0)
    return jnp.concatenate([main, jnp.concatenate(blocks, axis=0)], axis=1)


def substep(eta, tu, tv, wet, depth, push=None):
    div = (turn(tu, -1, 0) - turn(tu, 1, 0)) + (turn(tv, -1, 1) - turn(tv, 1, 1))
    eta = wet * (eta - 0.125 * div)
    thick = 0.125 * (depth + eta)
    new_u = 0.98 * tu - thick * (turn(eta, -1, 0) - turn(eta, 1, 0)) + 0.05 * tv
    new_v = 0.98 * tv - thick * (turn(eta, -1, 1) - turn(eta, 1, 1)) - 0.05 * tu
    if push is not None:
        new_u, new_v = new_u + push[0], new_v + push[1]
    return eta, wet * new_u, wet * new_v


def barotropic(state, push, wet, depth):
    eta, tu, tv = state
    tu, tv = tu + wet * push[0], tv + wet * push[1]

    def one(_, carry):
        eta, tu, tv, sum_u, sum_v = carry
        eta, tu, tv = substep(eta, tu, tv, wet, depth, push)
        return eta, tu, tv, sum_u + tu, sum_v + tv

    return lax.fori_loop(0, SUB - 1, one, (eta, tu, tv, tu, tv), unroll=True)


def inside(cells):
    return cells[ROWS : 2 * ROWS, 0:LANES]


def lane_pair(odd, cells, even_at, odd_at):
    shape = odd.shape
    return jnp.where(
        odd,
        jnp.broadcast_to(cells[:, odd_at : odd_at + 1], shape),
        jnp.broadcast_to(cells[:, even_at : even_at + 1], shape),
    )


def store_kernel(*refs):
    count = (len(refs) - 1) // 2
    sem = refs[-1]
    copies = [
        pltpu.make_async_copy(src, dst, sem.at[i])
        for i, (src, dst) in enumerate(zip(refs[:count], refs[count:-1]))
    ]
    for copy in copies:
        copy.start()
    for copy in copies:
        copy.wait()


def kernel(
    vel_u, vel_v, buoy, surface, trans_u, trans_v, ocean, layers,
    out_u, out_v, out_b, out_eta, out_tu, out_tv,
    star_u, star_v,
    fx, lp, near_ext, ring_rows, rim_new, in_3d, in_2d, in_int,
    lane_w, mom_in, buoy_in, mom_out, buoy_out,
    x_send, y_send, x_recv, y_recv, gx_send, gy_send, gx_recv, gy_recv,
    fx_send, fy_send, fx_recv, fy_recv, in_sem, send_sem, recv_sem,
):
    loads = []
    for a, ref in enumerate((vel_u, vel_v, buoy)):
        loads.append(pltpu.make_async_copy(ref, in_3d.at[a], in_sem.at[a]))
    for a, ref in enumerate((surface, trans_u, trans_v)):
        loads.append(pltpu.make_async_copy(ref, in_2d.at[a], in_sem.at[3 + a]))
    for a, ref in enumerate((ocean, layers)):
        loads.append(pltpu.make_async_copy(ref, in_int.at[a], in_sem.at[6 + a]))
    for load in loads:
        load.start()
    gx, gy = lax.axis_index("gx"), lax.axis_index("gy")
    nx, ny = lax.axis_size("gx"), lax.axis_size("gy")

    def exists(d):
        ok = jnp.bool_(True)
        if d[0] == -1:
            ok = jnp.logical_and(ok, gx > 0)
        if d[0] == 1:
            ok = jnp.logical_and(ok, gx < nx - 1)
        if d[1] == -1:
            ok = jnp.logical_and(ok, gy > 0)
        if d[1] == 1:
            ok = jnp.logical_and(ok, gy < ny - 1)
        return ok

    here = {d: exists(d) for d in DIRS}
    barrier = pltpu.get_barrier_semaphore()
    total_near = jnp.int32(0)
    for d in DIRS:
        total_near = total_near + here[d].astype(jnp.int32)

        @pl.when(here[d])
        def _(d=d):
            pl.semaphore_signal(barrier, inc=1, device_id=(gx + d[0], gy + d[1]), device_id_type=MESH)

    for d in DIRS:
        @pl.when(jnp.logical_not(here[d]))
        def _(d=d):
            for p in range(STEPS):
                if d[1] == 0:
                    s = 0 if d[0] < 0 else 1
                    x_recv[p, s] = jnp.zeros(x_recv.shape[2:], F32)
                    gx_recv[p, s] = jnp.zeros(gx_recv.shape[2:], F32)
                    fx_recv[p, s] = jnp.zeros(fx_recv.shape[2:], F32)
                else:
                    s = SIDES.index(d)
                    y_recv[p, s] = jnp.zeros(y_recv.shape[2:], F32)
                    gy_recv[p, s] = jnp.zeros(gy_recv.shape[2:], F32)
                    fy_recv[p, s] = jnp.zeros(fy_recv.shape[2:], F32)

    def copies(phase, step):
        result = []
        for i, d in enumerate(DIRS):
            back = (-d[0], -d[1])
            if d[1] == 0:
                src_at, dst_at = (0 if d[0] < 0 else 1), (0 if back[0] < 0 else 1)
                if phase == FORCE:
                    src, dst = fx_send.at[step], fx_recv.at[step, dst_at]
                elif phase == PLANE:
                    src, dst = gx_send.at[step], gx_recv.at[step, dst_at]
                else:
                    if step == 0:
                        rows = pl.ds(0, BUOY_FAR) if phase == RIMS else pl.ds(BUOY_FAR, RIM - BUOY_FAR)
                    elif phase == EARLY:
                        rows = pl.ds(BUOY_NEAR, 2 * LEVELS)
                    else:
                        rows = pl.ds(0, BUOY_NEAR)
                    src, dst = x_send.at[step, src_at, rows], x_recv.at[step, dst_at, rows]
            else:
                src_at, dst_at = (0 if d[1] < 0 else 1), SIDES.index(back)
                if phase == FORCE:
                    src, dst = fy_send.at[step], fy_recv.at[step, dst_at]
                elif phase == PLANE:
                    src, dst = gy_send.at[step, src_at], gy_recv.at[step, dst_at]
                elif phase == (RIMS if step else EARLY):
                    continue
                else:
                    src, dst = y_send.at[step, src_at], y_recv.at[step, dst_at]
                    if d[0] != 0:
                        rows = pl.ds(0, 8) if d[0] < 0 else pl.ds(8, 8)
                        src, dst = src.at[rows], dst.at[rows]
            at = phase * STEPS + step
            copy = functools.partial(
                pltpu.make_async_remote_copy, src_ref=src, dst_ref=dst,
                send_sem=send_sem.at[at, i], recv_sem=recv_sem.at[at, DIRS.index(back)],
                device_id=(gx + d[0], gy + d[1]), device_id_type=MESH,
            )
            result.append((d, copy))
        return result

    odd_row = lax.rem(gx, 2) == 1

    def start_rows(phase, step, two_hops):
        pending = [(d, copy) for d, copy in copies(phase, step) if d[0]]
        pending.sort(key=lambda item: (item[0][1] == 0) != two_hops)
        for d, copy in pending:
            @pl.when(jnp.logical_and(here[d], odd_row == (two_hops == (d[0] > 0))))
            def _(copy=copy):
                copy().start()

    def start_far(phase, step):
        start_rows(phase, step, True)
        for d, copy in copies(phase, step):
            if d[0] == 0:
                @pl.when(here[d])
                def _(copy=copy):
                    copy().start()

    def start_near(phase, step):
        start_rows(phase, step, False)

    def start(phase, step):
        start_far(phase, step)
        start_near(phase, step)

    def arrive(phase, step):
        by_dir = dict(copies(phase, step))
        for d in by_dir:
            @pl.when(here[d])
            def _(d=d):
                by_dir[(-d[0], -d[1])]().wait_recv()

    def sent(phase, step):
        for d, copy in copies(phase, step):
            @pl.when(here[d])
            def _(copy=copy):
                copy().wait_send()

    lane = lax.broadcasted_iota(jnp.int32, (ROWS, LANES), 1)
    pair = lane >> 1
    lane8 = lane[0:8]
    odd = (lane & 1) == 1
    rim_lanes = jnp.logical_or(lane < 16, lane >= LANES - 16)
    zero = jnp.zeros((ROWS, LANES), F32)

    def put(step, j, near_at, far_at, cells, strips):
        x_send[step, 0, pl.ds(near_at, 1)] = cells[0:1]
        x_send[step, 0, pl.ds(far_at, 1)] = cells[1:2]
        x_send[step, 1, pl.ds(near_at, 1)] = cells[ROWS - 1 : ROWS]
        x_send[step, 1, pl.ds(far_at, 1)] = cells[ROWS - 2 : ROWS - 1]
        to_left, to_right = strips
        rolled = turn(cells, 2 * j + 2, 1)
        to_right = jnp.where(pair == j, rolled, to_right)
        to_left = jnp.where(pair == j + 1, rolled, to_left)
        return to_left, to_right

    def put_v(step, j, cells, strips):
        return put(step, j, j, MOVING + j, cells, strips)

    def put_b(step, k, cells, strips):
        j = MOVING + k
        return put(step, j, BUOY_NEAR + k, BUOY_FAR + k, cells, strips)

    def put_flat(step, a, cells, strips):
        return put(step, STACK + a, FLAT_ROW + 2 * a, FLAT_ROW + 2 * a + 1, cells, strips)

    def send_plane(step, flats):
        flat_left, flat_right = pack_flat(flats)
        gy_send[step, 0] = flat_left
        gy_send[step, 1] = flat_right
        for a, cells in enumerate(flats[0:3]):
            gx_send[step, ROWS * a : ROWS * (a + 1)] = cells
        start(PLANE, step)

    ring_rows[...] = jnp.zeros(ring_rows.shape, F32)
    for r, blocks in enumerate(lane_weights()):
        for c, block in enumerate(blocks):
            for at in (2 * r, 2 * r + 1):
                lane_w[LANES * at : LANES * (at + 1), LANES * c : LANES * (c + 1)] = block
    def put_parts(ref, at, rows, parts, col):
        for c, part in enumerate(parts):
            ref[pl.ds(at, rows), LANES * (col + c) : LANES * (col + c + 1)] = part

    def stage_own(ref, first, count, source):
        def one(i, carry):
            at = pl.multiple_of(ROWS * i, ROWS)
            put_parts(ref, at, ROWS, split(source[pl.ds(EXT * (first + i) + OWN, ROWS)]), 0)
            return carry

        lax.fori_loop(0, count, one, 0, unroll=True)

    def stage_edge(ref, first, count, edge):
        def one(i, carry):
            at = pl.multiple_of(ROWS * i, ROWS)
            put_parts(ref, at, ROWS, pick(pair == first + i, edge), 2)
            return carry

        lax.fori_loop(0, count, one, 0, unroll=True)

    loads[6].wait()
    loads[7].wait()
    lay = in_int[1].astype(F32)
    code = jnp.where(in_int[0] > 0, lay, 0.0)
    strips = put_flat(0, 0, code, (zero, zero))
    for a in range(FIELDS):
        loads[a].wait()

        def pack(k, strips, a=a):
            cells = in_3d[a, k]
            fx[pl.ds(EXT * (a * LEVELS + k) + OWN, ROWS)] = cells
            if a < 2:
                return put_v(0, a * LEVELS + k, cells, strips)
            return put_b(0, k, cells, strips)

        strips = lax.fori_loop(0, LEVELS, pack, strips, unroll=True)
    flats = [code]
    for a in range(3):
        loads[3 + a].wait()
        flats.append(in_2d[a])
        strips = put_flat(0, 1 + a, in_2d[a], strips)
    strips = turn(strips[0], -2, 1), strips[1]
    y_send[0, 0] = strips[0]
    y_send[0, 1] = strips[1]
    pl.semaphore_wait(barrier, total_near)
    for side in range(2):
        x_send[0, side, pl.ds(CODE_PLANE, ROWS)] = code
    start_far(RIMS, 0)
    stage_own(mom_in, 0, MOVING, fx)
    start_near(RIMS, 0)
    start(EARLY, 0)
    stage_own(buoy_in, MOVING, LEVELS, fx)

    around = (ROWS + 8, LANES)
    lane24 = lax.broadcasted_iota(jnp.int32, around, 1)
    odd24 = (lane24 & 1) == 1
    level24 = ((lane24 >> 1) & (LEVELS - 1)).astype(F32)
    level_pair = level24[0:ROWS]
    moving24 = lane24 < 2 * MOVING
    is_u24 = lane24 < 2 * LEVELS
    upper = lax.broadcasted_iota(jnp.int32, (8, LANES), 0) < 4

    def cyclic(own, below, above):
        return jnp.concatenate([own, jnp.where(upper, below, above)], axis=0)

    def beside_columns(left24, right24, j):
        return jnp.where(
            lane24 < HALF, turn(right24, -2 * j, 1), turn(left24, 126 - 2 * j, 1)
        )

    def side24(cells):
        tile = cells[:, LANES : 2 * LANES]
        return cyclic(tile[ROWS : 2 * ROWS], tile[2 * ROWS : 2 * ROWS + 8], tile[8:ROWS])

    for step in range(STEPS):
        if step == 0:
            arrive(RIMS, step)
        else:
            arrive(RIMS, step)
            arrive(EARLY, step)
        left24 = cyclic(y_recv[step, 1], y_recv[step, 2, 0:8], y_recv[step, 0, 8:16])
        right24 = cyclic(y_recv[step, 4], y_recv[step, 5, 0:8], y_recv[step, 3, 8:16])
        near24 = jnp.where(odd24, left24, right24)
        far = jnp.where(odd, right24[0:ROWS], left24[0:ROWS])
        far = jnp.where(odd, turn(far, 1, 1), turn(far, -1, 1))
        inner = jnp.where(odd, turn(strips[0], 1, 1), turn(strips[1], -1, 1))

        if step == 0:
            code_near = lane_pair(odd24, near24, 2 * STACK, 2 * STACK + 1)
            code_far = lane_pair(odd, far, 2 * STACK, 2 * STACK + 1)
            code_inner = lane_pair(odd, code, LANES - 1, 0)
            act_near = level24 < code_near
        else:
            shift_side = [
                (SCALE * side24(total) - beside_columns(left24, right24, STACK + 1 + a))
                / jnp.maximum(code_side, 1.0)
                for a, total in enumerate((sum_u, sum_v))
            ]

            def couple_pairs(cells, near_code, rows, levels, even_at, odd_at, sources):
                parity = odd24[0:rows]
                shift = jnp.where(
                    is_u24[0:rows],
                    lane_pair(parity, sources[0][0:rows], even_at, odd_at),
                    lane_pair(parity, sources[1][0:rows], even_at, odd_at),
                )
                moved = jnp.where(levels < near_code, cells + shift, 0.0)
                return jnp.where(moving24[0:rows], moved, cells)

            near24 = couple_pairs(
                near24, code_near, ROWS + 8, level24, 0, LANES - 1, shift_side
            )
            far = couple_pairs(far, code_far, ROWS, level_pair, 1, LANES - 2, shift_side)
            inner = couple_pairs(
                inner, code_inner, ROWS, level_pair, LANES - 1, 0, (shift_u, shift_v)
            )
            level16 = lax.broadcasted_iota(jnp.int32, (LEVELS, LANES), 0).astype(F32)
            for side in range(2):
                for away in range(2):
                    at = (ROWS - 1 - away, 2 * ROWS + away)[side]
                    code_row = x_recv[0, side, pl.ds(FLAT_ROW + away, 1)]
                    for a, total in enumerate((sum_u, sum_v)):
                        column = x_recv[1, side, pl.ds(FLAT_ROW + 2 * (1 + a) + away, 1)]
                        shift = (
                            SCALE * total[at : at + 1, 0:LANES] - column
                        ) / jnp.maximum(code_row, 1.0)
                        rows = pl.ds(MOVING * away + LEVELS * a, LEVELS)
                        rim_new[side, rows] = jnp.where(
                            level16 < code_row, x_recv[1, side, rows] + shift, 0.0
                        )

        near_ext[...] = near24
        near = near24[0:ROWS]
        lap_near = jnp.where(
            act_near,
            turn(near24, 1, 0) + turn(near24, -1, 0) - 4.0 * near24,
            0.0,
        )[0:ROWS] + jnp.where(act_near[0:ROWS], far + inner, 0.0)

        def rim_cells(side, first, count, at):
            if first == 0 and step:
                return rim_new[side, pl.ds(at, count)]
            return x_recv[step, side, pl.ds(at, count)]

        def rim_rows(ref, first, count, near_at):
            row = lax.broadcasted_iota(jnp.int32, (count, LANES), 0)
            group = lax.broadcasted_iota(jnp.int32, (count, LANES), 1) >> 1
            for side in range(2):
                cells = rim_cells(side, first, count, near_at)
                at = ROWS * count + count * side
                corner = jnp.broadcast_to(
                    near_ext[pl.ds((ROWS + 7, ROWS)[side], 1)], (count, LANES)
                )
                put_parts(ref, at, count, split(cells), 0)
                put_parts(ref, at, count, pick(group == first + row, corner), 2)
                fx[pl.ds(EXT * first + (OWN - 1, OWN + ROWS)[side], count, stride=EXT)] = cells

        def rim_laps(ref, first, count, near_at, far_at):
            level_of = lax.broadcasted_iota(jnp.int32, (count, LANES), 0) & (LEVELS - 1)
            for side in range(2):
                cells = rim_cells(side, first, count, near_at)
                edge = EXT * first + (OWN, OWN + ROWS - 1)[side]
                beside = rim_cells(side, first, count, far_at) + fx[
                    pl.ds(edge, count, stride=EXT)
                ]
                lanes_sum = ref[pl.ds(ROWS * count + count * side, count), 0:LANES]
                code_row = x_recv[0, side, pl.ds(FLAT_ROW, 1)]
                lap = jnp.where(
                    level_of.astype(F32) < code_row, beside + lanes_sum - 4.0 * cells, 0.0
                )
                lp[pl.ds(EXT * first + (OWN - 1, OWN + ROWS)[side], count, stride=EXT)] = lap

        def laplace(j, source, lanes_sum):
            at = EXT * j + OWN
            return (
                source[pl.ds(at - 1, ROWS)] + source[pl.ds(at + 1, ROWS)]
                + lanes_sum - 4.0 * source[pl.ds(at, ROWS)]
            )

        def own_laps(ref, first, count):
            def one(i, carry):
                level_at = lax.convert_element_type(i & (LEVELS - 1), F32)
                lanes_sum = ref[pl.ds(pl.multiple_of(ROWS * i, ROWS), ROWS), 0:LANES]
                lap = laplace(first + i, fx, lanes_sum)
                lp[pl.ds(EXT * (first + i) + OWN, ROWS)] = jnp.where(level_at < code, lap, 0.0)
                return carry

            lax.fori_loop(0, count, one, 0, unroll=True)

        def apply(source, rows, width):
            return jnp.dot(
                source[0:rows], lane_w[:, 0:width], preferred_element_type=F32
            )

        rows_uv, rows_b = MOVING * ROWS, LEVELS * ROWS
        rim_rows(buoy_in, MOVING, LEVELS, BUOY_NEAR)
        stage_edge(buoy_in, MOVING, LEVELS, near)
        buoy_out[...] = apply(buoy_in, rows_b + 2 * LEVELS, 2 * LANES)
        if step == 0:
            grids = []
            for a, own in enumerate(flats):
                near_at, far_at = FLAT_ROW + 2 * a, FLAT_ROW + 2 * a + 1
                ring_rows[a, 0:1] = x_recv[0, 1, pl.ds(near_at, 1)]
                ring_rows[a, 1:2] = x_recv[0, 1, pl.ds(far_at, 1)]
                ring_rows[a, 6:7] = x_recv[0, 0, pl.ds(far_at, 1)]
                ring_rows[a, 7:8] = x_recv[0, 0, pl.ds(near_at, 1)]
                main = jnp.concatenate([own, ring_rows[a]], axis=0)
                grids.append(jnp.concatenate(
                    [main, beside_columns(left24, right24, STACK + a)], axis=1
                ))
            code_side = grids[0][:, LANES : 2 * LANES]
            ahead = substep(
                *grids[1:], (grids[0] > 0.0).astype(F32), grids[0] / LEVELS
            )
            flats = [cells[0:ROWS, 0:LANES] for cells in ahead]
            send_plane(step, flats + [code])
        else:
            flats = [inside(c) for c in substep(eta, flow_u, flow_v, wet, depth)]
            send_plane(step, flats)
        rim_rows(mom_in, 0, MOVING, 0)
        stage_edge(mom_in, 0, MOVING, near)
        mom_out[...] = apply(mom_in, rows_uv + 2 * MOVING, LANES)
        rim_laps(mom_out, 0, MOVING, 0, MOVING)
        own_laps(mom_out, 0, MOVING)
        stage_own(mom_in, 0, MOVING, lp)
        stage_edge(mom_in, 0, MOVING, lap_near)
        mom_out[0:rows_uv] = apply(mom_in, rows_uv, LANES)

        def buoyancy(k, carry):
            act = lax.convert_element_type(k, F32) < code
            at = EXT * (MOVING + k) + OWN
            rows = pl.ds(pl.multiple_of(ROWS * k, ROWS), ROWS)
            bih_b = laplace(MOVING + k, lp, buoy_out[rows, 0:LANES])
            u, v = fx[pl.ds(EXT * k + OWN, ROWS)], fx[pl.ds(EXT * (LEVELS + k) + OWN, ROWS)]
            b = fx[pl.ds(at, ROWS)]
            b_x = fx[pl.ds(at + 1, ROWS)] - fx[pl.ds(at - 1, ROWS)]
            b_y = buoy_out[rows, LANES : 2 * LANES]
            tend_b = -0.5 * (u * b_x + v * b_y) - 0.02 * bih_b
            new_b = jnp.where(act, b + 0.2 * tend_b, 0.0)
            if step == STEPS - 1:
                out_b[k] = new_b
            else:
                in_3d[2, k] = new_b
            return carry

        def level(k, carry):
            press_x, press_y, force_u, force_v, col_u, col_v = carry
            act = (lax.convert_element_type(k, F32) < code).astype(F32)
            rows = pl.ds(pl.multiple_of(ROWS * k, ROWS), ROWS)
            rows_v = pl.ds(pl.multiple_of(ROWS * (LEVELS + k), ROWS), ROWS)
            bih_u = laplace(k, lp, mom_out[rows])
            bih_v = laplace(LEVELS + k, lp, mom_out[rows_v])
            u, v = fx[pl.ds(EXT * k + OWN, ROWS)], fx[pl.ds(EXT * (LEVELS + k) + OWN, ROWS)]
            at = EXT * (MOVING + k) + OWN
            press_x = press_x + (fx[pl.ds(at + 1, ROWS)] - fx[pl.ds(at - 1, ROWS)])
            press_y = press_y + buoy_out[rows, LANES : 2 * LANES]
            tend_u = (-0.25 / LEVELS) * press_x + 0.1 * v - 0.02 * bih_u
            tend_v = (-0.25 / LEVELS) * press_y - 0.1 * u - 0.02 * bih_v
            su = act * (u + 0.2 * tend_u)
            sv = act * (v + 0.2 * tend_v)
            star_u[k] = su
            star_v[k] = sv
            return (
                press_x, press_y, force_u + act * tend_u, force_v + act * tend_v,
                col_u + su, col_v + sv,
            )

        _, _, force_u, force_v, col_u, col_v = lax.fori_loop(
            0, LEVELS, level, (zero,) * 6, unroll=True
        )
        force_u, force_v = force_u / LEVELS, force_v / LEVELS
        fx_send[step, 0:ROWS] = force_u
        fx_send[step, ROWS : 2 * ROWS] = force_v
        fy_send[step] = jnp.where(
            rim_lanes[0:8], force_u[0:8],
            jnp.where(
                lane8 < 48, turn(force_u[8:16], 32, 1),
                jnp.where(lane8 < 80, turn(force_v[0:8], 64, 1), turn(force_v[8:16], 96, 1)),
            ),
        )
        start(FORCE, step)
        if step < STEPS - 1:
            def pack_star(k, strips):
                strips = put_v(step + 1, k, star_u[k], strips)
                return put_v(step + 1, LEVELS + k, star_v[k], strips)

            strips = lax.fori_loop(0, LEVELS, pack_star, (zero, zero), unroll=True)
            strips = put_flat(step + 1, 1, col_u, strips)
            strips = put_flat(step + 1, 2, col_v, strips)
            start_far(RIMS, step + 1)
        if step == 0:
            arrive(EARLY, step)
        rim_laps(buoy_out, MOVING, LEVELS, BUOY_NEAR, BUOY_FAR)
        own_laps(buoy_out, MOVING, LEVELS)
        stage_own(buoy_in, MOVING, LEVELS, lp)
        stage_edge(buoy_in, MOVING, LEVELS, lap_near)
        buoy_out[0:rows_b, 0:LANES] = apply(buoy_in, rows_b, LANES)
        lax.fori_loop(0, LEVELS, buoyancy, 0, unroll=True)
        if step < STEPS - 1:
            def pack_b(k, strips):
                cells = in_3d[2, k]
                fx[pl.ds(EXT * (MOVING + k) + OWN, ROWS)] = cells
                return put_b(step + 1, k, cells, strips)

            strips = lax.fori_loop(0, LEVELS, pack_b, strips, unroll=True)
            strips = turn(strips[0], -2, 1), strips[1]
            y_send[step + 1, 0] = strips[0]
            y_send[step + 1, 1] = strips[1]
            start_far(EARLY, step + 1)
            start_near(RIMS, step + 1)
            start_near(EARLY, step + 1)
            stage_own(buoy_in, MOVING, LEVELS, fx)
        arrive(PLANE, step)
        sides = [gy_recv[step, r] for r in range(6)]

        def plane(own, a):
            rows = slice(ROWS * a, ROWS * (a + 1))
            return wide(own, gx_recv[step, 0, rows], gx_recv[step, 1, rows], sides, a)

        if step == 0:
            rows = pl.ds(CODE_PLANE, ROWS)
            code_wide = wide(code, x_recv[0, 0, rows], x_recv[0, 1, rows], sides, 3)
            wet, depth = (code_wide > 0.0).astype(F32), code_wide / LEVELS
        state = [plane(cells, a) for a, cells in enumerate(flats)]
        arrive(FORCE, step)
        beside = [[], []]
        for r in range(3):
            strip = jnp.where((lane8 & 16) == 0, fy_recv[step, r + 3], fy_recv[step, r])
            for part in range(4):
                rolled = turn(strip, -32 * part, 1) if part else strip
                beside[part // 2].append(jnp.where(rim_lanes[0:8], rolled, 0.0))
        push = []
        for a, own in enumerate((force_u, force_v)):
            rows = slice(ROWS * a, ROWS * (a + 1))
            main = [fx_recv[step, 0, rows], own, fx_recv[step, 1, rows]]
            push.append(0.2 * jnp.concatenate(
                [jnp.concatenate(main, axis=0), jnp.concatenate(beside[a], axis=0)], axis=1
            ))
        eta, flow_u, flow_v, sum_u, sum_v = barotropic(state, push, wet, depth)
        shift_u = (SCALE * inside(sum_u) - col_u) / lay
        shift_v = (SCALE * inside(sum_v) - col_v) / lay

        def couple(k, carry):
            act = lax.convert_element_type(k, F32) < code
            new_u = jnp.where(act, star_u[k] + shift_u, 0.0)
            new_v = jnp.where(act, star_v[k] + shift_v, 0.0)
            if step == STEPS - 1:
                out_u[k] = new_u
                out_v[k] = new_v
            else:
                fx[pl.ds(EXT * k + OWN, ROWS)] = new_u
                fx[pl.ds(EXT * (LEVELS + k) + OWN, ROWS)] = new_v
            return carry

        lax.fori_loop(0, LEVELS, couple, 0, unroll=True)
        if step < STEPS - 1:
            stage_own(mom_in, 0, MOVING, fx)

    out_eta[...] = inside(eta)
    out_tu[...] = inside(flow_u)
    out_tv[...] = inside(flow_v)
    for step in range(STEPS):
        for phase in (RIMS, FORCE, PLANE, EARLY):
            sent(phase, step)


def per_device(velocity_u, velocity_v, buoyancy, surface, transport_u, transport_v, ocean, layers):
    cube = jax.ShapeDtypeStruct(velocity_u.shape, F32)
    flat = jax.ShapeDtypeStruct(surface.shape, F32)
    hbm = pl.BlockSpec(memory_space=pltpu.HBM)
    vmem = pl.BlockSpec(memory_space=pltpu.VMEM)
    outs = (cube, cube, cube, flat, flat, flat)
    args = [
        pltpu.with_memory_space_constraint(x, pltpu.HBM)
        for x in (velocity_u, velocity_v, buoyancy, surface, transport_u, transport_v, ocean, layers)
    ]
    block = (LEVELS, ROWS, LANES)
    middle = pl.pallas_call(
        kernel,
        out_shape=outs,
        in_specs=[hbm] * 8,
        out_specs=(vmem,) * 6,
        scratch_shapes=[
            pltpu.VMEM(block, F32),
            pltpu.VMEM(block, F32),
            pltpu.VMEM((STACK * EXT, LANES), F32),
            pltpu.VMEM((STACK * EXT, LANES), F32),
            pltpu.VMEM((ROWS + 8, LANES), F32),
            pltpu.VMEM((4, 8, LANES), F32),
            pltpu.VMEM((2, 2 * MOVING, LANES), F32),
            pltpu.VMEM((FIELDS,) + block, F32),
            pltpu.VMEM((3, ROWS, LANES), F32),
            pltpu.VMEM((2, ROWS, LANES), jnp.int32),
            pltpu.VMEM((4 * LANES, 2 * LANES), BF16),
            pltpu.VMEM((MOVING * (ROWS + 2), 4 * LANES), BF16),
            pltpu.VMEM((LEVELS * (ROWS + 2), 4 * LANES), BF16),
            pltpu.VMEM((MOVING * (ROWS + 2), LANES), F32),
            pltpu.VMEM((LEVELS * (ROWS + 2), 2 * LANES), F32),
            pltpu.VMEM((STEPS, 2, RIM, LANES), F32),
            pltpu.VMEM((STEPS, 2, ROWS, LANES), F32),
            pltpu.VMEM((STEPS, 2, RIM, LANES), F32),
            pltpu.VMEM((STEPS, 6, ROWS, LANES), F32),
            pltpu.VMEM((STEPS, 3 * ROWS, LANES), F32),
            pltpu.VMEM((STEPS, 2, 8, LANES), F32),
            pltpu.VMEM((STEPS, 2, 3 * ROWS, LANES), F32),
            pltpu.VMEM((STEPS, 6, 8, LANES), F32),
            pltpu.VMEM((STEPS, 2 * ROWS, LANES), F32),
            pltpu.VMEM((STEPS, 8, LANES), F32),
            pltpu.VMEM((STEPS, 2, 2 * ROWS, LANES), F32),
            pltpu.VMEM((STEPS, 6, 8, LANES), F32),
            pltpu.SemaphoreType.DMA((8,)),
            pltpu.SemaphoreType.DMA((4 * STEPS, 8)),
            pltpu.SemaphoreType.DMA((4 * STEPS, 8)),
        ],
        compiler_params=pltpu.CompilerParams(
            collective_id=0, has_side_effects=True, vmem_limit_bytes=16 * 2**20
        ),
    )(*args)
    return tuple(
        pl.pallas_call(
            store_kernel,
            out_shape=outs,
            in_specs=[vmem] * 6,
            out_specs=(hbm,) * 6,
            scratch_shapes=[pltpu.SemaphoreType.DMA((6,))],
            compiler_params=pltpu.CompilerParams(vmem_limit_bytes=16 * 2**20),
        )(*middle)
    )


def solution(mesh):
    cube, flat = P(None, "gx", "gy"), P("gx", "gy")
    return jax.shard_map(
        per_device,
        mesh=mesh,
        in_specs=(cube, cube, cube, flat, flat, flat, flat, flat),
        out_specs=(cube, cube, cube, flat, flat, flat),
        check_vma=False,
    )
```

```python
import functools

import jax
import jax.numpy as jnp
from jax import lax
from jax.experimental import pallas as pl
from jax.experimental.pallas import tpu as pltpu
from jax.sharding import PartitionSpec as P

SUB = 8
STEPS = 2
LANES = 128
ROWS = 16
LEVELS = 16
FIELDS = 3
STACK = FIELDS * LEVELS
MESH = pl.DeviceIdType.MESH
F32 = jnp.float32
BF16 = jnp.bfloat16

DIRS = [(-1, 0), (1, 0), (0, -1), (0, 1), (-1, -1), (-1, 1), (1, -1), (1, 1)]
SIDES = [(-1, -1), (0, -1), (1, -1), (-1, 1), (0, 1), (1, 1)]
MOVING = 2 * LEVELS
FLAT_ROW = 0
MOM_NEAR = FLAT_ROW + 8
MOM_FAR = MOM_NEAR + MOVING
BUOY_NEAR = MOM_FAR + MOVING
BUOY_FAR = BUOY_NEAR + LEVELS
CODE_PLANE = BUOY_FAR + LEVELS
RIM = CODE_PLANE + ROWS
HALF = LANES // 2


RIMS, FORCE, PLANE, EARLY, CUBES = 0, 1, 2, 3, 4
PHASES = 5
EXT = 32
OWN = 8
SCALE = LEVELS / SUB


def turn(x, shift, axis):
    return pltpu.roll(x, shift % x.shape[axis] if isinstance(shift, int) else shift, axis)


def fold(cells):
    low = lax.broadcasted_iota(jnp.int32, (8, LANES), 1) < HALF
    return jnp.where(low, cells[0:8], turn(cells[8:16], HALF, 1))


def unfold(cells):
    return jnp.concatenate([cells, turn(cells, HALF, 1)], axis=0)


def split(x):
    high = x.astype(BF16)
    return high, (x - high.astype(F32)).astype(BF16)


def pick(mask, x):
    return tuple(jnp.where(mask, part.astype(F32), 0.0).astype(BF16) for part in split(x))


def lane_weights():
    src = lax.broadcasted_iota(jnp.int32, (LANES, LANES), 0)
    dst = lax.broadcasted_iota(jnp.int32, (LANES, LANES), 1)
    ahead, behind = (src == dst + 1).astype(F32), (src == dst - 1).astype(F32)
    odd = (src & 1) == 1
    first = jnp.logical_and(odd, dst == 0).astype(F32)
    last = jnp.logical_and(jnp.logical_not(odd), dst == LANES - 1).astype(F32)
    return [
        [(ahead + behind).astype(BF16), (ahead - behind).astype(BF16)],
        [(last + first).astype(BF16), (last - first).astype(BF16)],
    ]


def pack_flat(arrays):
    lane = lax.broadcasted_iota(jnp.int32, (ROWS, LANES), 1)
    to_left = to_right = jnp.zeros((ROWS, LANES), F32)
    for a, cells in enumerate(arrays):
        to_right = jnp.where((lane >> 4) == a, turn(cells, 16 * a + 16, 1), to_right)
        to_left = jnp.where((lane >> 4) == a, turn(cells, 16 * a, 1), to_left)
    return fold(to_left), fold(to_right)


def wide(own, up, down, sides, a):
    lane = lax.broadcasted_iota(jnp.int32, (ROWS, LANES), 1)
    blocks = []
    for r in range(3):
        from_left, from_right = unfold(sides[r]), unfold(sides[r + 3])
        left, right = turn(from_left, 112 - 16 * a, 1), turn(from_right, -16 * a, 1)
        blocks.append(jnp.where(lane < 16, right, jnp.where(lane >= 112, left, 0.0)))
    main = jnp.concatenate([up, own, down], axis=0)
    return jnp.concatenate([main, jnp.concatenate(blocks, axis=0)], axis=1)


def substep(eta, tu, tv, wet, depth, push=None):
    div = (turn(tu, -1, 0) - turn(tu, 1, 0)) + (turn(tv, -1, 1) - turn(tv, 1, 1))
    eta = wet * (eta - 0.125 * div)
    thick = 0.125 * (depth + eta)
    new_u = 0.98 * tu - thick * (turn(eta, -1, 0) - turn(eta, 1, 0)) + 0.05 * tv
    new_v = 0.98 * tv - thick * (turn(eta, -1, 1) - turn(eta, 1, 1)) - 0.05 * tu
    if push is not None:
        new_u, new_v = new_u + push[0], new_v + push[1]
    return eta, wet * new_u, wet * new_v


def barotropic(state, push, wet, depth):
    eta, tu, tv = state
    tu, tv = tu + wet * push[0], tv + wet * push[1]

    def one(_, carry):
        eta, tu, tv, sum_u, sum_v = carry
        eta, tu, tv = substep(eta, tu, tv, wet, depth, push)
        return eta, tu, tv, sum_u + tu, sum_v + tv

    return lax.fori_loop(0, SUB - 1, one, (eta, tu, tv, tu, tv), unroll=True)


def inside(cells):
    return cells[ROWS : 2 * ROWS, 0:LANES]


def lane_pair(odd, cells, even_at, odd_at):
    shape = odd.shape
    return jnp.where(
        odd,
        jnp.broadcast_to(cells[:, odd_at : odd_at + 1], shape),
        jnp.broadcast_to(cells[:, even_at : even_at + 1], shape),
    )


def store_kernel(*refs):
    count = (len(refs) - 1) // 2
    sem = refs[-1]
    copies = [
        pltpu.make_async_copy(src, dst, sem.at[i])
        for i, (src, dst) in enumerate(zip(refs[:count], refs[count:-1]))
    ]
    for copy in copies:
        copy.start()
    for copy in copies:
        copy.wait()


def kernel(
    vel_u, vel_v, buoy, surface, trans_u, trans_v, ocean, layers,
    out_u, out_v, out_b, out_eta, out_tu, out_tv,
    star_u, star_v,
    fx, lp, near_ext, ring_rows, rim_new, in_3d, in_2d, in_int,
    lane_w, mom_in, buoy_in, mom_out, buoy_out,
    x_send, y_send, x_recv, y_recv, gx_send, gy_send, gx_recv, gy_recv,
    fx_send, fy_send, fx_recv, fy_recv, in_sem, send_sem, recv_sem,
):
    loads = []
    for a, ref in enumerate((vel_u, vel_v, buoy)):
        loads.append(pltpu.make_async_copy(ref, in_3d.at[a], in_sem.at[a]))
    for a, ref in enumerate((surface, trans_u, trans_v)):
        loads.append(pltpu.make_async_copy(ref, in_2d.at[a], in_sem.at[3 + a]))
    for a, ref in enumerate((ocean, layers)):
        loads.append(pltpu.make_async_copy(ref, in_int.at[a], in_sem.at[6 + a]))
    for load in loads:
        load.start()
    gx, gy = lax.axis_index("gx"), lax.axis_index("gy")
    nx, ny = lax.axis_size("gx"), lax.axis_size("gy")

    def exists(d):
        ok = jnp.bool_(True)
        if d[0] == -1:
            ok = jnp.logical_and(ok, gx > 0)
        if d[0] == 1:
            ok = jnp.logical_and(ok, gx < nx - 1)
        if d[1] == -1:
            ok = jnp.logical_and(ok, gy > 0)
        if d[1] == 1:
            ok = jnp.logical_and(ok, gy < ny - 1)
        return ok

    here = {d: exists(d) for d in DIRS}
    barrier = pltpu.get_barrier_semaphore()
    total_near = jnp.int32(0)
    for d in DIRS:
        total_near = total_near + here[d].astype(jnp.int32)

        @pl.when(here[d])
        def _(d=d):
            pl.semaphore_signal(barrier, inc=1, device_id=(gx + d[0], gy + d[1]), device_id_type=MESH)

    for d in DIRS:
        @pl.when(jnp.logical_not(here[d]))
        def _(d=d):
            for p in range(STEPS):
                if d[1] == 0:
                    s = 0 if d[0] < 0 else 1
                    x_recv[p, s] = jnp.zeros(x_recv.shape[2:], F32)
                    gx_recv[p, s] = jnp.zeros(gx_recv.shape[2:], F32)
                    fx_recv[p, s] = jnp.zeros(fx_recv.shape[2:], F32)
                else:
                    s = SIDES.index(d)
                    y_recv[p, s] = jnp.zeros(y_recv.shape[2:], F32)
                    gy_recv[p, s] = jnp.zeros(gy_recv.shape[2:], F32)
                    fy_recv[p, s] = jnp.zeros(fy_recv.shape[2:], F32)

    def copies(phase, step):
        result = []
        for i, d in enumerate(DIRS):
            back = (-d[0], -d[1])
            if d[1] == 0:
                src_at, dst_at = (0 if d[0] < 0 else 1), (0 if back[0] < 0 else 1)
                if phase == FORCE:
                    src, dst = fx_send.at[step], fx_recv.at[step, dst_at]
                elif phase == PLANE:
                    src, dst = gx_send.at[step], gx_recv.at[step, dst_at]
                else:
                    first, end = {
                        (RIMS, 0): (FLAT_ROW, MOM_NEAR),
                        (CUBES, 0): (MOM_NEAR, BUOY_FAR),
                        (EARLY, 0): (BUOY_FAR, RIM),
                        (RIMS, 1): (FLAT_ROW, BUOY_NEAR),
                        (EARLY, 1): (BUOY_NEAR, CODE_PLANE),
                    }[phase, min(step, 1)]
                    rows = pl.ds(first, end - first)
                    src, dst = x_send.at[step, src_at, rows], x_recv.at[step, dst_at, rows]
            else:
                src_at, dst_at = (0 if d[1] < 0 else 1), SIDES.index(back)
                if phase == FORCE:
                    src, dst = fy_send.at[step], fy_recv.at[step, dst_at]
                elif phase == PLANE:
                    src, dst = gy_send.at[step, src_at], gy_recv.at[step, dst_at]
                elif phase == CUBES or phase == (RIMS if step else EARLY):
                    continue
                else:
                    src, dst = y_send.at[step, src_at], y_recv.at[step, dst_at]
                    if d[0] != 0:
                        rows = pl.ds(0, 8) if d[0] < 0 else pl.ds(8, 8)
                        src, dst = src.at[rows], dst.at[rows]
            at = phase * STEPS + step
            copy = functools.partial(
                pltpu.make_async_remote_copy, src_ref=src, dst_ref=dst,
                send_sem=send_sem.at[at, i], recv_sem=recv_sem.at[at, DIRS.index(back)],
                device_id=(gx + d[0], gy + d[1]), device_id_type=MESH,
            )
            result.append((d, copy))
        return result

    odd_row = lax.rem(gx, 2) == 1

    def start_rows(phase, step, two_hops):
        pending = [(d, copy) for d, copy in copies(phase, step) if d[0]]
        pending.sort(key=lambda item: (item[0][1] == 0) != two_hops)
        for d, copy in pending:
            @pl.when(jnp.logical_and(here[d], odd_row == (two_hops == (d[0] > 0))))
            def _(copy=copy):
                copy().start()

    def start_far(phase, step):
        start_rows(phase, step, True)
        for d, copy in copies(phase, step):
            if d[0] == 0:
                @pl.when(here[d])
                def _(copy=copy):
                    copy().start()

    def start_near(phase, step):
        start_rows(phase, step, False)

    def start(phase, step):
        start_far(phase, step)
        start_near(phase, step)

    def arrive(phase, step):
        by_dir = dict(copies(phase, step))
        for d in by_dir:
            @pl.when(here[d])
            def _(d=d):
                by_dir[(-d[0], -d[1])]().wait_recv()

    def sent(phase, step):
        for d, copy in copies(phase, step):
            @pl.when(here[d])
            def _(copy=copy):
                copy().wait_send()

    lane = lax.broadcasted_iota(jnp.int32, (ROWS, LANES), 1)
    pair = lane >> 1
    lane8 = lane[0:8]
    odd = (lane & 1) == 1
    rim_lanes = jnp.logical_or(lane < 16, lane >= LANES - 16)
    zero = jnp.zeros((ROWS, LANES), F32)

    def put(step, j, near_at, far_at, cells, strips):
        x_send[step, 0, pl.ds(near_at, 1)] = cells[0:1]
        x_send[step, 0, pl.ds(far_at, 1)] = cells[1:2]
        x_send[step, 1, pl.ds(near_at, 1)] = cells[ROWS - 1 : ROWS]
        x_send[step, 1, pl.ds(far_at, 1)] = cells[ROWS - 2 : ROWS - 1]
        to_left, to_right = strips
        rolled = turn(cells, 2 * j + 2, 1)
        to_right = jnp.where(pair == j, rolled, to_right)
        to_left = jnp.where(pair == j + 1, rolled, to_left)
        return to_left, to_right

    def put_v(step, j, cells, strips):
        return put(step, j, MOM_NEAR + j, MOM_FAR + j, cells, strips)

    def put_b(step, k, cells, strips):
        j = MOVING + k
        return put(step, j, BUOY_NEAR + k, BUOY_FAR + k, cells, strips)

    def put_flat(step, a, cells, strips):
        return put(step, STACK + a, FLAT_ROW + 2 * a, FLAT_ROW + 2 * a + 1, cells, strips)

    def send_plane(step, flats):
        flat_left, flat_right = pack_flat(flats)
        gy_send[step, 0] = flat_left
        gy_send[step, 1] = flat_right
        for a, cells in enumerate(flats[0:3]):
            gx_send[step, ROWS * a : ROWS * (a + 1)] = cells
        start(PLANE, step)

    ring_rows[...] = jnp.zeros(ring_rows.shape, F32)
    for r, blocks in enumerate(lane_weights()):
        for c, block in enumerate(blocks):
            for at in (2 * r, 2 * r + 1):
                lane_w[LANES * at : LANES * (at + 1), LANES * c : LANES * (c + 1)] = block
    def put_parts(ref, at, rows, parts, col):
        for c, part in enumerate(parts):
            ref[pl.ds(at, rows), LANES * (col + c) : LANES * (col + c + 1)] = part

    def stage_own(ref, first, count, source):
        def one(i, carry):
            at = pl.multiple_of(ROWS * i, ROWS)
            put_parts(ref, at, ROWS, split(source[pl.ds(EXT * (first + i) + OWN, ROWS)]), 0)
            return carry

        lax.fori_loop(0, count, one, 0, unroll=True)

    def stage_edge(ref, first, count, edge):
        def one(i, carry):
            at = pl.multiple_of(ROWS * i, ROWS)
            put_parts(ref, at, ROWS, pick(pair == first + i, edge), 2)
            return carry

        lax.fori_loop(0, count, one, 0, unroll=True)

    loads[6].wait()
    loads[7].wait()
    lay = in_int[1].astype(F32)
    code = jnp.where(in_int[0] > 0, lay, 0.0)
    strips = put_flat(0, 0, code, (zero, zero))
    for a in range(FIELDS):
        loads[a].wait()

        def pack(k, strips, a=a):
            cells = in_3d[a, k]
            fx[pl.ds(EXT * (a * LEVELS + k) + OWN, ROWS)] = cells
            if a < 2:
                return put_v(0, a * LEVELS + k, cells, strips)
            return put_b(0, k, cells, strips)

        strips = lax.fori_loop(0, LEVELS, pack, strips, unroll=True)
    flats = [code]
    for a in range(3):
        loads[3 + a].wait()
        flats.append(in_2d[a])
        strips = put_flat(0, 1 + a, in_2d[a], strips)
    strips = turn(strips[0], -2, 1), strips[1]
    y_send[0, 0] = strips[0]
    y_send[0, 1] = strips[1]
    pl.semaphore_wait(barrier, total_near)
    for side in range(2):
        x_send[0, side, pl.ds(CODE_PLANE, ROWS)] = code
    start_far(RIMS, 0)
    start_far(CUBES, 0)
    start_near(RIMS, 0)
    stage_own(mom_in, 0, MOVING, fx)
    start_near(CUBES, 0)
    start(EARLY, 0)
    stage_own(buoy_in, MOVING, LEVELS, fx)

    around = (ROWS + 8, LANES)
    lane24 = lax.broadcasted_iota(jnp.int32, around, 1)
    odd24 = (lane24 & 1) == 1
    level24 = ((lane24 >> 1) & (LEVELS - 1)).astype(F32)
    level_pair = level24[0:ROWS]
    moving24 = lane24 < 2 * MOVING
    is_u24 = lane24 < 2 * LEVELS
    upper = lax.broadcasted_iota(jnp.int32, (8, LANES), 0) < 4

    def cyclic(own, below, above):
        return jnp.concatenate([own, jnp.where(upper, below, above)], axis=0)

    def beside_columns(left24, right24, j):
        return jnp.where(
            lane24 < HALF, turn(right24, -2 * j, 1), turn(left24, 126 - 2 * j, 1)
        )

    def side24(cells):
        tile = cells[:, LANES : 2 * LANES]
        return cyclic(tile[ROWS : 2 * ROWS], tile[2 * ROWS : 2 * ROWS + 8], tile[8:ROWS])

    for step in range(STEPS):
        if step:
            flats = [inside(c) for c in substep(eta, flow_u, flow_v, wet, depth)]
            send_plane(step, flats)
        arrive(RIMS, step)
        if step:
            arrive(EARLY, step)
        left24 = cyclic(y_recv[step, 1], y_recv[step, 2, 0:8], y_recv[step, 0, 8:16])
        right24 = cyclic(y_recv[step, 4], y_recv[step, 5, 0:8], y_recv[step, 3, 8:16])
        near24 = jnp.where(odd24, left24, right24)
        far = jnp.where(odd, right24[0:ROWS], left24[0:ROWS])
        far = jnp.where(odd, turn(far, 1, 1), turn(far, -1, 1))
        inner = jnp.where(odd, turn(strips[0], 1, 1), turn(strips[1], -1, 1))

        if step == 0:
            code_near = lane_pair(odd24, near24, 2 * STACK, 2 * STACK + 1)
            code_far = lane_pair(odd, far, 2 * STACK, 2 * STACK + 1)
            code_inner = lane_pair(odd, code, LANES - 1, 0)
            act_near = level24 < code_near
            grids = []
            for a, own in enumerate(flats):
                near_at, far_at = FLAT_ROW + 2 * a, FLAT_ROW + 2 * a + 1
                ring_rows[a, 0:1] = x_recv[0, 1, pl.ds(near_at, 1)]
                ring_rows[a, 1:2] = x_recv[0, 1, pl.ds(far_at, 1)]
                ring_rows[a, 6:7] = x_recv[0, 0, pl.ds(far_at, 1)]
                ring_rows[a, 7:8] = x_recv[0, 0, pl.ds(near_at, 1)]
                main = jnp.concatenate([own, ring_rows[a]], axis=0)
                grids.append(jnp.concatenate(
                    [main, beside_columns(left24, right24, STACK + a)], axis=1
                ))
            code_side = grids[0][:, LANES : 2 * LANES]
            ahead = substep(
                *grids[1:], (grids[0] > 0.0).astype(F32), grids[0] / LEVELS
            )
            flats = [cells[0:ROWS, 0:LANES] for cells in ahead]
            send_plane(step, flats + [code])
        else:
            shift_side = [
                (SCALE * side24(total) - beside_columns(left24, right24, STACK + 1 + a))
                / jnp.maximum(code_side, 1.0)
                for a, total in enumerate((sum_u, sum_v))
            ]

            def couple_pairs(cells, near_code, rows, levels, even_at, odd_at, sources):
                parity = odd24[0:rows]
                shift = jnp.where(
                    is_u24[0:rows],
                    lane_pair(parity, sources[0][0:rows], even_at, odd_at),
                    lane_pair(parity, sources[1][0:rows], even_at, odd_at),
                )
                moved = jnp.where(levels < near_code, cells + shift, 0.0)
                return jnp.where(moving24[0:rows], moved, cells)

            near24 = couple_pairs(
                near24, code_near, ROWS + 8, level24, 0, LANES - 1, shift_side
            )
            far = couple_pairs(far, code_far, ROWS, level_pair, 1, LANES - 2, shift_side)
            inner = couple_pairs(
                inner, code_inner, ROWS, level_pair, LANES - 1, 0, (shift_u, shift_v)
            )
            level16 = lax.broadcasted_iota(jnp.int32, (LEVELS, LANES), 0).astype(F32)
            for side in range(2):
                for away in range(2):
                    at = (ROWS - 1 - away, 2 * ROWS + away)[side]
                    code_row = x_recv[0, side, pl.ds(FLAT_ROW + away, 1)]
                    for a, total in enumerate((sum_u, sum_v)):
                        column = x_recv[1, side, pl.ds(FLAT_ROW + 2 * (1 + a) + away, 1)]
                        shift = (
                            SCALE * total[at : at + 1, 0:LANES] - column
                        ) / jnp.maximum(code_row, 1.0)
                        at_row = MOVING * away + LEVELS * a
                        star = x_recv[1, side, pl.ds(MOM_NEAR + at_row, LEVELS)]
                        rim_new[side, pl.ds(at_row, LEVELS)] = jnp.where(
                            level16 < code_row, star + shift, 0.0
                        )

        near_ext[...] = near24
        near = near24[0:ROWS]
        lap_near = jnp.where(
            act_near,
            turn(near24, 1, 0) + turn(near24, -1, 0) - 4.0 * near24,
            0.0,
        )[0:ROWS] + jnp.where(act_near[0:ROWS], far + inner, 0.0)

        def rim_cells(side, first, count, at):
            if first == 0 and step:
                return rim_new[side, pl.ds(at - MOM_NEAR, count)]
            return x_recv[step, side, pl.ds(at, count)]

        def rim_rows(ref, first, count, near_at):
            row = lax.broadcasted_iota(jnp.int32, (count, LANES), 0)
            group = lax.broadcasted_iota(jnp.int32, (count, LANES), 1) >> 1
            for side in range(2):
                cells = rim_cells(side, first, count, near_at)
                at = ROWS * count + count * side
                corner = jnp.broadcast_to(
                    near_ext[pl.ds((ROWS + 7, ROWS)[side], 1)], (count, LANES)
                )
                put_parts(ref, at, count, split(cells), 0)
                put_parts(ref, at, count, pick(group == first + row, corner), 2)
                fx[pl.ds(EXT * first + (OWN - 1, OWN + ROWS)[side], count, stride=EXT)] = cells

        def rim_laps(ref, first, count, near_at, far_at):
            level_of = lax.broadcasted_iota(jnp.int32, (count, LANES), 0) & (LEVELS - 1)
            for side in range(2):
                cells = rim_cells(side, first, count, near_at)
                edge = EXT * first + (OWN, OWN + ROWS - 1)[side]
                beside = rim_cells(side, first, count, far_at) + fx[
                    pl.ds(edge, count, stride=EXT)
                ]
                lanes_sum = ref[pl.ds(ROWS * count + count * side, count), 0:LANES]
                code_row = x_recv[0, side, pl.ds(FLAT_ROW, 1)]
                lap = jnp.where(
                    level_of.astype(F32) < code_row, beside + lanes_sum - 4.0 * cells, 0.0
                )
                lp[pl.ds(EXT * first + (OWN - 1, OWN + ROWS)[side], count, stride=EXT)] = lap

        def laplace(j, source, lanes_sum):
            at = EXT * j + OWN
            return (
                source[pl.ds(at - 1, ROWS)] + source[pl.ds(at + 1, ROWS)]
                + lanes_sum - 4.0 * source[pl.ds(at, ROWS)]
            )

        def own_laps(ref, first, count):
            def one(i, carry):
                level_at = lax.convert_element_type(i & (LEVELS - 1), F32)
                lanes_sum = ref[pl.ds(pl.multiple_of(ROWS * i, ROWS), ROWS), 0:LANES]
                lap = laplace(first + i, fx, lanes_sum)
                lp[pl.ds(EXT * (first + i) + OWN, ROWS)] = jnp.where(level_at < code, lap, 0.0)
                return carry

            lax.fori_loop(0, count, one, 0, unroll=True)

        def apply(source, rows, width):
            return jnp.dot(
                source[0:rows], lane_w[:, 0:width], preferred_element_type=F32
            )

        rows_uv, rows_b = MOVING * ROWS, LEVELS * ROWS
        stage_edge(buoy_in, MOVING, LEVELS, near)
        stage_edge(mom_in, 0, MOVING, near)
        if step == 0:
            arrive(CUBES, step)
        rim_rows(buoy_in, MOVING, LEVELS, BUOY_NEAR)
        buoy_out[...] = apply(buoy_in, rows_b + 2 * LEVELS, 2 * LANES)
        rim_rows(mom_in, 0, MOVING, MOM_NEAR)
        mom_out[...] = apply(mom_in, rows_uv + 2 * MOVING, LANES)
        rim_laps(mom_out, 0, MOVING, MOM_NEAR, MOM_FAR)
        own_laps(mom_out, 0, MOVING)
        stage_own(mom_in, 0, MOVING, lp)
        stage_edge(mom_in, 0, MOVING, lap_near)
        mom_out[0:rows_uv] = apply(mom_in, rows_uv, LANES)

        def buoyancy(k, carry):
            act = lax.convert_element_type(k, F32) < code
            at = EXT * (MOVING + k) + OWN
            rows = pl.ds(pl.multiple_of(ROWS * k, ROWS), ROWS)
            bih_b = laplace(MOVING + k, lp, buoy_out[rows, 0:LANES])
            u, v = fx[pl.ds(EXT * k + OWN, ROWS)], fx[pl.ds(EXT * (LEVELS + k) + OWN, ROWS)]
            b = fx[pl.ds(at, ROWS)]
            b_x = fx[pl.ds(at + 1, ROWS)] - fx[pl.ds(at - 1, ROWS)]
            b_y = buoy_out[rows, LANES : 2 * LANES]
            tend_b = -0.5 * (u * b_x + v * b_y) - 0.02 * bih_b
            new_b = jnp.where(act, b + 0.2 * tend_b, 0.0)
            if step == STEPS - 1:
                out_b[k] = new_b
            else:
                in_3d[2, k] = new_b
            return carry

        def level(k, carry):
            press_x, press_y, force_u, force_v, col_u, col_v = carry
            act = (lax.convert_element_type(k, F32) < code).astype(F32)
            rows = pl.ds(pl.multiple_of(ROWS * k, ROWS), ROWS)
            rows_v = pl.ds(pl.multiple_of(ROWS * (LEVELS + k), ROWS), ROWS)
            bih_u = laplace(k, lp, mom_out[rows])
            bih_v = laplace(LEVELS + k, lp, mom_out[rows_v])
            u, v = fx[pl.ds(EXT * k + OWN, ROWS)], fx[pl.ds(EXT * (LEVELS + k) + OWN, ROWS)]
            at = EXT * (MOVING + k) + OWN
            press_x = press_x + (fx[pl.ds(at + 1, ROWS)] - fx[pl.ds(at - 1, ROWS)])
            press_y = press_y + buoy_out[rows, LANES : 2 * LANES]
            tend_u = (-0.25 / LEVELS) * press_x + 0.1 * v - 0.02 * bih_u
            tend_v = (-0.25 / LEVELS) * press_y - 0.1 * u - 0.02 * bih_v
            su = act * (u + 0.2 * tend_u)
            sv = act * (v + 0.2 * tend_v)
            star_u[k] = su
            star_v[k] = sv
            return (
                press_x, press_y, force_u + act * tend_u, force_v + act * tend_v,
                col_u + su, col_v + sv,
            )

        _, _, force_u, force_v, col_u, col_v = lax.fori_loop(
            0, LEVELS, level, (zero,) * 6, unroll=True
        )
        force_u, force_v = force_u / LEVELS, force_v / LEVELS
        fx_send[step, 0:ROWS] = force_u
        fx_send[step, ROWS : 2 * ROWS] = force_v
        fy_send[step] = jnp.where(
            rim_lanes[0:8], force_u[0:8],
            jnp.where(
                lane8 < 48, turn(force_u[8:16], 32, 1),
                jnp.where(lane8 < 80, turn(force_v[0:8], 64, 1), turn(force_v[8:16], 96, 1)),
            ),
        )
        start(FORCE, step)
        if step < STEPS - 1:
            def pack_star(k, strips):
                strips = put_v(step + 1, k, star_u[k], strips)
                return put_v(step + 1, LEVELS + k, star_v[k], strips)

            strips = lax.fori_loop(0, LEVELS, pack_star, (zero, zero), unroll=True)
            strips = put_flat(step + 1, 1, col_u, strips)
            strips = put_flat(step + 1, 2, col_v, strips)
            start_far(RIMS, step + 1)
        if step == 0:
            arrive(EARLY, step)
        rim_laps(buoy_out, MOVING, LEVELS, BUOY_NEAR, BUOY_FAR)
        own_laps(buoy_out, MOVING, LEVELS)
        stage_own(buoy_in, MOVING, LEVELS, lp)
        stage_edge(buoy_in, MOVING, LEVELS, lap_near)
        buoy_out[0:rows_b, 0:LANES] = apply(buoy_in, rows_b, LANES)
        lax.fori_loop(0, LEVELS, buoyancy, 0, unroll=True)
        if step < STEPS - 1:
            def pack_b(k, strips):
                cells = in_3d[2, k]
                fx[pl.ds(EXT * (MOVING + k) + OWN, ROWS)] = cells
                return put_b(step + 1, k, cells, strips)

            strips = lax.fori_loop(0, LEVELS, pack_b, strips, unroll=True)
            strips = turn(strips[0], -2, 1), strips[1]
            y_send[step + 1, 0] = strips[0]
            y_send[step + 1, 1] = strips[1]
            start_far(EARLY, step + 1)
            start_near(RIMS, step + 1)
            start_near(EARLY, step + 1)
            stage_own(buoy_in, MOVING, LEVELS, fx)
        arrive(PLANE, step)
        sides = [gy_recv[step, r] for r in range(6)]

        def plane(own, a):
            rows = slice(ROWS * a, ROWS * (a + 1))
            return wide(own, gx_recv[step, 0, rows], gx_recv[step, 1, rows], sides, a)

        if step == 0:
            rows = pl.ds(CODE_PLANE, ROWS)
            code_wide = wide(code, x_recv[0, 0, rows], x_recv[0, 1, rows], sides, 3)
            wet, depth = (code_wide > 0.0).astype(F32), code_wide / LEVELS
        state = [plane(cells, a) for a, cells in enumerate(flats)]
        arrive(FORCE, step)
        beside = [[], []]
        for r in range(3):
            strip = jnp.where((lane8 & 16) == 0, fy_recv[step, r + 3], fy_recv[step, r])
            for part in range(4):
                rolled = turn(strip, -32 * part, 1) if part else strip
                beside[part // 2].append(jnp.where(rim_lanes[0:8], rolled, 0.0))
        push = []
        for a, own in enumerate((force_u, force_v)):
            rows = slice(ROWS * a, ROWS * (a + 1))
            main = [fx_recv[step, 0, rows], own, fx_recv[step, 1, rows]]
            push.append(0.2 * jnp.concatenate(
                [jnp.concatenate(main, axis=0), jnp.concatenate(beside[a], axis=0)], axis=1
            ))
        eta, flow_u, flow_v, sum_u, sum_v = barotropic(state, push, wet, depth)
        shift_u = (SCALE * inside(sum_u) - col_u) / lay
        shift_v = (SCALE * inside(sum_v) - col_v) / lay

        def couple(k, carry):
            act = lax.convert_element_type(k, F32) < code
            new_u = jnp.where(act, star_u[k] + shift_u, 0.0)
            new_v = jnp.where(act, star_v[k] + shift_v, 0.0)
            if step == STEPS - 1:
                out_u[k] = new_u
                out_v[k] = new_v
            else:
                fx[pl.ds(EXT * k + OWN, ROWS)] = new_u
                fx[pl.ds(EXT * (LEVELS + k) + OWN, ROWS)] = new_v
            return carry

        lax.fori_loop(0, LEVELS, couple, 0, unroll=True)
        if step < STEPS - 1:
            stage_own(mom_in, 0, MOVING, fx)

    out_eta[...] = inside(eta)
    out_tu[...] = inside(flow_u)
    out_tv[...] = inside(flow_v)
    for step in range(STEPS):
        for phase in range(PHASES):
            if phase != CUBES or step == 0:
                sent(phase, step)


def per_device(velocity_u, velocity_v, buoyancy, surface, transport_u, transport_v, ocean, layers):
    cube = jax.ShapeDtypeStruct(velocity_u.shape, F32)
    flat = jax.ShapeDtypeStruct(surface.shape, F32)
    hbm = pl.BlockSpec(memory_space=pltpu.HBM)
    vmem = pl.BlockSpec(memory_space=pltpu.VMEM)
    outs = (cube, cube, cube, flat, flat, flat)
    args = [
        pltpu.with_memory_space_constraint(x, pltpu.HBM)
        for x in (velocity_u, velocity_v, buoyancy, surface, transport_u, transport_v, ocean, layers)
    ]
    block = (LEVELS, ROWS, LANES)
    middle = pl.pallas_call(
        kernel,
        out_shape=outs,
        in_specs=[hbm] * 8,
        out_specs=(vmem,) * 6,
        scratch_shapes=[
            pltpu.VMEM(block, F32),
            pltpu.VMEM(block, F32),
            pltpu.VMEM((STACK * EXT, LANES), F32),
            pltpu.VMEM((STACK * EXT, LANES), F32),
            pltpu.VMEM((ROWS + 8, LANES), F32),
            pltpu.VMEM((4, 8, LANES), F32),
            pltpu.VMEM((2, 2 * MOVING, LANES), F32),
            pltpu.VMEM((FIELDS,) + block, F32),
            pltpu.VMEM((3, ROWS, LANES), F32),
            pltpu.VMEM((2, ROWS, LANES), jnp.int32),
            pltpu.VMEM((4 * LANES, 2 * LANES), BF16),
            pltpu.VMEM((MOVING * (ROWS + 2), 4 * LANES), BF16),
            pltpu.VMEM((LEVELS * (ROWS + 2), 4 * LANES), BF16),
            pltpu.VMEM((MOVING * (ROWS + 2), LANES), F32),
            pltpu.VMEM((LEVELS * (ROWS + 2), 2 * LANES), F32),
            pltpu.VMEM((STEPS, 2, RIM, LANES), F32),
            pltpu.VMEM((STEPS, 2, ROWS, LANES), F32),
            pltpu.VMEM((STEPS, 2, RIM, LANES), F32),
            pltpu.VMEM((STEPS, 6, ROWS, LANES), F32),
            pltpu.VMEM((STEPS, 3 * ROWS, LANES), F32),
            pltpu.VMEM((STEPS, 2, 8, LANES), F32),
            pltpu.VMEM((STEPS, 2, 3 * ROWS, LANES), F32),
            pltpu.VMEM((STEPS, 6, 8, LANES), F32),
            pltpu.VMEM((STEPS, 2 * ROWS, LANES), F32),
            pltpu.VMEM((STEPS, 8, LANES), F32),
            pltpu.VMEM((STEPS, 2, 2 * ROWS, LANES), F32),
            pltpu.VMEM((STEPS, 6, 8, LANES), F32),
            pltpu.SemaphoreType.DMA((8,)),
            pltpu.SemaphoreType.DMA((PHASES * STEPS, 8)),
            pltpu.SemaphoreType.DMA((PHASES * STEPS, 8)),
        ],
        compiler_params=pltpu.CompilerParams(
            collective_id=0, has_side_effects=True, vmem_limit_bytes=16 * 2**20
        ),
    )(*args)
    return tuple(
        pl.pallas_call(
            store_kernel,
            out_shape=outs,
            in_specs=[vmem] * 6,
            out_specs=(hbm,) * 6,
            scratch_shapes=[pltpu.SemaphoreType.DMA((6,))],
            compiler_params=pltpu.CompilerParams(vmem_limit_bytes=16 * 2**20),
        )(*middle)
    )


def solution(mesh):
    cube, flat = P(None, "gx", "gy"), P("gx", "gy")
    return jax.shard_map(
        per_device,
        mesh=mesh,
        in_specs=(cube, cube, cube, flat, flat, flat, flat, flat),
        out_specs=(cube, cube, cube, flat, flat, flat),
        check_vma=False,
    )
```

```python
import functools

import jax
import jax.numpy as jnp
from jax import lax
from jax.experimental import pallas as pl
from jax.experimental.pallas import tpu as pltpu
from jax.sharding import PartitionSpec as P

SUB = 8
STEPS = 2
LANES = 128
ROWS = 16
LEVELS = 16
FIELDS = 3
STACK = FIELDS * LEVELS
MESH = pl.DeviceIdType.MESH
F32 = jnp.float32
BF16 = jnp.bfloat16

DIRS = [(-1, 0), (1, 0), (0, -1), (0, 1), (-1, -1), (-1, 1), (1, -1), (1, 1)]
SIDES = [(-1, -1), (0, -1), (1, -1), (-1, 1), (0, 1), (1, 1)]
MOVING = 2 * LEVELS
FLAT_ROW = 0
MOM_NEAR = FLAT_ROW + 8
MOM_FAR = MOM_NEAR + MOVING
BUOY_NEAR = MOM_FAR + MOVING
BUOY_FAR = BUOY_NEAR + LEVELS
CODE_PLANE = BUOY_FAR + LEVELS
RIM = CODE_PLANE + ROWS
HALF = LANES // 2


RIMS, FORCE, PLANE, EARLY, CUBES = 0, 1, 2, 3, 4
PHASES = 5
EXT = 32
OWN = 8
SCALE = LEVELS / SUB


def turn(x, shift, axis):
    return pltpu.roll(x, shift % x.shape[axis] if isinstance(shift, int) else shift, axis)


def fold(cells):
    low = lax.broadcasted_iota(jnp.int32, (8, LANES), 1) < HALF
    return jnp.where(low, cells[0:8], turn(cells[8:16], HALF, 1))


def unfold(cells):
    return jnp.concatenate([cells, turn(cells, HALF, 1)], axis=0)


def split(x):
    high = x.astype(BF16)
    return high, (x - high.astype(F32)).astype(BF16)


def pick(mask, x):
    return tuple(jnp.where(mask, part.astype(F32), 0.0).astype(BF16) for part in split(x))


def lane_weights():
    src = lax.broadcasted_iota(jnp.int32, (LANES, LANES), 0)
    dst = lax.broadcasted_iota(jnp.int32, (LANES, LANES), 1)
    ahead, behind = (src == dst + 1).astype(F32), (src == dst - 1).astype(F32)
    odd = (src & 1) == 1
    first = jnp.logical_and(odd, dst == 0).astype(F32)
    last = jnp.logical_and(jnp.logical_not(odd), dst == LANES - 1).astype(F32)
    return [
        [(ahead + behind).astype(BF16), (ahead - behind).astype(BF16)],
        [(last + first).astype(BF16), (last - first).astype(BF16)],
    ]


def pack_flat(arrays):
    lane = lax.broadcasted_iota(jnp.int32, (ROWS, LANES), 1)
    group = lane[0:8] >> 4
    to_left = to_right = jnp.zeros((8, LANES), F32)
    for a, cells in enumerate(arrays):
        for half in range(2):
            part, at = cells[8 * half : 8 * half + 8], a + 4 * half
            to_right = jnp.where(group == at, turn(part, 16 * at + 16, 1), to_right)
            to_left = jnp.where(group == at, turn(part, 16 * at, 1), to_left)
    return to_left, to_right


def wide(own, up, down, sides, a):
    lane = lax.broadcasted_iota(jnp.int32, (8, LANES), 1)
    blocks = []
    for r in range(3):
        for half in range(2):
            at = a + 4 * half
            left = turn(sides[r], 112 - 16 * at, 1)
            right = turn(sides[r + 3], -16 * at, 1)
            blocks.append(jnp.where(lane < 16, right, jnp.where(lane >= 112, left, 0.0)))
    main = jnp.concatenate([up, own, down], axis=0)
    return jnp.concatenate([main, jnp.concatenate(blocks, axis=0)], axis=1)


def substep(eta, tu, tv, wet, depth, push=None):
    div = (turn(tu, -1, 0) - turn(tu, 1, 0)) + (turn(tv, -1, 1) - turn(tv, 1, 1))
    eta = wet * (eta - 0.125 * div)
    thick = 0.125 * (depth + eta)
    new_u = 0.98 * tu - thick * (turn(eta, -1, 0) - turn(eta, 1, 0)) + 0.05 * tv
    new_v = 0.98 * tv - thick * (turn(eta, -1, 1) - turn(eta, 1, 1)) - 0.05 * tu
    if push is not None:
        new_u, new_v = new_u + push[0], new_v + push[1]
    return eta, wet * new_u, wet * new_v


def substep_once(eta, tu, tv, wet, depth, push, wet_ahead, wet_behind):
    mid = eta - 0.125 * (turn(tu, -1, 0) - turn(tu, 1, 0))
    ahead = wet_ahead * (turn(mid, -1, 1) - 0.125 * (turn(tv, -2, 1) - tv))
    behind = wet_behind * (turn(mid, 1, 1) - 0.125 * (tv - turn(tv, 2, 1)))
    eta = wet * (mid - 0.125 * (turn(tv, -1, 1) - turn(tv, 1, 1)))
    thick = 0.125 * (depth + eta)
    new_u = 0.98 * tu - thick * (turn(eta, -1, 0) - turn(eta, 1, 0)) + 0.05 * tv + push[0]
    new_v = 0.98 * tv - thick * (ahead - behind) - 0.05 * tu + push[1]
    return eta, wet * new_u, wet * new_v


def barotropic(state, push, wet, depth, tail):
    eta, tu, tv = state
    tu, tv = tu + wet * push[0], tv + wet * push[1]

    def one(_, carry):
        eta, tu, tv, sum_u, sum_v = carry
        eta, tu, tv = substep(eta, tu, tv, wet, depth, push)
        return eta, tu, tv, sum_u + tu, sum_v + tv

    cells = lax.fori_loop(0, SUB - 1 - tail, one, (eta, tu, tv, tu, tv), unroll=True)
    kept = slice(8, 2 * ROWS + 8)
    wet, depth = wet[kept], depth[kept]
    push = [part[kept] for part in push]
    beside = turn(wet, -1, 1), turn(wet, 1, 1)

    def last(_, carry):
        eta, tu, tv, sum_u, sum_v = carry
        eta, tu, tv = substep_once(eta, tu, tv, wet, depth, push, *beside)
        return eta, tu, tv, sum_u + tu, sum_v + tv

    cells = lax.fori_loop(0, tail, last, tuple(part[kept] for part in cells), unroll=True)
    return tuple(jnp.concatenate([part[-8:], part, part[0:8]], axis=0) for part in cells)


def inside(cells):
    return cells[ROWS : 2 * ROWS, 0:LANES]


def lane_pair(odd, cells, even_at, odd_at):
    shape = odd.shape
    return jnp.where(
        odd,
        jnp.broadcast_to(cells[:, odd_at : odd_at + 1], shape),
        jnp.broadcast_to(cells[:, even_at : even_at + 1], shape),
    )


def store_kernel(*refs):
    count = (len(refs) - 1) // 2
    sem = refs[-1]
    copies = [
        pltpu.make_async_copy(src, dst, sem.at[i])
        for i, (src, dst) in enumerate(zip(refs[:count], refs[count:-1]))
    ]
    for copy in copies:
        copy.start()
    for copy in copies:
        copy.wait()


def kernel(
    vel_u, vel_v, buoy, surface, trans_u, trans_v, ocean, layers,
    out_u, out_v, out_b, out_eta, out_tu, out_tv,
    star_u, star_v,
    fx, lp, near_ext, ring_rows, rim_new, in_3d, in_2d, in_int,
    lane_w, mom_in, buoy_in, mom_out, buoy_out, mom_edge,
    x_send, y_send, x_recv, y_recv, gx_send, gy_send, gx_recv, gy_recv,
    fx_send, fy_send, fx_recv, fy_recv, in_sem, send_sem, recv_sem,
):
    loads = []
    for a, ref in enumerate((vel_u, vel_v, buoy)):
        loads.append(pltpu.make_async_copy(ref, in_3d.at[a], in_sem.at[a]))
    for a, ref in enumerate((surface, trans_u, trans_v)):
        loads.append(pltpu.make_async_copy(ref, in_2d.at[a], in_sem.at[3 + a]))
    for a, ref in enumerate((ocean, layers)):
        loads.append(pltpu.make_async_copy(ref, in_int.at[a], in_sem.at[6 + a]))
    for load in loads:
        load.start()
    gx, gy = lax.axis_index("gx"), lax.axis_index("gy")
    nx, ny = lax.axis_size("gx"), lax.axis_size("gy")

    def exists(d):
        ok = jnp.bool_(True)
        if d[0] == -1:
            ok = jnp.logical_and(ok, gx > 0)
        if d[0] == 1:
            ok = jnp.logical_and(ok, gx < nx - 1)
        if d[1] == -1:
            ok = jnp.logical_and(ok, gy > 0)
        if d[1] == 1:
            ok = jnp.logical_and(ok, gy < ny - 1)
        return ok

    here = {d: exists(d) for d in DIRS}
    barrier = pltpu.get_barrier_semaphore()
    total_near = jnp.int32(0)
    for d in DIRS:
        total_near = total_near + here[d].astype(jnp.int32)

        @pl.when(here[d])
        def _(d=d):
            pl.semaphore_signal(barrier, inc=1, device_id=(gx + d[0], gy + d[1]), device_id_type=MESH)

    for d in DIRS:
        @pl.when(jnp.logical_not(here[d]))
        def _(d=d):
            for p in range(STEPS):
                if d[1] == 0:
                    s = 0 if d[0] < 0 else 1
                    x_recv[p, s] = jnp.zeros(x_recv.shape[2:], F32)
                    gx_recv[p, s] = jnp.zeros(gx_recv.shape[2:], F32)
                    fx_recv[p, s] = jnp.zeros(fx_recv.shape[2:], F32)
                else:
                    s = SIDES.index(d)
                    y_recv[p, s] = jnp.zeros(y_recv.shape[2:], F32)
                    gy_recv[p, s] = jnp.zeros(gy_recv.shape[2:], F32)
                    fy_recv[p, s] = jnp.zeros(fy_recv.shape[2:], F32)

    def copies(phase, step):
        result = []
        for i, d in enumerate(DIRS):
            back = (-d[0], -d[1])
            if d[1] == 0:
                src_at, dst_at = (0 if d[0] < 0 else 1), (0 if back[0] < 0 else 1)
                if phase == FORCE:
                    src, dst = fx_send.at[step], fx_recv.at[step, dst_at]
                elif phase == PLANE:
                    src, dst = gx_send.at[step], gx_recv.at[step, dst_at]
                else:
                    first, end = {
                        (RIMS, 0): (FLAT_ROW, MOM_NEAR),
                        (CUBES, 0): (MOM_NEAR, BUOY_FAR),
                        (EARLY, 0): (BUOY_FAR, RIM),
                        (RIMS, 1): (FLAT_ROW, BUOY_NEAR),
                        (EARLY, 1): (BUOY_NEAR, CODE_PLANE),
                    }[phase, min(step, 1)]
                    rows = pl.ds(first, end - first)
                    src, dst = x_send.at[step, src_at, rows], x_recv.at[step, dst_at, rows]
            else:
                src_at, dst_at = (0 if d[1] < 0 else 1), SIDES.index(back)
                if phase == FORCE:
                    src, dst = fy_send.at[step], fy_recv.at[step, dst_at]
                elif phase == PLANE:
                    src, dst = gy_send.at[step, src_at], gy_recv.at[step, dst_at]
                elif phase == CUBES or phase == (RIMS if step else EARLY):
                    continue
                else:
                    src, dst = y_send.at[step, src_at], y_recv.at[step, dst_at]
                    if d[0] != 0:
                        rows = pl.ds(0, 8) if d[0] < 0 else pl.ds(8, 8)
                        src, dst = src.at[rows], dst.at[rows]
            at = phase * STEPS + step
            copy = functools.partial(
                pltpu.make_async_remote_copy, src_ref=src, dst_ref=dst,
                send_sem=send_sem.at[at, i], recv_sem=recv_sem.at[at, DIRS.index(back)],
                device_id=(gx + d[0], gy + d[1]), device_id_type=MESH,
            )
            result.append((d, copy))
        return result

    odd_row = lax.rem(gx, 2) == 1

    def start_rows(phase, step, two_hops):
        pending = [(d, copy) for d, copy in copies(phase, step) if d[0]]
        pending.sort(key=lambda item: (item[0][1] == 0) != two_hops)
        for d, copy in pending:
            @pl.when(jnp.logical_and(here[d], odd_row == (two_hops == (d[0] > 0))))
            def _(copy=copy):
                copy().start()

    def start_far(phase, step):
        start_rows(phase, step, True)
        for d, copy in copies(phase, step):
            if d[0] == 0:
                @pl.when(here[d])
                def _(copy=copy):
                    copy().start()

    def start_near(phase, step):
        start_rows(phase, step, False)

    def start(phase, step):
        start_far(phase, step)
        start_near(phase, step)

    def arrive(phase, step):
        by_dir = dict(copies(phase, step))
        for d in by_dir:
            @pl.when(here[d])
            def _(d=d):
                by_dir[(-d[0], -d[1])]().wait_recv()

    def sent(phase, step):
        for d, copy in copies(phase, step):
            @pl.when(here[d])
            def _(copy=copy):
                copy().wait_send()

    lane = lax.broadcasted_iota(jnp.int32, (ROWS, LANES), 1)
    pair = lane >> 1
    lane8 = lane[0:8]
    odd = (lane & 1) == 1
    rim_lanes = jnp.logical_or(lane < 16, lane >= LANES - 16)
    zero = jnp.zeros((ROWS, LANES), F32)

    def put_rows(step, near_at, far_at, cells):
        x_send[step, 0, pl.ds(near_at, 1)] = cells[0:1]
        x_send[step, 0, pl.ds(far_at, 1)] = cells[1:2]
        x_send[step, 1, pl.ds(near_at, 1)] = cells[ROWS - 1 : ROWS]
        x_send[step, 1, pl.ds(far_at, 1)] = cells[ROWS - 2 : ROWS - 1]

    def put_strip(j, cells, strips):
        to_left, to_right = strips
        rolled = turn(cells, 2 * j + 2, 1)
        to_right = jnp.where(pair == j, rolled, to_right)
        to_left = jnp.where(pair == j + 1, rolled, to_left)
        return to_left, to_right

    def put(step, j, near_at, far_at, cells, strips):
        put_rows(step, near_at, far_at, cells)
        return put_strip(j, cells, strips)

    def put_v(step, j, cells, strips):
        return put(step, j, MOM_NEAR + j, MOM_FAR + j, cells, strips)

    def put_b(step, k, cells, strips):
        j = MOVING + k
        return put(step, j, BUOY_NEAR + k, BUOY_FAR + k, cells, strips)

    def put_flat(step, a, cells, strips):
        return put(step, STACK + a, FLAT_ROW + 2 * a, FLAT_ROW + 2 * a + 1, cells, strips)

    def send_plane(step, flats):
        flat_left, flat_right = pack_flat(flats)
        gy_send[step, 0] = flat_left
        gy_send[step, 1] = flat_right
        for a, cells in enumerate(flats[0:3]):
            gx_send[step, ROWS * a : ROWS * (a + 1)] = cells
        start(PLANE, step)

    ring_rows[...] = jnp.zeros(ring_rows.shape, F32)
    for r, blocks in enumerate(lane_weights()):
        for c, block in enumerate(blocks):
            for at in (2 * r, 2 * r + 1):
                lane_w[LANES * at : LANES * (at + 1), LANES * c : LANES * (c + 1)] = block
    def put_parts(ref, at, rows, parts, col):
        for c, part in enumerate(parts):
            ref[pl.ds(at, rows), LANES * (col + c) : LANES * (col + c + 1)] = part

    def stage_own(ref, first, count, source):
        def one(i, carry):
            at = pl.multiple_of(ROWS * i, ROWS)
            put_parts(ref, at, ROWS, split(source[pl.ds(EXT * (first + i) + OWN, ROWS)]), 0)
            return carry

        lax.fori_loop(0, count, one, 0, unroll=True)

    def own_product(source, rows):
        return jnp.dot(
            source[0:rows, 0 : 2 * LANES], lane_w[0 : 2 * LANES, 0:LANES],
            preferred_element_type=F32,
        )

    def edge_product(source, rows):
        return jnp.dot(
            source[0:rows, 2 * LANES : 4 * LANES], lane_w[2 * LANES : 4 * LANES, 0:LANES],
            preferred_element_type=F32,
        )

    def stage_edge(ref, first, count, edge):
        def one(i, carry):
            at = pl.multiple_of(ROWS * i, ROWS)
            put_parts(ref, at, ROWS, pick(pair == first + i, edge), 2)
            return carry

        lax.fori_loop(0, count, one, 0, unroll=True)

    loads[6].wait()
    loads[7].wait()
    lay = in_int[1].astype(F32)
    code = jnp.where(in_int[0] > 0, lay, 0.0)
    strips = put_flat(0, 0, code, (zero, zero))
    for a in range(FIELDS):
        loads[a].wait()

        def pack(k, strips, a=a):
            cells = in_3d[a, k]
            fx[pl.ds(EXT * (a * LEVELS + k) + OWN, ROWS)] = cells
            if a < 2:
                return put_v(0, a * LEVELS + k, cells, strips)
            return put_b(0, k, cells, strips)

        strips = lax.fori_loop(0, LEVELS, pack, strips, unroll=True)
    flats = [code]
    for a in range(3):
        loads[3 + a].wait()
        flats.append(in_2d[a])
        strips = put_flat(0, 1 + a, in_2d[a], strips)
    strips = turn(strips[0], -2, 1), strips[1]
    y_send[0, 0] = strips[0]
    y_send[0, 1] = strips[1]
    pl.semaphore_wait(barrier, total_near)
    for side in range(2):
        x_send[0, side, pl.ds(CODE_PLANE, ROWS)] = code
    start_far(RIMS, 0)
    start_far(CUBES, 0)
    start_near(RIMS, 0)
    stage_own(mom_in, 0, MOVING, fx)
    mom_out[0 : MOVING * ROWS] = own_product(mom_in, MOVING * ROWS)
    start_near(CUBES, 0)
    start(EARLY, 0)
    stage_own(buoy_in, MOVING, LEVELS, fx)

    around = (ROWS + 8, LANES)
    lane24 = lax.broadcasted_iota(jnp.int32, around, 1)
    odd24 = (lane24 & 1) == 1
    level24 = ((lane24 >> 1) & (LEVELS - 1)).astype(F32)
    level_pair = level24[0:ROWS]
    moving24 = lane24 < 2 * MOVING
    is_u24 = lane24 < 2 * LEVELS
    upper = lax.broadcasted_iota(jnp.int32, (8, LANES), 0) < 4

    def cyclic(own, below, above):
        return jnp.concatenate([own, jnp.where(upper, below, above)], axis=0)

    def beside_columns(left24, right24, j):
        return jnp.where(
            lane24 < HALF, turn(right24, -2 * j, 1), turn(left24, 126 - 2 * j, 1)
        )

    def side24(cells):
        tile = cells[:, LANES : 2 * LANES]
        return cyclic(tile[ROWS : 2 * ROWS], tile[2 * ROWS : 2 * ROWS + 8], tile[8:ROWS])

    for step in range(STEPS):
        if step:
            flats = [inside(c) for c in substep(eta, flow_u, flow_v, wet, depth)]
            send_plane(step, flats)
        arrive(RIMS, step)
        if step:
            arrive(EARLY, step)
        left24 = cyclic(y_recv[step, 1], y_recv[step, 2, 0:8], y_recv[step, 0, 8:16])
        right24 = cyclic(y_recv[step, 4], y_recv[step, 5, 0:8], y_recv[step, 3, 8:16])
        near24 = jnp.where(odd24, left24, right24)
        far = jnp.where(odd, right24[0:ROWS], left24[0:ROWS])
        far = jnp.where(odd, turn(far, 1, 1), turn(far, -1, 1))
        inner = jnp.where(odd, turn(strips[0], 1, 1), turn(strips[1], -1, 1))

        if step == 0:
            code_near = lane_pair(odd24, near24, 2 * STACK, 2 * STACK + 1)
            code_far = lane_pair(odd, far, 2 * STACK, 2 * STACK + 1)
            code_inner = lane_pair(odd, code, LANES - 1, 0)
            act_near = level24 < code_near
            grids = []
            for a, own in enumerate(flats):
                near_at, far_at = FLAT_ROW + 2 * a, FLAT_ROW + 2 * a + 1
                ring_rows[a, 0:1] = x_recv[0, 1, pl.ds(near_at, 1)]
                ring_rows[a, 1:2] = x_recv[0, 1, pl.ds(far_at, 1)]
                ring_rows[a, 6:7] = x_recv[0, 0, pl.ds(far_at, 1)]
                ring_rows[a, 7:8] = x_recv[0, 0, pl.ds(near_at, 1)]
                main = jnp.concatenate([own, ring_rows[a]], axis=0)
                grids.append(jnp.concatenate(
                    [main, beside_columns(left24, right24, STACK + a)], axis=1
                ))
            code_side = grids[0][:, LANES : 2 * LANES]
            ahead = substep(
                *grids[1:], (grids[0] > 0.0).astype(F32), grids[0] / LEVELS
            )
            flats = [cells[0:ROWS, 0:LANES] for cells in ahead]
            stage_edge(mom_in, 0, MOVING, near24[0:ROWS])
            stage_edge(buoy_in, MOVING, LEVELS, near24[0:ROWS])
            send_plane(step, flats + [code])
        else:
            shift_side = [
                (SCALE * side24(total) - beside_columns(left24, right24, STACK + 1 + a))
                / jnp.maximum(code_side, 1.0)
                for a, total in enumerate((sum_u, sum_v))
            ]

            def couple_pairs(cells, near_code, rows, levels, even_at, odd_at, sources):
                parity = odd24[0:rows]
                shift = jnp.where(
                    is_u24[0:rows],
                    lane_pair(parity, sources[0][0:rows], even_at, odd_at),
                    lane_pair(parity, sources[1][0:rows], even_at, odd_at),
                )
                moved = jnp.where(levels < near_code, cells + shift, 0.0)
                return jnp.where(moving24[0:rows], moved, cells)

            near24 = couple_pairs(
                near24, code_near, ROWS + 8, level24, 0, LANES - 1, shift_side
            )
            far = couple_pairs(far, code_far, ROWS, level_pair, 1, LANES - 2, shift_side)
            inner = couple_pairs(
                inner, code_inner, ROWS, level_pair, LANES - 1, 0, (shift_u, shift_v)
            )
            level16 = lax.broadcasted_iota(jnp.int32, (LEVELS, LANES), 0).astype(F32)
            for side in range(2):
                for away in range(2):
                    at = (ROWS - 1 - away, 2 * ROWS + away)[side]
                    code_row = x_recv[0, side, pl.ds(FLAT_ROW + away, 1)]
                    for a, total in enumerate((sum_u, sum_v)):
                        column = x_recv[1, side, pl.ds(FLAT_ROW + 2 * (1 + a) + away, 1)]
                        shift = (
                            SCALE * total[at : at + 1, 0:LANES] - column
                        ) / jnp.maximum(code_row, 1.0)
                        at_row = MOVING * away + LEVELS * a
                        star = x_recv[1, side, pl.ds(MOM_NEAR + at_row, LEVELS)]
                        rim_new[side, pl.ds(at_row, LEVELS)] = jnp.where(
                            level16 < code_row, star + shift, 0.0
                        )

        near_ext[...] = near24
        near = near24[0:ROWS]
        lap_near = jnp.where(
            act_near,
            turn(near24, 1, 0) + turn(near24, -1, 0) - 4.0 * near24,
            0.0,
        )[0:ROWS] + jnp.where(act_near[0:ROWS], far + inner, 0.0)

        def rim_cells(side, first, count, at):
            if first == 0 and step:
                return rim_new[side, pl.ds(at - MOM_NEAR, count)]
            return x_recv[step, side, pl.ds(at, count)]

        def rim_rows(ref, first, count, near_at):
            row = lax.broadcasted_iota(jnp.int32, (count, LANES), 0)
            group = lax.broadcasted_iota(jnp.int32, (count, LANES), 1) >> 1
            for side in range(2):
                cells = rim_cells(side, first, count, near_at)
                at = ROWS * count + count * side
                corner = jnp.broadcast_to(
                    near_ext[pl.ds((ROWS + 7, ROWS)[side], 1)], (count, LANES)
                )
                put_parts(ref, at, count, split(cells), 0)
                put_parts(ref, at, count, pick(group == first + row, corner), 2)
                fx[pl.ds(EXT * first + (OWN - 1, OWN + ROWS)[side], count, stride=EXT)] = cells

        def rim_laps(ref, first, count, near_at, far_at):
            level_of = lax.broadcasted_iota(jnp.int32, (count, LANES), 0) & (LEVELS - 1)
            for side in range(2):
                cells = rim_cells(side, first, count, near_at)
                edge = EXT * first + (OWN, OWN + ROWS - 1)[side]
                beside = rim_cells(side, first, count, far_at) + fx[
                    pl.ds(edge, count, stride=EXT)
                ]
                lanes_sum = ref[pl.ds(ROWS * count + count * side, count), 0:LANES]
                code_row = x_recv[0, side, pl.ds(FLAT_ROW, 1)]
                lap = jnp.where(
                    level_of.astype(F32) < code_row, beside + lanes_sum - 4.0 * cells, 0.0
                )
                lp[pl.ds(EXT * first + (OWN - 1, OWN + ROWS)[side], count, stride=EXT)] = lap

        def laplace(j, source, lanes_sum):
            at = EXT * j + OWN
            return (
                source[pl.ds(at - 1, ROWS)] + source[pl.ds(at + 1, ROWS)]
                + lanes_sum - 4.0 * source[pl.ds(at, ROWS)]
            )

        def own_laps(ref, first, count):
            def one(i, carry):
                level_at = lax.convert_element_type(i & (LEVELS - 1), F32)
                at = pl.ds(pl.multiple_of(ROWS * i, ROWS), ROWS)
                lanes_sum = ref[at, 0:LANES]
                if first == 0:
                    lanes_sum = lanes_sum + mom_edge[at]
                lap = laplace(first + i, fx, lanes_sum)
                lp[pl.ds(EXT * (first + i) + OWN, ROWS)] = jnp.where(level_at < code, lap, 0.0)
                return carry

            lax.fori_loop(0, count, one, 0, unroll=True)

        def apply(source, rows, width):
            return jnp.dot(
                source[0:rows], lane_w[:, 0:width], preferred_element_type=F32
            )

        rows_uv, rows_b = MOVING * ROWS, LEVELS * ROWS
        if step:
            stage_edge(mom_in, 0, MOVING, near)
            stage_edge(buoy_in, MOVING, LEVELS, near)
        if step == 0:
            arrive(CUBES, step)
        rim_rows(mom_in, 0, MOVING, MOM_NEAR)
        mom_edge[...] = edge_product(mom_in, rows_uv)
        mom_out[pl.ds(rows_uv, 2 * MOVING)] = jnp.dot(
            mom_in[pl.ds(rows_uv, 2 * MOVING)], lane_w[:, 0:LANES], preferred_element_type=F32
        )
        rim_rows(buoy_in, MOVING, LEVELS, BUOY_NEAR)
        buoy_out[...] = apply(buoy_in, rows_b + 2 * LEVELS, 2 * LANES)
        rim_laps(mom_out, 0, MOVING, MOM_NEAR, MOM_FAR)
        own_laps(mom_out, 0, MOVING)
        stage_own(mom_in, 0, MOVING, lp)
        stage_edge(mom_in, 0, MOVING, lap_near)
        mom_out[0:rows_uv] = apply(mom_in, rows_uv, LANES)

        def buoyancy(k, carry):
            act = lax.convert_element_type(k, F32) < code
            at = EXT * (MOVING + k) + OWN
            rows = pl.ds(pl.multiple_of(ROWS * k, ROWS), ROWS)
            bih_b = laplace(MOVING + k, lp, buoy_out[rows, 0:LANES])
            u, v = fx[pl.ds(EXT * k + OWN, ROWS)], fx[pl.ds(EXT * (LEVELS + k) + OWN, ROWS)]
            b = fx[pl.ds(at, ROWS)]
            b_x = fx[pl.ds(at + 1, ROWS)] - fx[pl.ds(at - 1, ROWS)]
            b_y = buoy_out[rows, LANES : 2 * LANES]
            tend_b = -0.5 * (u * b_x + v * b_y) - 0.02 * bih_b
            new_b = jnp.where(act, b + 0.2 * tend_b, 0.0)
            if step == STEPS - 1:
                out_b[k] = new_b
            else:
                in_3d[2, k] = new_b
            return carry

        def level(k, carry):
            press_x, press_y, force_u, force_v, col_u, col_v = carry
            act = (lax.convert_element_type(k, F32) < code).astype(F32)
            rows = pl.ds(pl.multiple_of(ROWS * k, ROWS), ROWS)
            rows_v = pl.ds(pl.multiple_of(ROWS * (LEVELS + k), ROWS), ROWS)
            bih_u = laplace(k, lp, mom_out[rows])
            bih_v = laplace(LEVELS + k, lp, mom_out[rows_v])
            u, v = fx[pl.ds(EXT * k + OWN, ROWS)], fx[pl.ds(EXT * (LEVELS + k) + OWN, ROWS)]
            at = EXT * (MOVING + k) + OWN
            press_x = press_x + (fx[pl.ds(at + 1, ROWS)] - fx[pl.ds(at - 1, ROWS)])
            press_y = press_y + buoy_out[rows, LANES : 2 * LANES]
            tend_u = (-0.25 / LEVELS) * press_x + 0.1 * v - 0.02 * bih_u
            tend_v = (-0.25 / LEVELS) * press_y - 0.1 * u - 0.02 * bih_v
            su = act * (u + 0.2 * tend_u)
            sv = act * (v + 0.2 * tend_v)
            star_u[k] = su
            star_v[k] = sv
            if step < STEPS - 1:
                put_rows(step + 1, MOM_NEAR + k, MOM_FAR + k, su)
                put_rows(step + 1, MOM_NEAR + LEVELS + k, MOM_FAR + LEVELS + k, sv)
            return (
                press_x, press_y, force_u + act * tend_u, force_v + act * tend_v,
                col_u + su, col_v + sv,
            )

        _, _, force_u, force_v, col_u, col_v = lax.fori_loop(
            0, LEVELS, level, (zero,) * 6, unroll=True
        )
        force_u, force_v = force_u / LEVELS, force_v / LEVELS
        fx_send[step, 0:ROWS] = force_u
        fx_send[step, ROWS : 2 * ROWS] = force_v
        fy_send[step] = jnp.where(
            rim_lanes[0:8], force_u[0:8],
            jnp.where(
                lane8 < 48, turn(force_u[8:16], 32, 1),
                jnp.where(lane8 < 80, turn(force_v[0:8], 64, 1), turn(force_v[8:16], 96, 1)),
            ),
        )
        start(FORCE, step)
        if step < STEPS - 1:
            for a, cells in enumerate((col_u, col_v)):
                at = FLAT_ROW + 2 * (1 + a)
                put_rows(step + 1, at, at + 1, cells)
            start_far(RIMS, step + 1)
            def pack_star(k, strips):
                strips = put_strip(k, star_u[k], strips)
                return put_strip(LEVELS + k, star_v[k], strips)

            strips = lax.fori_loop(0, LEVELS, pack_star, (zero, zero), unroll=True)
            strips = put_strip(STACK + 1, col_u, strips)
            strips = put_strip(STACK + 2, col_v, strips)
        if step == 0:
            arrive(EARLY, step)
        rim_laps(buoy_out, MOVING, LEVELS, BUOY_NEAR, BUOY_FAR)
        own_laps(buoy_out, MOVING, LEVELS)
        stage_own(buoy_in, MOVING, LEVELS, lp)
        stage_edge(buoy_in, MOVING, LEVELS, lap_near)
        buoy_out[0:rows_b, 0:LANES] = apply(buoy_in, rows_b, LANES)
        lax.fori_loop(0, LEVELS, buoyancy, 0, unroll=True)
        if step < STEPS - 1:
            def pack_b(k, strips):
                cells = in_3d[2, k]
                fx[pl.ds(EXT * (MOVING + k) + OWN, ROWS)] = cells
                return put_b(step + 1, k, cells, strips)

            strips = lax.fori_loop(0, LEVELS, pack_b, strips, unroll=True)
            strips = turn(strips[0], -2, 1), strips[1]
            y_send[step + 1, 0] = strips[0]
            y_send[step + 1, 1] = strips[1]
            start_far(EARLY, step + 1)
            start_near(EARLY, step + 1)
            start_near(RIMS, step + 1)
            stage_own(buoy_in, MOVING, LEVELS, fx)
        arrive(PLANE, step)
        sides = [gy_recv[step, r] for r in range(6)]

        def plane(own, a):
            rows = slice(ROWS * a, ROWS * (a + 1))
            return wide(own, gx_recv[step, 0, rows], gx_recv[step, 1, rows], sides, a)

        if step == 0:
            rows = pl.ds(CODE_PLANE, ROWS)
            code_wide = wide(code, x_recv[0, 0, rows], x_recv[0, 1, rows], sides, 3)
            wet, depth = (code_wide > 0.0).astype(F32), code_wide / LEVELS
        state = [plane(cells, a) for a, cells in enumerate(flats)]
        arrive(FORCE, step)
        beside = [[], []]
        for r in range(3):
            strip = jnp.where((lane8 & 16) == 0, fy_recv[step, r + 3], fy_recv[step, r])
            for part in range(4):
                rolled = turn(strip, -32 * part, 1) if part else strip
                beside[part // 2].append(jnp.where(rim_lanes[0:8], rolled, 0.0))
        push = []
        for a, own in enumerate((force_u, force_v)):
            rows = slice(ROWS * a, ROWS * (a + 1))
            main = [fx_recv[step, 0, rows], own, fx_recv[step, 1, rows]]
            push.append(0.2 * jnp.concatenate(
                [jnp.concatenate(main, axis=0), jnp.concatenate(beside[a], axis=0)], axis=1
            ))
        eta, flow_u, flow_v, sum_u, sum_v = barotropic(state, push, wet, depth, 3 if step < STEPS - 1 else 4)
        shift_u = (SCALE * inside(sum_u) - col_u) / lay
        shift_v = (SCALE * inside(sum_v) - col_v) / lay

        def couple(k, carry):
            act = lax.convert_element_type(k, F32) < code
            new_u = jnp.where(act, star_u[k] + shift_u, 0.0)
            new_v = jnp.where(act, star_v[k] + shift_v, 0.0)
            if step == STEPS - 1:
                out_u[k] = new_u
                out_v[k] = new_v
            else:
                fx[pl.ds(EXT * k + OWN, ROWS)] = new_u
                fx[pl.ds(EXT * (LEVELS + k) + OWN, ROWS)] = new_v
            return carry

        lax.fori_loop(0, LEVELS, couple, 0, unroll=True)
        if step < STEPS - 1:
            stage_own(mom_in, 0, MOVING, fx)
            mom_out[0 : MOVING * ROWS] = own_product(mom_in, MOVING * ROWS)

    out_eta[...] = inside(eta)
    out_tu[...] = inside(flow_u)
    out_tv[...] = inside(flow_v)
    for step in range(STEPS):
        for phase in range(PHASES):
            if phase != CUBES or step == 0:
                sent(phase, step)


def per_device(velocity_u, velocity_v, buoyancy, surface, transport_u, transport_v, ocean, layers):
    cube = jax.ShapeDtypeStruct(velocity_u.shape, F32)
    flat = jax.ShapeDtypeStruct(surface.shape, F32)
    hbm = pl.BlockSpec(memory_space=pltpu.HBM)
    vmem = pl.BlockSpec(memory_space=pltpu.VMEM)
    outs = (cube, cube, cube, flat, flat, flat)
    args = [
        pltpu.with_memory_space_constraint(x, pltpu.HBM)
        for x in (velocity_u, velocity_v, buoyancy, surface, transport_u, transport_v, ocean, layers)
    ]
    block = (LEVELS, ROWS, LANES)
    middle = pl.pallas_call(
        kernel,
        out_shape=outs,
        in_specs=[hbm] * 8,
        out_specs=(vmem,) * 6,
        scratch_shapes=[
            pltpu.VMEM(block, F32),
            pltpu.VMEM(block, F32),
            pltpu.VMEM((STACK * EXT, LANES), F32),
            pltpu.VMEM((STACK * EXT, LANES), F32),
            pltpu.VMEM((ROWS + 8, LANES), F32),
            pltpu.VMEM((4, 8, LANES), F32),
            pltpu.VMEM((2, 2 * MOVING, LANES), F32),
            pltpu.VMEM((FIELDS,) + block, F32),
            pltpu.VMEM((3, ROWS, LANES), F32),
            pltpu.VMEM((2, ROWS, LANES), jnp.int32),
            pltpu.VMEM((4 * LANES, 2 * LANES), BF16),
            pltpu.VMEM((MOVING * (ROWS + 2), 4 * LANES), BF16),
            pltpu.VMEM((LEVELS * (ROWS + 2), 4 * LANES), BF16),
            pltpu.VMEM((MOVING * (ROWS + 2), LANES), F32),
            pltpu.VMEM((LEVELS * (ROWS + 2), 2 * LANES), F32),
            pltpu.VMEM((MOVING * ROWS, LANES), F32),
            pltpu.VMEM((STEPS, 2, RIM, LANES), F32),
            pltpu.VMEM((STEPS, 2, ROWS, LANES), F32),
            pltpu.VMEM((STEPS, 2, RIM, LANES), F32),
            pltpu.VMEM((STEPS, 6, ROWS, LANES), F32),
            pltpu.VMEM((STEPS, 3 * ROWS, LANES), F32),
            pltpu.VMEM((STEPS, 2, 8, LANES), F32),
            pltpu.VMEM((STEPS, 2, 3 * ROWS, LANES), F32),
            pltpu.VMEM((STEPS, 6, 8, LANES), F32),
            pltpu.VMEM((STEPS, 2 * ROWS, LANES), F32),
            pltpu.VMEM((STEPS, 8, LANES), F32),
            pltpu.VMEM((STEPS, 2, 2 * ROWS, LANES), F32),
            pltpu.VMEM((STEPS, 6, 8, LANES), F32),
            pltpu.SemaphoreType.DMA((8,)),
            pltpu.SemaphoreType.DMA((PHASES * STEPS, 8)),
            pltpu.SemaphoreType.DMA((PHASES * STEPS, 8)),
        ],
        compiler_params=pltpu.CompilerParams(
            collective_id=0, has_side_effects=True, vmem_limit_bytes=16 * 2**20
        ),
    )(*args)
    return tuple(
        pl.pallas_call(
            store_kernel,
            out_shape=outs,
            in_specs=[vmem] * 6,
            out_specs=(hbm,) * 6,
            scratch_shapes=[pltpu.SemaphoreType.DMA((6,))],
            compiler_params=pltpu.CompilerParams(vmem_limit_bytes=16 * 2**20),
        )(*middle)
    )


def solution(mesh):
    cube, flat = P(None, "gx", "gy"), P("gx", "gy")
    return jax.shard_map(
        per_device,
        mesh=mesh,
        in_specs=(cube, cube, cube, flat, flat, flat, flat, flat),
        out_specs=(cube, cube, cube, flat, flat, flat),
        check_vma=False,
    )
```

```python
import functools

import jax
import jax.numpy as jnp
from jax import lax
from jax.experimental import pallas as pl
from jax.experimental.pallas import tpu as pltpu
from jax.sharding import PartitionSpec as P

SUB = 8
STEPS = 2
LANES = 128
ROWS = 16
LEVELS = 16
FIELDS = 3
STACK = FIELDS * LEVELS
MESH = pl.DeviceIdType.MESH
F32 = jnp.float32
BF16 = jnp.bfloat16

DIRS = [(-1, 0), (1, 0), (0, -1), (0, 1), (-1, -1), (-1, 1), (1, -1), (1, 1)]
SIDES = [(-1, -1), (0, -1), (1, -1), (-1, 1), (0, 1), (1, 1)]
MOVING = 2 * LEVELS
FLAT_ROW = 0
MOM_NEAR = FLAT_ROW + 8
MOM_FAR = MOM_NEAR + MOVING
BUOY_NEAR = MOM_FAR + MOVING
BUOY_FAR = BUOY_NEAR + LEVELS
CODE_PLANE = BUOY_FAR + LEVELS
RIM = CODE_PLANE + ROWS
HALF = LANES // 2


RIMS, FORCE, PLANE, EARLY, CUBES = 0, 1, 2, 3, 4
PHASES = 5
EXT = 32
OWN = 8
SCALE = LEVELS / SUB


def turn(x, shift, axis):
    return pltpu.roll(x, shift % x.shape[axis] if isinstance(shift, int) else shift, axis)


def fold(cells):
    low = lax.broadcasted_iota(jnp.int32, (8, LANES), 1) < HALF
    return jnp.where(low, cells[0:8], turn(cells[8:16], HALF, 1))


def unfold(cells):
    return jnp.concatenate([cells, turn(cells, HALF, 1)], axis=0)


def split(x):
    high = x.astype(BF16)
    return high, (x - high.astype(F32)).astype(BF16)


def pick(mask, x):
    return tuple(jnp.where(mask, part.astype(F32), 0.0).astype(BF16) for part in split(x))


def lane_weights():
    src = lax.broadcasted_iota(jnp.int32, (LANES, LANES), 0)
    dst = lax.broadcasted_iota(jnp.int32, (LANES, LANES), 1)
    ahead, behind = (src == dst + 1).astype(F32), (src == dst - 1).astype(F32)
    odd = (src & 1) == 1
    first = jnp.logical_and(odd, dst == 0).astype(F32)
    last = jnp.logical_and(jnp.logical_not(odd), dst == LANES - 1).astype(F32)
    return [
        [(ahead + behind).astype(BF16), (ahead - behind).astype(BF16)],
        [(last + first).astype(BF16), (last - first).astype(BF16)],
    ]


def pack_flat(arrays):
    lane = lax.broadcasted_iota(jnp.int32, (ROWS, LANES), 1)
    group = lane[0:8] >> 4
    to_left = to_right = jnp.zeros((8, LANES), F32)
    for a, cells in enumerate(arrays):
        for half in range(2):
            part, at = cells[8 * half : 8 * half + 8], a + 4 * half
            to_right = jnp.where(group == at, turn(part, 16 * at + 16, 1), to_right)
            to_left = jnp.where(group == at, turn(part, 16 * at, 1), to_left)
    return to_left, to_right


def wide(own, up, down, sides, a):
    lane = lax.broadcasted_iota(jnp.int32, (8, LANES), 1)
    blocks = []
    for r in range(3):
        for half in range(2):
            at = a + 4 * half
            left = turn(sides[r], 112 - 16 * at, 1)
            right = turn(sides[r + 3], -16 * at, 1)
            blocks.append(jnp.where(lane < 16, right, jnp.where(lane >= 112, left, 0.0)))
    main = jnp.concatenate([up, own, down], axis=0)
    return jnp.concatenate([main, jnp.concatenate(blocks, axis=0)], axis=1)


def substep(eta, tu, tv, wet, depth, push=None):
    div = (turn(tu, -1, 0) - turn(tu, 1, 0)) + (turn(tv, -1, 1) - turn(tv, 1, 1))
    eta = wet * (eta - 0.125 * div)
    thick = 0.125 * (depth + eta)
    new_u = 0.98 * tu - thick * (turn(eta, -1, 0) - turn(eta, 1, 0)) + 0.05 * tv
    new_v = 0.98 * tv - thick * (turn(eta, -1, 1) - turn(eta, 1, 1)) - 0.05 * tu
    if push is not None:
        new_u, new_v = new_u + push[0], new_v + push[1]
    return eta, wet * new_u, wet * new_v


def substep_once(eta, tu, tv, wet, depth, push, wet_ahead, wet_behind):
    mid = eta - 0.125 * (turn(tu, -1, 0) - turn(tu, 1, 0))
    ahead = wet_ahead * (turn(mid, -1, 1) - 0.125 * (turn(tv, -2, 1) - tv))
    behind = wet_behind * (turn(mid, 1, 1) - 0.125 * (tv - turn(tv, 2, 1)))
    eta = wet * (mid - 0.125 * (turn(tv, -1, 1) - turn(tv, 1, 1)))
    thick = 0.125 * (depth + eta)
    new_u = 0.98 * tu - thick * (turn(eta, -1, 0) - turn(eta, 1, 0)) + 0.05 * tv + push[0]
    new_v = 0.98 * tv - thick * (ahead - behind) - 0.05 * tu + push[1]
    return eta, wet * new_u, wet * new_v


def barotropic(state, push, wet, depth, tail):
    eta, tu, tv = state
    tu, tv = tu + wet * push[0], tv + wet * push[1]

    def one(_, carry):
        eta, tu, tv, sum_u, sum_v = carry
        eta, tu, tv = substep(eta, tu, tv, wet, depth, push)
        return eta, tu, tv, sum_u + tu, sum_v + tv

    cells = lax.fori_loop(0, SUB - 1 - tail, one, (eta, tu, tv, tu, tv), unroll=True)
    kept = slice(8, 2 * ROWS + 8)
    wet, depth = wet[kept], depth[kept]
    push = [part[kept] for part in push]
    beside = turn(wet, -1, 1), turn(wet, 1, 1)

    def last(_, carry):
        eta, tu, tv, sum_u, sum_v = carry
        eta, tu, tv = substep_once(eta, tu, tv, wet, depth, push, *beside)
        return eta, tu, tv, sum_u + tu, sum_v + tv

    cells = lax.fori_loop(0, tail, last, tuple(part[kept] for part in cells), unroll=True)
    return tuple(jnp.concatenate([part[-8:], part, part[0:8]], axis=0) for part in cells)


def inside(cells):
    return cells[ROWS : 2 * ROWS, 0:LANES]


def lane_pair(odd, cells, even_at, odd_at):
    shape = odd.shape
    return jnp.where(
        odd,
        jnp.broadcast_to(cells[:, odd_at : odd_at + 1], shape),
        jnp.broadcast_to(cells[:, even_at : even_at + 1], shape),
    )


def store_kernel(*refs):
    count = (len(refs) - 1) // 2
    sem = refs[-1]
    copies = [
        pltpu.make_async_copy(src, dst, sem.at[i])
        for i, (src, dst) in enumerate(zip(refs[:count], refs[count:-1]))
    ]
    for copy in copies:
        copy.start()
    for copy in copies:
        copy.wait()


def kernel(
    vel_u, vel_v, buoy, surface, trans_u, trans_v, ocean, layers,
    out_u, out_v, out_b, out_eta, out_tu, out_tv,
    star_u, star_v,
    fx, lp, near_ext, ring_rows, rim_new, in_3d, in_2d, in_int,
    lane_w, mom_in, buoy_in, mom_out, buoy_out, mom_edge,
    x_send, y_send, x_recv, y_recv, gx_send, gy_send, gx_recv, gy_recv,
    fx_send, fy_send, fx_recv, fy_recv, in_sem, send_sem, recv_sem,
):
    loads = []
    for a, ref in enumerate((vel_u, vel_v, buoy)):
        loads.append(pltpu.make_async_copy(ref, in_3d.at[a], in_sem.at[a]))
    for a, ref in enumerate((surface, trans_u, trans_v)):
        loads.append(pltpu.make_async_copy(ref, in_2d.at[a], in_sem.at[3 + a]))
    for a, ref in enumerate((ocean, layers)):
        loads.append(pltpu.make_async_copy(ref, in_int.at[a], in_sem.at[6 + a]))
    for load in loads:
        load.start()
    gx, gy = lax.axis_index("gx"), lax.axis_index("gy")
    nx, ny = lax.axis_size("gx"), lax.axis_size("gy")

    def exists(d):
        ok = jnp.bool_(True)
        if d[0] == -1:
            ok = jnp.logical_and(ok, gx > 0)
        if d[0] == 1:
            ok = jnp.logical_and(ok, gx < nx - 1)
        if d[1] == -1:
            ok = jnp.logical_and(ok, gy > 0)
        if d[1] == 1:
            ok = jnp.logical_and(ok, gy < ny - 1)
        return ok

    here = {d: exists(d) for d in DIRS}
    barrier = pltpu.get_barrier_semaphore()
    total_near = jnp.int32(0)
    for d in DIRS[::-1]:
        total_near = total_near + here[d].astype(jnp.int32)

        @pl.when(here[d])
        def _(d=d):
            pl.semaphore_signal(barrier, inc=1, device_id=(gx + d[0], gy + d[1]), device_id_type=MESH)

    for d in DIRS:
        @pl.when(jnp.logical_not(here[d]))
        def _(d=d):
            for p in range(STEPS):
                if d[1] == 0:
                    s = 0 if d[0] < 0 else 1
                    x_recv[p, s] = jnp.zeros(x_recv.shape[2:], F32)
                    gx_recv[p, s] = jnp.zeros(gx_recv.shape[2:], F32)
                    fx_recv[p, s] = jnp.zeros(fx_recv.shape[2:], F32)
                else:
                    s = SIDES.index(d)
                    y_recv[p, s] = jnp.zeros(y_recv.shape[2:], F32)
                    gy_recv[p, s] = jnp.zeros(gy_recv.shape[2:], F32)
                    fy_recv[p, s] = jnp.zeros(fy_recv.shape[2:], F32)

    def copies(phase, step):
        result = []
        for i, d in enumerate(DIRS):
            back = (-d[0], -d[1])
            if d[1] == 0:
                src_at, dst_at = (0 if d[0] < 0 else 1), (0 if back[0] < 0 else 1)
                if phase == FORCE:
                    src, dst = fx_send.at[step], fx_recv.at[step, dst_at]
                elif phase == PLANE:
                    src, dst = gx_send.at[step], gx_recv.at[step, dst_at]
                else:
                    first, end = {
                        (RIMS, 0): (FLAT_ROW, MOM_NEAR),
                        (CUBES, 0): (MOM_NEAR, BUOY_FAR),
                        (EARLY, 0): (BUOY_FAR, RIM),
                        (RIMS, 1): (FLAT_ROW, BUOY_NEAR),
                        (EARLY, 1): (BUOY_NEAR, CODE_PLANE),
                    }[phase, min(step, 1)]
                    rows = pl.ds(first, end - first)
                    src, dst = x_send.at[step, src_at, rows], x_recv.at[step, dst_at, rows]
            else:
                src_at, dst_at = (0 if d[1] < 0 else 1), SIDES.index(back)
                if phase == FORCE:
                    src, dst = fy_send.at[step], fy_recv.at[step, dst_at]
                elif phase == PLANE:
                    src, dst = gy_send.at[step, src_at], gy_recv.at[step, dst_at]
                elif phase == CUBES or phase == (RIMS if step else EARLY):
                    continue
                else:
                    src, dst = y_send.at[step, src_at], y_recv.at[step, dst_at]
                    if d[0] != 0:
                        rows = pl.ds(0, 8) if d[0] < 0 else pl.ds(8, 8)
                        src, dst = src.at[rows], dst.at[rows]
            at = phase * STEPS + step
            copy = functools.partial(
                pltpu.make_async_remote_copy, src_ref=src, dst_ref=dst,
                send_sem=send_sem.at[at, i], recv_sem=recv_sem.at[at, DIRS.index(back)],
                device_id=(gx + d[0], gy + d[1]), device_id_type=MESH,
            )
            result.append((d, copy))
        return result

    odd_row = lax.rem(gx, 2) == 1

    def start_rows(phase, step, two_hops):
        pending = [(d, copy) for d, copy in copies(phase, step) if d[0]]
        pending.sort(key=lambda item: (item[0][1] == 0) != two_hops)
        for d, copy in pending:
            @pl.when(jnp.logical_and(here[d], odd_row == (two_hops == (d[0] > 0))))
            def _(copy=copy):
                copy().start()

    def start_far(phase, step):
        start_rows(phase, step, True)
        for d, copy in copies(phase, step):
            if d[0] == 0:
                @pl.when(here[d])
                def _(copy=copy):
                    copy().start()

    def start_near(phase, step):
        start_rows(phase, step, False)

    def start(phase, step):
        start_far(phase, step)
        start_near(phase, step)

    def arrive(phase, step):
        by_dir = dict(copies(phase, step))
        for d in by_dir:
            @pl.when(here[d])
            def _(d=d):
                by_dir[(-d[0], -d[1])]().wait_recv()

    def sent(phase, step):
        for d, copy in copies(phase, step):
            @pl.when(here[d])
            def _(copy=copy):
                copy().wait_send()

    lane = lax.broadcasted_iota(jnp.int32, (ROWS, LANES), 1)
    pair = lane >> 1
    lane8 = lane[0:8]
    odd = (lane & 1) == 1
    rim_lanes = jnp.logical_or(lane < 16, lane >= LANES - 16)
    zero = jnp.zeros((ROWS, LANES), F32)

    def put_rows(step, near_at, far_at, cells):
        x_send[step, 0, pl.ds(near_at, 1)] = cells[0:1]
        x_send[step, 0, pl.ds(far_at, 1)] = cells[1:2]
        x_send[step, 1, pl.ds(near_at, 1)] = cells[ROWS - 1 : ROWS]
        x_send[step, 1, pl.ds(far_at, 1)] = cells[ROWS - 2 : ROWS - 1]

    def put_strip(j, cells, strips):
        to_left, to_right = strips
        rolled = turn(cells, 2 * j + 2, 1)
        to_right = jnp.where(pair == j, rolled, to_right)
        to_left = jnp.where(pair == j + 1, rolled, to_left)
        return to_left, to_right

    def put(step, j, near_at, far_at, cells, strips):
        put_rows(step, near_at, far_at, cells)
        return put_strip(j, cells, strips)

    def put_v(step, j, cells, strips):
        return put(step, j, MOM_NEAR + j, MOM_FAR + j, cells, strips)

    def put_b(step, k, cells, strips):
        j = MOVING + k
        return put(step, j, BUOY_NEAR + k, BUOY_FAR + k, cells, strips)

    def put_flat(step, a, cells, strips):
        return put(step, STACK + a, FLAT_ROW + 2 * a, FLAT_ROW + 2 * a + 1, cells, strips)

    def send_plane(step, flats):
        flat_left, flat_right = pack_flat(flats)
        gy_send[step, 0] = flat_left
        gy_send[step, 1] = flat_right
        for a, cells in enumerate(flats[0:3]):
            gx_send[step, ROWS * a : ROWS * (a + 1)] = cells
        start(PLANE, step)

    ring_rows[...] = jnp.zeros(ring_rows.shape, F32)
    for r, blocks in enumerate(lane_weights()):
        for c, block in enumerate(blocks):
            for at in (2 * r, 2 * r + 1):
                lane_w[LANES * at : LANES * (at + 1), LANES * c : LANES * (c + 1)] = block
    def put_parts(ref, at, rows, parts, col):
        for c, part in enumerate(parts):
            ref[pl.ds(at, rows), LANES * (col + c) : LANES * (col + c + 1)] = part

    def stage_own(ref, first, count, source):
        def one(i, carry):
            at = pl.multiple_of(ROWS * i, ROWS)
            put_parts(ref, at, ROWS, split(source[pl.ds(EXT * (first + i) + OWN, ROWS)]), 0)
            return carry

        lax.fori_loop(0, count, one, 0, unroll=True)

    def own_product(source, rows):
        return jnp.dot(
            source[0:rows, 0 : 2 * LANES], lane_w[0 : 2 * LANES, 0:LANES],
            preferred_element_type=F32,
        )

    def edge_product(source, rows):
        return jnp.dot(
            source[0:rows, 2 * LANES : 4 * LANES], lane_w[2 * LANES : 4 * LANES, 0:LANES],
            preferred_element_type=F32,
        )

    def stage_edge(ref, first, count, edge):
        def one(i, carry):
            at = pl.multiple_of(ROWS * i, ROWS)
            put_parts(ref, at, ROWS, pick(pair == first + i, edge), 2)
            return carry

        lax.fori_loop(0, count, one, 0, unroll=True)

    loads[6].wait()
    loads[7].wait()
    lay = in_int[1].astype(F32)
    code = jnp.where(in_int[0] > 0, lay, 0.0)
    strips = put_flat(0, 0, code, (zero, zero))
    for a in range(FIELDS):
        loads[a].wait()

        def pack(k, strips, a=a):
            cells = in_3d[a, k]
            fx[pl.ds(EXT * (a * LEVELS + k) + OWN, ROWS)] = cells
            if a < 2:
                return put_v(0, a * LEVELS + k, cells, strips)
            return put_b(0, k, cells, strips)

        strips = lax.fori_loop(0, LEVELS, pack, strips, unroll=True)
    flats = [code]
    for a in range(3):
        loads[3 + a].wait()
        flats.append(in_2d[a])
        strips = put_flat(0, 1 + a, in_2d[a], strips)
    strips = turn(strips[0], -2, 1), strips[1]
    y_send[0, 0] = strips[0]
    y_send[0, 1] = strips[1]
    pl.semaphore_wait(barrier, total_near)
    for side in range(2):
        x_send[0, side, pl.ds(CODE_PLANE, ROWS)] = code
    start_far(RIMS, 0)
    start_far(CUBES, 0)
    start_near(RIMS, 0)
    stage_own(mom_in, 0, MOVING, fx)
    mom_out[0 : MOVING * ROWS] = own_product(mom_in, MOVING * ROWS)
    start_near(CUBES, 0)
    start(EARLY, 0)
    stage_own(buoy_in, MOVING, LEVELS, fx)

    around = (ROWS + 8, LANES)
    lane24 = lax.broadcasted_iota(jnp.int32, around, 1)
    odd24 = (lane24 & 1) == 1
    level24 = ((lane24 >> 1) & (LEVELS - 1)).astype(F32)
    level_pair = level24[0:ROWS]
    moving24 = lane24 < 2 * MOVING
    is_u24 = lane24 < 2 * LEVELS
    upper = lax.broadcasted_iota(jnp.int32, (8, LANES), 0) < 4

    def cyclic(own, below, above):
        return jnp.concatenate([own, jnp.where(upper, below, above)], axis=0)

    def beside_columns(left24, right24, j):
        return jnp.where(
            lane24 < HALF, turn(right24, -2 * j, 1), turn(left24, 126 - 2 * j, 1)
        )

    def side24(cells):
        tile = cells[:, LANES : 2 * LANES]
        return cyclic(tile[ROWS : 2 * ROWS], tile[2 * ROWS : 2 * ROWS + 8], tile[8:ROWS])

    for step in range(STEPS):
        if step:
            flats = [inside(c) for c in substep(eta, flow_u, flow_v, wet, depth)]
            send_plane(step, flats)
        arrive(RIMS, step)
        if step:
            arrive(EARLY, step)
        left24 = cyclic(y_recv[step, 1], y_recv[step, 2, 0:8], y_recv[step, 0, 8:16])
        right24 = cyclic(y_recv[step, 4], y_recv[step, 5, 0:8], y_recv[step, 3, 8:16])
        near24 = jnp.where(odd24, left24, right24)
        far = jnp.where(odd, right24[0:ROWS], left24[0:ROWS])
        far = jnp.where(odd, turn(far, 1, 1), turn(far, -1, 1))
        inner = jnp.where(odd, turn(strips[0], 1, 1), turn(strips[1], -1, 1))

        if step == 0:
            code_near = lane_pair(odd24, near24, 2 * STACK, 2 * STACK + 1)
            code_far = lane_pair(odd, far, 2 * STACK, 2 * STACK + 1)
            code_inner = lane_pair(odd, code, LANES - 1, 0)
            act_near = level24 < code_near
            grids = []
            for a, own in enumerate(flats):
                near_at, far_at = FLAT_ROW + 2 * a, FLAT_ROW + 2 * a + 1
                ring_rows[a, 0:1] = x_recv[0, 1, pl.ds(near_at, 1)]
                ring_rows[a, 1:2] = x_recv[0, 1, pl.ds(far_at, 1)]
                ring_rows[a, 6:7] = x_recv[0, 0, pl.ds(far_at, 1)]
                ring_rows[a, 7:8] = x_recv[0, 0, pl.ds(near_at, 1)]
                main = jnp.concatenate([own, ring_rows[a]], axis=0)
                grids.append(jnp.concatenate(
                    [main, beside_columns(left24, right24, STACK + a)], axis=1
                ))
            code_side = grids[0][:, LANES : 2 * LANES]
            ahead = substep(
                *grids[1:], (grids[0] > 0.0).astype(F32), grids[0] / LEVELS
            )
            flats = [cells[0:ROWS, 0:LANES] for cells in ahead]
            stage_edge(mom_in, 0, MOVING, near24[0:ROWS])
            stage_edge(buoy_in, MOVING, LEVELS, near24[0:ROWS])
            send_plane(step, flats + [code])
        else:
            shift_side = [
                (SCALE * side24(total) - beside_columns(left24, right24, STACK + 1 + a))
                / jnp.maximum(code_side, 1.0)
                for a, total in enumerate((sum_u, sum_v))
            ]

            def couple_pairs(cells, near_code, rows, levels, even_at, odd_at, sources):
                parity = odd24[0:rows]
                shift = jnp.where(
                    is_u24[0:rows],
                    lane_pair(parity, sources[0][0:rows], even_at, odd_at),
                    lane_pair(parity, sources[1][0:rows], even_at, odd_at),
                )
                moved = jnp.where(levels < near_code, cells + shift, 0.0)
                return jnp.where(moving24[0:rows], moved, cells)

            near24 = couple_pairs(
                near24, code_near, ROWS + 8, level24, 0, LANES - 1, shift_side
            )
            far = couple_pairs(far, code_far, ROWS, level_pair, 1, LANES - 2, shift_side)
            inner = couple_pairs(
                inner, code_inner, ROWS, level_pair, LANES - 1, 0, (shift_u, shift_v)
            )
            level16 = lax.broadcasted_iota(jnp.int32, (LEVELS, LANES), 0).astype(F32)
            for side in range(2):
                for away in range(2):
                    at = (ROWS - 1 - away, 2 * ROWS + away)[side]
                    code_row = x_recv[0, side, pl.ds(FLAT_ROW + away, 1)]
                    for a, total in enumerate((sum_u, sum_v)):
                        column = x_recv[1, side, pl.ds(FLAT_ROW + 2 * (1 + a) + away, 1)]
                        shift = (
                            SCALE * total[at : at + 1, 0:LANES] - column
                        ) / jnp.maximum(code_row, 1.0)
                        at_row = MOVING * away + LEVELS * a
                        star = x_recv[1, side, pl.ds(MOM_NEAR + at_row, LEVELS)]
                        rim_new[side, pl.ds(at_row, LEVELS)] = jnp.where(
                            level16 < code_row, star + shift, 0.0
                        )

        near_ext[...] = near24
        near = near24[0:ROWS]
        lap_near = jnp.where(
            act_near,
            turn(near24, 1, 0) + turn(near24, -1, 0) - 4.0 * near24,
            0.0,
        )[0:ROWS] + jnp.where(act_near[0:ROWS], far + inner, 0.0)

        def rim_cells(side, first, count, at):
            if first == 0 and step:
                return rim_new[side, pl.ds(at - MOM_NEAR, count)]
            return x_recv[step, side, pl.ds(at, count)]

        def rim_rows(ref, first, count, near_at):
            row = lax.broadcasted_iota(jnp.int32, (count, LANES), 0)
            group = lax.broadcasted_iota(jnp.int32, (count, LANES), 1) >> 1
            for side in range(2):
                cells = rim_cells(side, first, count, near_at)
                at = ROWS * count + count * side
                corner = jnp.broadcast_to(
                    near_ext[pl.ds((ROWS + 7, ROWS)[side], 1)], (count, LANES)
                )
                put_parts(ref, at, count, split(cells), 0)
                put_parts(ref, at, count, pick(group == first + row, corner), 2)
                fx[pl.ds(EXT * first + (OWN - 1, OWN + ROWS)[side], count, stride=EXT)] = cells

        def rim_laps(ref, first, count, near_at, far_at):
            level_of = lax.broadcasted_iota(jnp.int32, (count, LANES), 0) & (LEVELS - 1)
            for side in range(2):
                cells = rim_cells(side, first, count, near_at)
                edge = EXT * first + (OWN, OWN + ROWS - 1)[side]
                beside = rim_cells(side, first, count, far_at) + fx[
                    pl.ds(edge, count, stride=EXT)
                ]
                lanes_sum = ref[pl.ds(ROWS * count + count * side, count), 0:LANES]
                code_row = x_recv[0, side, pl.ds(FLAT_ROW, 1)]
                lap = jnp.where(
                    level_of.astype(F32) < code_row, beside + lanes_sum - 4.0 * cells, 0.0
                )
                lp[pl.ds(EXT * first + (OWN - 1, OWN + ROWS)[side], count, stride=EXT)] = lap

        def laplace(j, source, lanes_sum):
            at = EXT * j + OWN
            return (
                source[pl.ds(at - 1, ROWS)] + source[pl.ds(at + 1, ROWS)]
                + lanes_sum - 4.0 * source[pl.ds(at, ROWS)]
            )

        def own_laps(ref, first, count):
            def one(i, carry):
                level_at = lax.convert_element_type(i & (LEVELS - 1), F32)
                at = pl.ds(pl.multiple_of(ROWS * i, ROWS), ROWS)
                lanes_sum = ref[at, 0:LANES]
                if first == 0:
                    lanes_sum = lanes_sum + mom_edge[at]
                lap = laplace(first + i, fx, lanes_sum)
                lp[pl.ds(EXT * (first + i) + OWN, ROWS)] = jnp.where(level_at < code, lap, 0.0)
                return carry

            lax.fori_loop(0, count, one, 0, unroll=True)

        def apply(source, rows, width):
            return jnp.dot(
                source[0:rows], lane_w[:, 0:width], preferred_element_type=F32
            )

        rows_uv, rows_b = MOVING * ROWS, LEVELS * ROWS
        if step:
            stage_edge(mom_in, 0, MOVING, near)
            stage_edge(buoy_in, MOVING, LEVELS, near)
        if step == 0:
            arrive(CUBES, step)
        rim_rows(mom_in, 0, MOVING, MOM_NEAR)
        mom_edge[...] = edge_product(mom_in, rows_uv)
        mom_out[pl.ds(rows_uv, 2 * MOVING)] = jnp.dot(
            mom_in[pl.ds(rows_uv, 2 * MOVING)], lane_w[:, 0:LANES], preferred_element_type=F32
        )
        rim_rows(buoy_in, MOVING, LEVELS, BUOY_NEAR)
        buoy_out[...] = apply(buoy_in, rows_b + 2 * LEVELS, 2 * LANES)
        rim_laps(mom_out, 0, MOVING, MOM_NEAR, MOM_FAR)
        own_laps(mom_out, 0, MOVING)
        stage_own(mom_in, 0, MOVING, lp)
        stage_edge(mom_in, 0, MOVING, lap_near)
        mom_out[0:rows_uv] = apply(mom_in, rows_uv, LANES)

        def buoyancy(k, carry):
            act = lax.convert_element_type(k, F32) < code
            at = EXT * (MOVING + k) + OWN
            rows = pl.ds(pl.multiple_of(ROWS * k, ROWS), ROWS)
            bih_b = laplace(MOVING + k, lp, buoy_out[rows, 0:LANES])
            u, v = fx[pl.ds(EXT * k + OWN, ROWS)], fx[pl.ds(EXT * (LEVELS + k) + OWN, ROWS)]
            b = fx[pl.ds(at, ROWS)]
            b_x = fx[pl.ds(at + 1, ROWS)] - fx[pl.ds(at - 1, ROWS)]
            b_y = buoy_out[rows, LANES : 2 * LANES]
            tend_b = -0.5 * (u * b_x + v * b_y) - 0.02 * bih_b
            new_b = jnp.where(act, b + 0.2 * tend_b, 0.0)
            if step == STEPS - 1:
                out_b[k] = new_b
            else:
                in_3d[2, k] = new_b
            return carry

        def level(k, carry):
            press_x, press_y, force_u, force_v, col_u, col_v = carry
            act = (lax.convert_element_type(k, F32) < code).astype(F32)
            rows = pl.ds(pl.multiple_of(ROWS * k, ROWS), ROWS)
            rows_v = pl.ds(pl.multiple_of(ROWS * (LEVELS + k), ROWS), ROWS)
            bih_u = laplace(k, lp, mom_out[rows])
            bih_v = laplace(LEVELS + k, lp, mom_out[rows_v])
            u, v = fx[pl.ds(EXT * k + OWN, ROWS)], fx[pl.ds(EXT * (LEVELS + k) + OWN, ROWS)]
            at = EXT * (MOVING + k) + OWN
            press_x = press_x + (fx[pl.ds(at + 1, ROWS)] - fx[pl.ds(at - 1, ROWS)])
            press_y = press_y + buoy_out[rows, LANES : 2 * LANES]
            tend_u = (-0.25 / LEVELS) * press_x + 0.1 * v - 0.02 * bih_u
            tend_v = (-0.25 / LEVELS) * press_y - 0.1 * u - 0.02 * bih_v
            su = act * (u + 0.2 * tend_u)
            sv = act * (v + 0.2 * tend_v)
            star_u[k] = su
            star_v[k] = sv
            if step < STEPS - 1:
                put_rows(step + 1, MOM_NEAR + k, MOM_FAR + k, su)
                put_rows(step + 1, MOM_NEAR + LEVELS + k, MOM_FAR + LEVELS + k, sv)
            return (
                press_x, press_y, force_u + act * tend_u, force_v + act * tend_v,
                col_u + su, col_v + sv,
            )

        _, _, force_u, force_v, col_u, col_v = lax.fori_loop(
            0, LEVELS, level, (zero,) * 6, unroll=True
        )
        force_u, force_v = force_u / LEVELS, force_v / LEVELS
        fx_send[step, 0:ROWS] = force_u
        fx_send[step, ROWS : 2 * ROWS] = force_v
        fy_send[step] = jnp.where(
            rim_lanes[0:8], force_u[0:8],
            jnp.where(
                lane8 < 48, turn(force_u[8:16], 32, 1),
                jnp.where(lane8 < 80, turn(force_v[0:8], 64, 1), turn(force_v[8:16], 96, 1)),
            ),
        )
        start(FORCE, step)
        if step < STEPS - 1:
            for a, cells in enumerate((col_u, col_v)):
                at = FLAT_ROW + 2 * (1 + a)
                put_rows(step + 1, at, at + 1, cells)
            start_far(RIMS, step + 1)
            def pack_star(k, strips):
                strips = put_strip(k, star_u[k], strips)
                return put_strip(LEVELS + k, star_v[k], strips)

            strips = lax.fori_loop(0, LEVELS, pack_star, (zero, zero), unroll=True)
            strips = put_strip(STACK + 1, col_u, strips)
            strips = put_strip(STACK + 2, col_v, strips)
        if step == 0:
            arrive(EARLY, step)
        rim_laps(buoy_out, MOVING, LEVELS, BUOY_NEAR, BUOY_FAR)
        own_laps(buoy_out, MOVING, LEVELS)
        stage_own(buoy_in, MOVING, LEVELS, lp)
        stage_edge(buoy_in, MOVING, LEVELS, lap_near)
        buoy_out[0:rows_b, 0:LANES] = apply(buoy_in, rows_b, LANES)
        lax.fori_loop(0, LEVELS, buoyancy, 0, unroll=True)
        if step < STEPS - 1:
            def pack_b(k, strips):
                cells = in_3d[2, k]
                fx[pl.ds(EXT * (MOVING + k) + OWN, ROWS)] = cells
                return put_b(step + 1, k, cells, strips)

            strips = lax.fori_loop(0, LEVELS, pack_b, strips, unroll=True)
            strips = turn(strips[0], -2, 1), strips[1]
            y_send[step + 1, 0] = strips[0]
            y_send[step + 1, 1] = strips[1]
            start_far(EARLY, step + 1)
            start_near(EARLY, step + 1)
            start_near(RIMS, step + 1)
            stage_own(buoy_in, MOVING, LEVELS, fx)
        arrive(PLANE, step)
        sides = [gy_recv[step, r] for r in range(6)]

        def plane(own, a):
            rows = slice(ROWS * a, ROWS * (a + 1))
            return wide(own, gx_recv[step, 0, rows], gx_recv[step, 1, rows], sides, a)

        if step == 0:
            rows = pl.ds(CODE_PLANE, ROWS)
            code_wide = wide(code, x_recv[0, 0, rows], x_recv[0, 1, rows], sides, 3)
            wet, depth = (code_wide > 0.0).astype(F32), code_wide / LEVELS
        state = [plane(cells, a) for a, cells in enumerate(flats)]
        arrive(FORCE, step)
        beside = [[], []]
        for r in range(3):
            strip = jnp.where((lane8 & 16) == 0, fy_recv[step, r + 3], fy_recv[step, r])
            for part in range(4):
                rolled = turn(strip, -32 * part, 1) if part else strip
                beside[part // 2].append(jnp.where(rim_lanes[0:8], rolled, 0.0))
        push = []
        for a, own in enumerate((force_u, force_v)):
            rows = slice(ROWS * a, ROWS * (a + 1))
            main = [fx_recv[step, 0, rows], own, fx_recv[step, 1, rows]]
            push.append(0.2 * jnp.concatenate(
                [jnp.concatenate(main, axis=0), jnp.concatenate(beside[a], axis=0)], axis=1
            ))
        eta, flow_u, flow_v, sum_u, sum_v = barotropic(state, push, wet, depth, 3 if step < STEPS - 1 else 4)
        shift_u = (SCALE * inside(sum_u) - col_u) / lay
        shift_v = (SCALE * inside(sum_v) - col_v) / lay

        def couple(k, carry):
            act = lax.convert_element_type(k, F32) < code
            new_u = jnp.where(act, star_u[k] + shift_u, 0.0)
            new_v = jnp.where(act, star_v[k] + shift_v, 0.0)
            if step == STEPS - 1:
                out_u[k] = new_u
                out_v[k] = new_v
            else:
                fx[pl.ds(EXT * k + OWN, ROWS)] = new_u
                fx[pl.ds(EXT * (LEVELS + k) + OWN, ROWS)] = new_v
            return carry

        lax.fori_loop(0, LEVELS, couple, 0, unroll=True)
        if step < STEPS - 1:
            stage_own(mom_in, 0, MOVING, fx)
            mom_out[0 : MOVING * ROWS] = own_product(mom_in, MOVING * ROWS)

    out_eta[...] = inside(eta)
    out_tu[...] = inside(flow_u)
    out_tv[...] = inside(flow_v)
    for step in range(STEPS):
        for phase in range(PHASES):
            if phase != CUBES or step == 0:
                sent(phase, step)


def per_device(velocity_u, velocity_v, buoyancy, surface, transport_u, transport_v, ocean, layers):
    cube = jax.ShapeDtypeStruct(velocity_u.shape, F32)
    flat = jax.ShapeDtypeStruct(surface.shape, F32)
    hbm = pl.BlockSpec(memory_space=pltpu.HBM)
    vmem = pl.BlockSpec(memory_space=pltpu.VMEM)
    outs = (cube, cube, cube, flat, flat, flat)
    args = [
        pltpu.with_memory_space_constraint(x, pltpu.HBM)
        for x in (velocity_u, velocity_v, buoyancy, surface, transport_u, transport_v, ocean, layers)
    ]
    block = (LEVELS, ROWS, LANES)
    middle = pl.pallas_call(
        kernel,
        out_shape=outs,
        in_specs=[hbm] * 8,
        out_specs=(vmem,) * 6,
        scratch_shapes=[
            pltpu.VMEM(block, F32),
            pltpu.VMEM(block, F32),
            pltpu.VMEM((STACK * EXT + EXT, LANES), F32),
            pltpu.VMEM((STACK * EXT + EXT, LANES), F32),
            pltpu.VMEM((ROWS + 8, LANES), F32),
            pltpu.VMEM((4, 8, LANES), F32),
            pltpu.VMEM((2, 2 * MOVING, LANES), F32),
            pltpu.VMEM((FIELDS,) + block, F32),
            pltpu.VMEM((3, ROWS, LANES), F32),
            pltpu.VMEM((2, ROWS, LANES), jnp.int32),
            pltpu.VMEM((4 * LANES, 2 * LANES), BF16),
            pltpu.VMEM((MOVING * (ROWS + 2), 4 * LANES), BF16),
            pltpu.VMEM((LEVELS * (ROWS + 2), 4 * LANES), BF16),
            pltpu.VMEM((MOVING * (ROWS + 2), LANES), F32),
            pltpu.VMEM((LEVELS * (ROWS + 2), 2 * LANES), F32),
            pltpu.VMEM((MOVING * ROWS, LANES), F32),
            pltpu.VMEM((STEPS, 2, RIM, LANES), F32),
            pltpu.VMEM((STEPS, 2, ROWS, LANES), F32),
            pltpu.VMEM((STEPS, 2, RIM, LANES), F32),
            pltpu.VMEM((STEPS, 6, ROWS, LANES), F32),
            pltpu.VMEM((STEPS, 3 * ROWS, LANES), F32),
            pltpu.VMEM((STEPS, 2, 8, LANES), F32),
            pltpu.VMEM((STEPS, 2, 3 * ROWS, LANES), F32),
            pltpu.VMEM((STEPS, 6, 8, LANES), F32),
            pltpu.VMEM((STEPS, 2 * ROWS, LANES), F32),
            pltpu.VMEM((STEPS, 8, LANES), F32),
            pltpu.VMEM((STEPS, 2, 2 * ROWS, LANES), F32),
            pltpu.VMEM((STEPS, 6, 8, LANES), F32),
            pltpu.SemaphoreType.DMA((8,)),
            pltpu.SemaphoreType.DMA((PHASES * STEPS, 8)),
            pltpu.SemaphoreType.DMA((PHASES * STEPS, 8)),
        ],
        compiler_params=pltpu.CompilerParams(
            collective_id=0, has_side_effects=True, vmem_limit_bytes=16 * 2**20
        ),
    )(*args)
    return tuple(
        pl.pallas_call(
            store_kernel,
            out_shape=outs,
            in_specs=[vmem] * 6,
            out_specs=(hbm,) * 6,
            scratch_shapes=[pltpu.SemaphoreType.DMA((6,))],
            compiler_params=pltpu.CompilerParams(vmem_limit_bytes=16 * 2**20),
        )(*middle)
    )


def solution(mesh):
    cube, flat = P(None, "gx", "gy"), P("gx", "gy")
    return jax.shard_map(
        per_device,
        mesh=mesh,
        in_specs=(cube, cube, cube, flat, flat, flat, flat, flat),
        out_specs=(cube, cube, cube, flat, flat, flat),
        check_vma=False,
    )
```
